128 devices in a mesh: section: 2 (over core), seq: 4 (over z), shard: 16 (over y, x).
Axes of the slice: x: 4, y: 4, z: 4, core: 2. Of those that a mesh axis runs over, the one named last changes fastest.
Arguments:
- acts_in: bfloat16 [2, 16, 288, 1024], P(None, 'shard', 'seq'), may hold values from -6 to 6
- cotangent: bfloat16 [2, 16, 288, 1024], P(None, 'shard', 'seq'), may hold values from -6 to 6
- qkv_weight: bfloat16 [2, 1024, 3072], P('section', 'shard'), may hold values from -0.1875 to 0.1875
- out_weight: bfloat16 [2, 1024, 1024], P('section', 'shard'), may hold values from -0.75 to 0.75
- up_weight: bfloat16 [2, 1024, 4096], P('section', 'shard'), may hold values from -0.1875 to 0.1875
- down_weight: bfloat16 [2, 4096, 1024], P('section', 'shard'), may hold values from -0.09375 to 0.09375
- vectors: bfloat16 [2, 4, 1024], P('section', None, 'shard'), may hold values from 0.25 to 1.75
- image_ids: int32 [2, 16, 288], P(None, 'shard'), may hold values from 0 to 2, as said below
Outputs:
- layer_out: bfloat16 [2, 2, 16, 288, 1024], P('section', None, 'shard', 'seq')
- grad_in: bfloat16 [2, 2, 16, 288, 1024], P('section', None, 'shard', 'seq')
- qkv_grad: float32 [2, 1024, 3072], P('section', 'shard')
- out_grad: float32 [2, 1024, 1024], P('section', 'shard')
- up_grad: float32 [2, 1024, 4096], P('section', 'shard')
- down_grad: float32 [2, 4096, 1024], P('section', 'shard')
- vector_grad: float32 [2, 4, 1024], P('section', None, 'shard')
The draws below stay inside these ranges and needn't reach their ends.
Inputs may be any that keep to these rules, and one draw needn't show every extreme that they name: `image_ids`: in every pack the ids never fall and begin at 0. In micro-batch 0 a pack holds the tail of an image, then one whole crop of 257 tokens (id 1), then the head of the next image; in micro-batch 1 it holds the tail of an image, then a piece of another (id 1) that fills the pack. In every pack one image begins within the first 72 tokens and ends within the last 72.
All inputs are finite; a program needn't handle non-finite values.
Results may differ from the reference program's by a relative error of at most 0.023.
Values may be sent and summed in bfloat16 or wider, within the bound.
A program may use at most 192 MiB of HBM per device.

```python
import jax
import jax.numpy as jnp
from jax import lax

D = 1024
HEADS = 16
HEAD_DIM = 64
FF = 4096
CROP = 257
TOK_DEV = 72
MICRO = 2
PACK = 288
PACKS = 16


def draw_image_ids(key, part):
    key = jax.random.fold_in(key, 11)
    keys_split = jax.random.split(key, 2)
    places = jnp.arange(PACK, dtype=jnp.int32)[None, :]
    earliest = max(1, PACK - TOK_DEV + 1 - CROP)
    latest = min(TOK_DEV - 1, PACK - CROP - 1)
    opening = jax.random.randint(keys_split[0], (PACKS, 1), earliest, latest + 1, dtype=jnp.int32)
    three_way = (places >= opening).astype(jnp.int32) + (places >= opening + CROP).astype(jnp.int32)
    ending = jax.random.randint(keys_split[1], (PACKS, 1), 1, TOK_DEV, dtype=jnp.int32)
    two_way = (places >= ending).astype(jnp.int32)
    return jnp.stack([three_way, two_way])


def block_levels(own_key, dims, cuts, least, top_value):
    def one(axis_at, shards_of):
        heights = jax.random.uniform(jax.random.fold_in(jax.random.fold_in(own_key, 6), axis_at), (shards_of,), jnp.float32, least / len(cuts), top_value / len(cuts))
        return jnp.repeat(jnp.exp(heights), dims[axis_at] // shards_of).reshape((-1,) + (1,) * (len(dims) - axis_at - 1))

    loudness = one(*cuts[0])
    for cut in cuts[1:]:
        loudness = loudness * one(*cut)
    return loudness


def scatter_about(own_key, extent, deviation, reach, pieces=(), kind=jnp.bfloat16):
    array = jax.random.normal(own_key, extent, jnp.float32) * deviation
    if len(pieces) > 0:
        array = block_levels(own_key, extent, pieces, -0.22, 0.18) * array
    return jnp.clip(array, min=-reach, max=reach).astype(kind)


def setup_inputs(seed: int = 0) -> dict:
    splits = jax.random.split(jax.random.key(seed), 9)
    acts_in = scatter_about(splits[0], (MICRO, PACKS, PACK, D), 1.0, 6.0, ((1, 16), (2, 4)))
    cotangent = scatter_about(splits[1], (MICRO, PACKS, PACK, D), 1.0, 6.0, ((1, 16), (2, 4)))
    qkv_weight = scatter_about(splits[2], (2, D, 3 * D), D ** -0.5, 0.1875, ((0, 2), (1, 16)))
    out_weight = scatter_about(splits[3], (2, D, D), (D // 16) ** -0.5, 0.75, ((0, 2), (1, 16)))
    up_weight = scatter_about(splits[4], (2, D, FF), D ** -0.5, 0.1875, ((0, 2), (1, 16)))
    down_weight = scatter_about(splits[5], (2, FF, D), FF ** -0.5, 0.09375, ((0, 2), (1, 16)))
    vectors = jnp.clip(1.0 + 0.15 * jax.random.normal(splits[6], (2, 4, D), jnp.float32), 0.25, 1.75).astype(jnp.bfloat16)
    image_ids = draw_image_ids(jax.random.fold_in(splits[8], 71), 0)
    return dict(acts_in=acts_in, cotangent=cotangent, qkv_weight=qkv_weight, out_weight=out_weight, up_weight=up_weight, down_weight=down_weight, vectors=vectors, image_ids=image_ids)


EPS = 1e-06
NEG = -1e+30

@jax.custom_vjp
def low(v):
    return lax.optimization_barrier(v.astype(jnp.bfloat16)).astype(jnp.float32)

@jax.custom_vjp
def low_back(v):
    return v

def low_keep(v):
    return (low(v), None)

def low_pass(kept, grad):
    return (grad,)

def back_keep(v):
    return (v, None)

def back_low(kept, grad):
    return (low(grad),)
low.defvjp(low_keep, low_pass)
low_back.defvjp(back_keep, back_low)

def layer_norm(values, gain):
    centre = values - lax.optimization_barrier(jnp.mean(values, axis=-1, keepdims=True))
    spread = lax.optimization_barrier(jnp.mean(centre * centre, axis=-1, keepdims=True))
    return centre * lax.rsqrt(spread + EPS) * gain

def block(tokens, image_row, w_qkv, w_out, w_up, w_down, gain_rows):
    highest = lax.Precision.HIGHEST
    normed = low(layer_norm(tokens, gain_rows[0]))
    packed = low(low_back(jnp.dot(normed, w_qkv, precision=highest)))
    packed = packed.reshape(PACK, 3, HEADS, HEAD_DIM)
    queries = packed[:, 0]
    keys_all = packed[:, 1]
    values_all = packed[:, 2]
    raw_scores = jnp.einsum('qhd,khd->hqk', queries, keys_all, precision=highest) * HEAD_DIM ** (-0.5)
    scores = low_back(raw_scores)
    same_image = image_row[:, None] == image_row[None, :]
    scores = jnp.where(same_image[None], scores, NEG)
    row_max = lax.optimization_barrier(jnp.max(scores, axis=-1, keepdims=True))
    raised = jnp.exp(scores - row_max)
    soft_weights = raised / lax.optimization_barrier(jnp.sum(raised, axis=-1, keepdims=True))
    attended = jnp.einsum('hqk,khd->qhd', low(soft_weights), values_all, precision=highest).reshape(PACK, D)
    attended = low(low_back(attended))
    branch = low_back(jnp.dot(attended, w_out, precision=highest))
    middle = tokens + gain_rows[1] * branch
    hidden_in = low(layer_norm(middle, gain_rows[2]))
    pre_act = low_back(jnp.dot(hidden_in, w_up, precision=highest))
    activated = low(jax.nn.gelu(pre_act, approximate=False))
    result = low_back(jnp.dot(activated, w_down, precision=highest))
    return middle + gain_rows[3] * result

def reference(acts_in, cotangent, qkv_weight, out_weight, up_weight, down_weight, vectors, image_ids):
    pack_total = MICRO * PACKS
    inputs = acts_in.astype(jnp.float32).reshape(pack_total, PACK, D)
    image_rows = image_ids.reshape(pack_total, PACK).astype(jnp.int32)

    def run_section(tokens, w_qkv, w_out, w_up, w_down, gain_rows):

        def single(pair):
            return block(pair[0], pair[1], w_qkv, w_out, w_up, w_down, gain_rows)
        return lax.map(jax.checkpoint(single), (tokens, image_rows))

    def params_of(layer):
        return (qkv_weight[layer].astype(jnp.float32), out_weight[layer].astype(jnp.float32), up_weight[layer].astype(jnp.float32), down_weight[layer].astype(jnp.float32), vectors[layer].astype(jnp.float32))
    first_w = params_of(0)
    second_w = params_of(1)
    middle, pull_first = jax.vjp(run_section, inputs, first_w[0], first_w[1], first_w[2], first_w[3], first_w[4])
    middle = low(middle)
    final, pull_second = jax.vjp(run_section, middle, second_w[0], second_w[1], second_w[2], second_w[3], second_w[4])
    grads_second = pull_second(cotangent.astype(jnp.float32).reshape(pack_total, PACK, D))
    middle_grad = low(grads_second[0])
    grads_first = pull_first(middle_grad)
    shape_out = (MICRO, PACKS, PACK, D)
    layer_out = jnp.stack([middle.reshape(shape_out), final.reshape(shape_out)]).astype(jnp.bfloat16)
    grad_in = jnp.stack([grads_first[0].reshape(shape_out), middle_grad.reshape(shape_out)]).astype(jnp.bfloat16)
    stacked = [jnp.stack([grads_first[index], grads_second[index]]) for index in range(1, 6)]
    return (layer_out, grad_in, stacked[0], stacked[1], stacked[2], stacked[3], stacked[4])
```

```python
import jax
import jax.numpy as jnp
from jax import lax
from jax.sharding import PartitionSpec as P

HEAD_DIM = 64
EPS = 1e-06
NEG = -1e30
BF = jnp.bfloat16
F32 = jnp.float32


def dot(a, b):
    return jnp.dot(a, b, preferred_element_type=F32)


def dot_rows(a, b):
    return lax.dot_general(a, b, (((0,), (0,)), ((), ())), preferred_element_type=F32)


def dot_cols(a, b):
    return lax.dot_general(a, b, (((1,), (1,)), ((), ())), preferred_element_type=F32)


def normalise(values):
    centre = values - jnp.mean(values, axis=-1, keepdims=True)
    scale = lax.rsqrt(jnp.mean(centre * centre, axis=-1, keepdims=True) + EPS)
    return centre * scale, scale


def norm_back(grad, values, gain):
    xhat, scale = normalise(values)
    f = grad * gain
    dv = scale * (
        f
        - jnp.mean(f, axis=-1, keepdims=True)
        - xhat * jnp.mean(f * xhat, axis=-1, keepdims=True)
    )
    return dv, jnp.sum(grad * xhat, axis=0)


def gelu_parts(u):
    cdf = 0.5 * (1.0 + lax.erf(u * 0.7071067811865476))
    slope = cdf + u * jnp.exp(-0.5 * u * u) * 0.3989422804014327
    return u * cdf, slope


def gather_tokens(rows):
    return lax.all_gather(rows, "seq", axis=0, tiled=True)


def scatter_tokens(partial):
    return lax.psum_scatter(partial.astype(BF), "seq", scatter_dimension=0, tiled=True).astype(F32)


def split_heads(packed):
    n = packed.shape[0]
    g = packed.reshape(n, 2, 3, 2, HEAD_DIM)
    return [g[:, :, t].reshape(n, 4, HEAD_DIM) for t in range(3)]


def attn_forward(x, ids, w, vec):
    xhat, _ = normalise(x)
    h1 = gather_tokens((xhat * vec[0]).astype(BF))
    packed = dot(h1, w["qkv"]).astype(BF)
    q, k, v = split_heads(packed)
    s = jnp.einsum("qhd,khd->hqk", q, k, preferred_element_type=F32) * HEAD_DIM**-0.5
    s = jnp.where((ids[:, None] == ids[None, :])[None], s, NEG)
    top = jnp.max(s, axis=-1, keepdims=True)
    e = jnp.exp(s - top)
    total = jnp.sum(e, axis=-1, keepdims=True)
    o = jnp.einsum(
        "hqk,khd->qhd", (e / total).astype(BF), v, preferred_element_type=F32
    ).astype(BF)
    o = o.reshape(o.shape[0], 4 * HEAD_DIM)
    joined = lax.all_to_all(o, "seq", split_axis=0, concat_axis=1, tiled=True)
    a = dot(joined, w["out"])
    y1 = x + vec[1] * a
    return y1, (x, h1, q, k, v, top + jnp.log(total), joined, a)


def mlp_forward(y1, w, vec):
    yhat, _ = normalise(y1)
    h2 = gather_tokens((yhat * vec[2]).astype(BF))
    u = dot(h2, w["up"])
    g, slope = gelu_parts(u)
    g = g.astype(BF)
    m = scatter_tokens(dot(g, w["down"]))
    return y1 + vec[3] * m, (y1, h2, slope.astype(BF), g, m)


def mlp_backward(dz, kept, w, vec):
    y1, h2, slope, g, m = kept
    dm = gather_tokens((vec[3] * dz).astype(BF))
    dc2 = jnp.sum(dz * m, axis=0)
    d_down = dot_rows(g, dm)
    du = (slope * dot_cols(dm, w["down"])).astype(BF)
    d_up = dot_rows(h2, du)
    dh2 = scatter_tokens(dot_cols(du, w["up"]))
    dn, dg2 = norm_back(dh2, y1, vec[2])
    return dz + dn, d_up, d_down, dg2, dc2


def attn_backward(dy1, ids, kept, w, vec):
    x, h1, q, k, v, logsum, joined, a = kept
    da = (vec[1] * dy1).astype(BF)
    dc1 = jnp.sum(dy1 * a, axis=0)
    d_out = dot_rows(joined, da)
    do = dot_cols(da, w["out"]).astype(BF)
    do = lax.all_to_all(do, "seq", split_axis=1, concat_axis=0, tiled=True)
    n = do.shape[0]
    do = do.reshape(n, 4, HEAD_DIM)
    s = jnp.einsum("qhd,khd->hqk", q, k, preferred_element_type=F32) * HEAD_DIM**-0.5
    s = jnp.where((ids[:, None] == ids[None, :])[None], s, NEG)
    p = jnp.exp(s - logsum)
    dp = jnp.einsum("qhd,khd->hqk", do, v, preferred_element_type=F32)
    dv = jnp.einsum("hqk,qhd->khd", p.astype(BF), do, preferred_element_type=F32)
    ds = (p * (dp - jnp.sum(p * dp, axis=-1, keepdims=True))).astype(BF)
    dq = jnp.einsum("hqk,khd->qhd", ds, k, preferred_element_type=F32) * HEAD_DIM**-0.5
    dk = jnp.einsum("hqk,qhd->khd", ds, q, preferred_element_type=F32) * HEAD_DIM**-0.5
    grads = jnp.stack([t.reshape(n, 2, 128) for t in (dq, dk, dv)], axis=2).astype(BF)
    grads = grads.reshape(n, 768)
    d_qkv = dot_rows(h1, grads)
    dh1 = scatter_tokens(dot_cols(grads, w["qkv"]))
    dn, dg1 = norm_back(dh1, x, vec[0])
    return dy1 + dn, d_qkv, d_out, dg1, dc1


def gather_weights(qkv, out, up, down, vec, z):
    parts = (
        lax.dynamic_index_in_dim(qkv.reshape(64, 3, 4, 2, 128), z, 2, False).transpose(2, 0, 1, 3),
        out.reshape(64, 2, 512).transpose(1, 0, 2),
        lax.dynamic_index_in_dim(up.reshape(64, 16, 4, 2, 32), z, 2, False).transpose(2, 0, 1, 3),
        lax.dynamic_index_in_dim(down.reshape(4, 2, 32, 1024), z, 0, False),
    )
    shapes = ((64, 384), (64, 512), (64, 512), (32, 1024))
    parts = [p.reshape((2,) + s) for p, s in zip(parts, shapes)]
    parts = [lax.all_to_all(p, "section", split_axis=0, concat_axis=0, tiled=True) for p in parts]
    layers = []
    vecs = lax.all_gather(vec, ("section", "shard"), axis=0)
    vecs = vecs.reshape(2, 16, 4, 64).transpose(0, 2, 1, 3).reshape(2, 4, 1024).astype(F32)
    for layer in range(2):
        w = {}
        for name, p, axis in zip(("qkv", "out", "up", "down"), parts, (1, 1, 1, 0)):
            whole = lax.all_gather(p[layer], "shard", axis=0, tiled=True)
            w[name] = lax.all_gather(whole, "section", axis=axis, tiled=True)
        layers.append(w)
    return layers, vecs


def reduce_pieces(pieces, c):
    flats = []
    for p, axis in zip(pieces, (1, 1, 1, 0)):
        half = lax.psum_scatter(p.astype(BF), "section", scatter_dimension=axis, tiled=True)
        own = lax.psum_scatter(half, "shard", scatter_dimension=0, tiled=True)
        flats.append(own.reshape(-1))
    return flats


def local(acts_in, cotangent, qkv_weight, out_weight, up_weight, down_weight, vectors, image_ids):
    c = lax.axis_index("section")
    z = lax.axis_index("seq")
    layers, vecs = gather_weights(
        qkv_weight[0], out_weight[0], up_weight[0], down_weight[0], vectors[0], z
    )
    x = lax.dynamic_index_in_dim(acts_in, c, 0, False)[0].astype(F32)
    dz = lax.dynamic_index_in_dim(cotangent, c, 0, False)[0].astype(F32)
    ids = lax.dynamic_index_in_dim(image_ids, c, 0, False)[0]
    kept = []
    outs = []
    for layer in range(2):
        w, vec = layers[layer], vecs[layer]
        y1, kept_a = attn_forward(x, ids, w, vec)
        y2, kept_m = mlp_forward(y1, w, vec)
        kept.append((kept_a, kept_m))
        sent = y2.astype(BF)
        outs.append(sent)
        x = sent.astype(F32)
    grads = [None, None]
    flats = [None, None]
    vparts = [None, None]
    for layer in (1, 0):
        w, vec = layers[layer], vecs[layer]
        kept_a, kept_m = kept[layer]
        dy1, d_up, d_down, dg2, dc2 = mlp_backward(dz, kept_m, w, vec)
        dx, d_qkv, d_out, dg1, dc1 = attn_backward(dy1, ids, kept_a, w, vec)
        grads[layer] = dx.astype(BF)
        dz = grads[layer].astype(F32)
        flats[layer] = reduce_pieces((d_qkv, d_out, d_up, d_down), c)
        vparts[layer] = jnp.stack([dg1, dc1, dg2, dc2])
    vown = lax.psum_scatter(
        jnp.stack(vparts).astype(BF), "shard", scatter_dimension=2, tiled=True
    )
    both = jnp.stack(
        [jnp.concatenate(flats[l] + [vown[l].reshape(-1)]) for l in range(2)]
    )
    mine = lax.all_to_all(both, "section", split_axis=0, concat_axis=0, tiled=True)
    every = lax.all_gather(mine, "seq", axis=0)
    every = every.astype(F32)
    sizes = (64 * 384, 64 * 512, 64 * 512, 32 * 1024, 256)
    at = 0
    cut = []
    for s in sizes:
        cut.append(every[:, :, at : at + s])
        at += s
    g_qkv = cut[0].reshape(4, 2, 64, 3, 128).transpose(2, 3, 0, 1, 4).reshape(64, 3072)
    g_out = jnp.sum(cut[1].reshape(4, 2, 64, 512), axis=0).transpose(1, 0, 2).reshape(64, 1024)
    g_up = cut[2].reshape(4, 2, 64, 16, 32).transpose(2, 3, 0, 1, 4).reshape(64, 4096)
    g_down = cut[3].reshape(256, 1024)
    g_vec = jnp.sum(cut[4].reshape(8, 4, 64), axis=0)
    pair = jnp.stack(outs + grads)[:, None]
    pair = pair.reshape(2, 2, 72, 1024).transpose(1, 0, 2, 3)
    pair = lax.all_to_all(pair, "section", split_axis=0, concat_axis=0, tiled=True)
    layer_out = pair[:, 0][None, :, None]
    grad_in = pair[:, 1][None, :, None]
    return (layer_out, grad_in, g_qkv[None], g_out[None], g_up[None], g_down[None], g_vec[None])


def solution(mesh):
    placed = (
        P(None, "shard", "seq", None),
        P(None, "shard", "seq", None),
        P("section", "shard", None),
        P("section", "shard", None),
        P("section", "shard", None),
        P("section", "shard", None),
        P("section", None, "shard"),
        P(None, "shard", None),
    )
    return jax.shard_map(
        local,
        mesh=mesh,
        in_specs=placed,
        out_specs=(
            P("section", None, "shard", "seq", None),
            P("section", None, "shard", "seq", None),
            P("section", "shard", None),
            P("section", "shard", None),
            P("section", "shard", None),
            P("section", "shard", None),
            P("section", None, "shard"),
        ),
        check_vma=False,
    )
```

```python
import jax
import jax.numpy as jnp
from jax import lax
from jax.experimental import pallas as pl
from jax.experimental.pallas import tpu as pltpu
from jax.sharding import PartitionSpec as P

EPS = 1e-06
NEG = -1e30
BF = jnp.bfloat16
F32 = jnp.float32
MESH = pl.DeviceIdType.MESH
D = 1024
ROWS = 80
TOK = 72
N = 4 * ROWS
TENSORS = {"q": (0, 384, True), "o": (384, 512, False), "u": (896, 512, True), "d": (1408, 512, False)}
HALF = 1920


def dot(a, b):
    return lax.dot_general(a, b, (((1,), (0,)), ((), ())), preferred_element_type=F32)


def dot_rows(a, b):
    return lax.dot_general(a, b, (((0,), (0,)), ((), ())), preferred_element_type=F32)


def dot_cols(a, b):
    return lax.dot_general(a, b, (((1,), (1,)), ((), ())), preferred_element_type=F32)


def normalise(values):
    centre = values - jnp.mean(values, axis=-1, keepdims=True)
    scale = lax.rsqrt(jnp.mean(centre * centre, axis=-1, keepdims=True) + EPS)
    return centre * scale, scale


def norm_back(grad, values, gain):
    xhat, scale = normalise(values)
    f = grad * gain
    dv = scale * (
        f
        - jnp.mean(f, axis=-1, keepdims=True)
        - xhat * jnp.mean(f * xhat, axis=-1, keepdims=True)
    )
    return dv, jnp.sum(grad * xhat, axis=0, keepdims=True)


def gelu_parts(u):
    cdf = 0.5 * (1.0 + lax.erf(u * 0.7071067811865476))
    slope = cdf + u * jnp.exp(-0.5 * u * u) * 0.3989422804014327
    return u * cdf, slope


SCRATCH = dict(
    own=((2, 64, HALF), BF),
    wq=((2, 4, 4, 64, 768), BF),
    wo=((2, 4, 4, 64, D), BF),
    wu=((2, 4, 4, 64, D), BF),
    wd=((2, 4, 4, 64, D), BF),
    vsend=((6, 8, D), F32),
    vrecv=((17, 8, D), F32),
    vec=((8, D), F32),
    vgrad=((8, D), F32),
    x=((80, D), BF),
    h1=((2, 4, ROWS, D), BF),
    qkv=((2, 4, ROWS, 768), BF),
    prob=((2, 4, N, N), BF),
    osend=((2, 4, ROWS, 256), BF),
    ojoin=((2, 4, ROWS, 256), BF),
    a=((2, ROWS, D), F32),
    y1=((2, ROWS, D), F32),
    h2=((2, 4, ROWS, D), BF),
    slope=((2, 4, ROWS, D), BF),
    g=((2, 4, ROWS, D), BF),
    stage=((2, 4, ROWS, D), BF),
    part=((6, 3, ROWS, D), BF),
    mine=((ROWS, D), F32),
    m=((2, ROWS, D), F32),
    dm=((2, 4, ROWS, D), BF),
    du=((4, ROWS, D), BF),
    dy1=((ROWS, D), F32),
    da=((ROWS, D), BF),
    dosend=((2, 4, ROWS, 256), BF),
    dojoin=((2, 4, ROWS, 256), BF),
    dqkv=((4, ROWS, 768), BF),
    zout=((2, ROWS, D), BF),
    gout=((2, ROWS, D), BF),
    zother=((ROWS, D), BF),
    gother=((ROWS, D), BF),
    fin=((2, 4, 64, HALF), BF),
    fother=((4, 64, HALF), BF),
)
for _t, (_, _h, _x) in TENSORS.items():
    SCRATCH["gs" + _t] = ((4, 4, 64, _h), BF)
    SCRATCH["ra" + _t] = ((2, 4, 4, 64, _h), BF)
    SCRATCH["rb" + _t] = ((2, 3, 4, 64, _h), BF)
    SCRATCH["rc" + _t] = ((2, 3, 64, _h), BF)

GROUPS = (
    ["A", "Alocal", "va", "vx", "vy", "ga", "gx", "gy", "gz", "zo", "go", "fo"]
    + [n + t + str(l) for n in ("B", "Bl", "C", "D", "ga", "gb", "gc", "ge") for t in "qoud" for l in (0, 1)]
    + [n + str(l) for n in ("h1", "h2", "o", "m", "dm", "dh2", "do", "dh1") for l in (0, 1)]
)
GROUP = {n: i for i, n in enumerate(dict.fromkeys(GROUPS))}


class Refs:
    pass


def kernel(x_in, dz_in, wown, vin, idc, idr, lo_ref, gi_ref, gq_ref, go_ref, gu_ref, gd_ref, gv_ref, *scratch):
    r = Refs()
    for name, ref in zip(SCRATCH, scratch):
        setattr(r, name, ref)
    ssem, rsem = scratch[len(SCRATCH) :]
    c = lax.axis_index("section")
    z = lax.axis_index("seq")
    p = lax.axis_index("shard")
    y, x = p // 4, p % 4
    sib = {"section": 1 - c}

    def zpeer(k):
        return {"seq": (z + k) % 4}

    def xpeer(k):
        return {"shard": y * 4 + (x + k) % 4}

    def ypeer(k):
        return {"shard": ((y + k) % 4) * 4 + x}

    pending = {}

    def copy(group, slot, src, dst, dev):
        return pltpu.make_async_remote_copy(
            src_ref=src,
            dst_ref=dst,
            send_sem=ssem.at[GROUP[group], slot],
            recv_sem=rsem.at[GROUP[group], slot],
            device_id=dev,
            device_id_type=MESH,
        )

    def push(group, slot, src, dst, dev):
        copy(group, slot, src, dst, dev).start()
        pending[(group, slot)] = (src, dev)

    def sent(group):
        for key in [k for k in pending if k[0] == group]:
            src, dev = pending.pop(key)
            copy(group, key[1], src, src, dev).wait_send()

    def arrived(group, slot, dst):
        copy(group, slot, dst, dst, sib).wait_recv()

    barrier = pltpu.get_barrier_semaphore()
    for dev in [sib] + [f(k) for f in (xpeer, ypeer, zpeer) for k in (1, 2, 3)]:
        pl.semaphore_signal(barrier, inc=1, device_id=dev, device_id_type=MESH)
    pl.semaphore_wait(barrier, 10)

    def half(h, which):
        return pl.ds(pl.multiple_of(which * h, 128), h)

    push("A", 0, wown.at[1 - c], r.own.at[c], sib)
    own_copy = pltpu.make_async_copy(wown.at[c], r.own.at[c], ssem.at[GROUP["Alocal"], 0])
    own_copy.start()
    push("va", 0, vin, r.vrecv.at[0], sib)

    def wref(t):
        return getattr(r, "w" + t)

    def local_copy(t, l):
        off, h, _ = TENSORS[t]
        return pltpu.make_async_copy(
            r.own.at[l, :, pl.ds(off, h)],
            wref(t).at[l, y, x, :, half(h, c)],
            ssem.at[GROUP["Bl" + t + str(l)], 0],
        )

    def weight_b(t, l):
        off, h, xfirst = TENSORS[t]
        peer = xpeer if xfirst else ypeer
        for k in (1, 2, 3):
            push(
                "B" + t + str(l), k - 1,
                r.own.at[l, :, pl.ds(off, h)],
                wref(t).at[l, y, x, :, half(h, c)],
                peer(k),
            )
        local_copy(t, l).start()

    def weight_c(t, l):
        _, h, xfirst = TENSORS[t]
        cols = half(h, c)
        local_copy(t, l).wait()
        for k in (1, 2, 3):
            if xfirst:
                arrived("B" + t + str(l), k - 1, wref(t).at[l, y, (x + 4 - k) % 4, :, cols])
            else:
                arrived("B" + t + str(l), k - 1, wref(t).at[l, (y + 4 - k) % 4, x, :, cols])
        line = wref(t).at[l, y, :, :, cols] if xfirst else wref(t).at[l, :, x, :, cols]
        peer = ypeer if xfirst else xpeer
        for k in (1, 2, 3):
            push("C" + t + str(l), k - 1, line, line, peer(k))

    def weight_d(t, l):
        _, h, xfirst = TENSORS[t]
        cols = half(h, c)
        for k in (1, 2, 3):
            if xfirst:
                line = wref(t).at[l, (y + 4 - k) % 4, :, :, cols]
            else:
                line = wref(t).at[l, :, (x + 4 - k) % 4, :, cols]
            arrived("C" + t + str(l), k - 1, line)
        mine = wref(t).at[l, :, :, :, cols]
        push("D" + t + str(l), 0, mine, mine, sib)

    def weight_done(t, l):
        _, h, _ = TENSORS[t]
        arrived("D" + t + str(l), 0, wref(t).at[l, :, :, :, half(h, 1 - c)])

    def spread(group, at, slots, value, peer):
        r.vsend[at] = value
        for k in (1, 2, 3):
            push(group, k - 1, r.vsend.at[at], r.vrecv.at[slots + k - 1], peer(k))

    def gathered(group, slots, value):
        for k in (1, 2, 3):
            arrived(group, k - 1, r.vrecv.at[slots + k - 1])
        return value + (r.vrecv[slots] + (r.vrecv[slots + 1] + r.vrecv[slots + 2]))

    own_copy.wait()
    arrived("A", 0, r.own.at[1 - c])
    weight_b("q", 0)
    arrived("va", 0, r.vrecv.at[0])
    v = vin[...] + r.vrecv[0]
    spread("vx", 0, 1, v, xpeer)
    weight_b("o", 0)
    weight_b("u", 0)
    weight_b("d", 0)
    xhat0, _ = normalise(x_in[...].astype(F32))
    v = gathered("vx", 1, v)
    spread("vy", 1, 4, v, ypeer)
    weight_c("q", 0)
    v = gathered("vy", 4, v)
    r.vec[...] = v

    def gain(l, row):
        return r.vec[4 * l + row : 4 * l + row + 1, :]

    def send_block(group, ref):
        for k in (1, 2, 3):
            push(group, k - 1, ref.at[z], ref.at[z], zpeer(k))

    def flat(value):
        return value.reshape(N, value.shape[-1])

    def weight(t, l, cols):
        return wref(t)[l, :, :, :, cols].reshape(D, -1)

    lanes = lax.broadcasted_iota(jnp.int32, (1, 128), 1)
    low_lanes = lanes < 64

    def mask_head(value, head):
        keep = low_lanes if head == 0 else jnp.logical_not(low_lanes)
        return jnp.where(keep, value, jnp.zeros_like(value))

    RS = {"m0": 0, "m1": 1, "dh21": 2, "dh11": 3, "dh20": 4, "dh10": 5}

    def rs_slot(group, k, blk, start):
        i = RS[group]
        return copy(
            group, 3 - k,
            r.stage.at[i % 2, blk], r.part.at[i, 3 - k],
            {"seq": blk},
        )

    def rs_put(group, k, blk, make):
        i = RS[group]
        for j in range(4):
            val = make(j)

            @pl.when(k == 0)
            def _():
                r.mine[:, 256 * j : 256 * j + 256] = val

            @pl.when(k > 0)
            def _():
                r.stage[i % 2, blk, :, 256 * j : 256 * j + 256] = val.astype(BF)

        @pl.when(k > 0)
        def _():
            rs_slot(group, k, blk, True).start()

    def rs_sum(group):
        i = RS[group]
        for s in range(3):
            arrived(group, s, r.part.at[i, s])
        return r.mine[...] + (
            r.part[i, 0].astype(F32) + (r.part[i, 1].astype(F32) + r.part[i, 2].astype(F32))
        )

    def rs_sent(group):
        i = RS[group]
        for k in (1, 2, 3):
            rs_slot(group, k, (z + 4 - k) % 4, False).wait_send()

    def ag_wait(group, ref, k, blk):
        @pl.when(k > 0)
        def _():
            copy(group, k - 1, ref.at[blk], ref.at[blk], sib).wait_recv()

    def attn_forward(l, xhat, xin, gap_a, gap_b):
        r.h1[l, z] = (xhat * gain(l, 0)).astype(BF)
        send_block("h1" + str(l), r.h1.at[l])
        gap_a()
        weight_done("q", l)

        @pl.loop(0, 4)
        def _(k):
            blk = (z + 4 - k) % 4
            ag_wait("h1" + str(l), r.h1.at[l], k, blk)
            for j in range(3):
                cols = pl.ds(256 * j, 256)
                r.qkv[l, blk, :, cols] = dot(r.h1[l, blk], weight("q", l, cols)).astype(BF)

        gap_b()
        same = idc[...] == idr[...]

        @pl.loop(0, 2)
        def _(pair):
            base = pl.multiple_of(pair * 384, 128)
            q = flat(r.qkv[l, :, :, pl.ds(base, 128)])
            kk = flat(r.qkv[l, :, :, pl.ds(pl.multiple_of(base + 128, 128), 128)])
            vv = flat(r.qkv[l, :, :, pl.ds(pl.multiple_of(base + 256, 128), 128)])
            q = q * jnp.asarray(0.125, BF)
            res = []
            for head in range(2):
                s = dot_cols(mask_head(q, head), kk)
                s = jnp.where(same, s, NEG)
                e = jnp.exp(s - jnp.max(s, axis=-1, keepdims=True))
                pb = (e * (1.0 / jnp.sum(e, axis=-1, keepdims=True))).astype(BF)
                r.prob[l, 2 * pair + head] = pb
                res.append(dot(pb, vv))
            o = jnp.where(low_lanes, res[0], res[1]).astype(BF)
            r.osend[l, :, :, pl.ds(pl.multiple_of(pair * 128, 128), 128)] = o.reshape(4, ROWS, 128)

        for k in (1, 2, 3):
            blk = (z + k) % 4
            push("o" + str(l), k - 1, r.osend.at[l, blk], r.ojoin.at[l, z], zpeer(k))
        r.ojoin[l, z] = r.osend[l, z]

    def out_proj(l, xin):
        weight_done("o", l)
        for k in (1, 2, 3):
            arrived("o" + str(l), k - 1, r.ojoin.at[l, (z + 4 - k) % 4])
        for j in range(4):
            cols = pl.ds(256 * j, 256)
            acc = None
            for b in range(4):
                w = wref("o")[l, b, :, :, cols].reshape(256, 256)
                term = dot(r.ojoin[l, b], w)
                acc = term if acc is None else acc + term
            r.a[l, :, cols] = acc
        y1 = xin + gain(l, 1) * r.a[l]
        r.y1[l] = y1
        yhat, _ = normalise(y1)
        r.h2[l, z] = (yhat * gain(l, 2)).astype(BF)
        send_block("h2" + str(l), r.h2.at[l])

    def mlp_forward(l, gap_a):
        gap_a()
        weight_done("u", l)
        weight_done("d", l)

        @pl.loop(0, 4)
        def _(k):
            blk = (z + 4 - k) % 4
            ag_wait("h2" + str(l), r.h2.at[l], k, blk)
            for j in range(4):
                cols = pl.ds(256 * j, 256)
                u = dot(r.h2[l, blk], weight("u", l, cols))
                g, slope = gelu_parts(u)
                r.g[l, blk, :, cols] = g.astype(BF)
                r.slope[l, blk, :, cols] = slope.astype(BF)

            def make(j):
                return dot(r.g[l, blk], weight("d", l, pl.ds(256 * j, 256)))

            rs_put("m" + str(l), k, blk, make)

    def finish_layer(l):
        m = rs_sum("m" + str(l))
        r.m[l] = m
        r.zout[l] = (r.y1[l] + gain(l, 3) * m).astype(BF)

    def grad_first(t, l, left, right):
        _, h, _ = TENSORS[t]
        gs = getattr(r, "gs" + t)

        @pl.loop(0, 4)
        def _(b):
            gs[b] = dot_rows(left(b), right(half(h, 1 - c))).astype(BF).reshape(4, 64, h)

        push("ga" + t + str(l), 0, gs, getattr(r, "ra" + t).at[l], sib)

    def grad_second(t, l, left, right):
        _, h, xfirst = TENSORS[t]
        ra = getattr(r, "ra" + t)
        arrived("ga" + t + str(l), 0, ra.at[l])

        @pl.loop(0, 4)
        def _(b):
            val = dot_rows(left(b), right(half(h, c))).reshape(4, 64, h)
            ra[l, b] = (val + ra[l, b].astype(F32)).astype(BF)

        for k in (1, 2, 3):
            if xfirst:
                src, dev = ra.at[l, (y + k) % 4], ypeer(k)
            else:
                src, dev = ra.at[l, :, (x + k) % 4], xpeer(k)
            push("gb" + t + str(l), k - 1, src, getattr(r, "rb" + t).at[l, k - 1], dev)

    def grad_third(t, l):
        _, h, xfirst = TENSORS[t]
        ra, rb = getattr(r, "ra" + t), getattr(r, "rb" + t)
        for k in (1, 2, 3):
            arrived("gb" + t + str(l), k - 1, rb.at[l, k - 1])

        @pl.loop(0, 4)
        def _(i):
            yy, xx = (y, i) if xfirst else (i, x)
            val = ra[l, yy, xx].astype(F32) + rb[l, 0, i].astype(F32)
            val = val + (rb[l, 1, i].astype(F32) + rb[l, 2, i].astype(F32))
            ra[l, yy, xx] = val.astype(BF)

        for k in (1, 2, 3):
            if xfirst:
                src, dev = ra.at[l, y, (x + k) % 4], xpeer(k)
            else:
                src, dev = ra.at[l, (y + k) % 4, x], ypeer(k)
            push("gc" + t + str(l), k - 1, src, getattr(r, "rc" + t).at[l, k - 1], dev)

    def grad_fourth(t, l):
        off, h, xfirst = TENSORS[t]
        ra, rc = getattr(r, "ra" + t), getattr(r, "rc" + t)
        for k in (1, 2, 3):
            arrived("gc" + t + str(l), k - 1, rc.at[l, k - 1])
        val = ra[l, y, x].astype(F32) + rc[l, 0].astype(F32)
        val = val + (rc[l, 1].astype(F32) + rc[l, 2].astype(F32))
        r.fin[l, z, :, off : off + h] = val.astype(BF)
        block = r.fin.at[l, z, :, pl.ds(off, h)]
        for k in (1, 2, 3):
            push("ge" + t + str(l), k - 1, block, block, zpeer(k))

    def grad_done(t, l):
        off, h, _ = TENSORS[t]
        for k in (1, 2, 3):
            arrived("ge" + t + str(l), k - 1, r.fin.at[l, (z + 4 - k) % 4, :, pl.ds(off, h)])

    def mlp_backward(l, dz, gap_a, gap_b):
        r.dm[l, z] = (gain(l, 3) * dz).astype(BF)
        send_block("dm" + str(l), r.dm.at[l])
        r.vgrad[4 * l + 3 : 4 * l + 4, :] = jnp.sum(dz * r.m[l], axis=0, keepdims=True)
        r.dy1[...] = dz
        gap_a()

        @pl.loop(0, 4)
        def _(k):
            blk = (z + 4 - k) % 4
            ag_wait("dm" + str(l), r.dm.at[l], k, blk)
            for b in range(4):
                w = wref("d")[l, b].reshape(256, D)
                cols = pl.ds(256 * b, 256)
                grad = dot_cols(r.dm[l, blk], w)
                r.du[blk, :, cols] = (grad * r.slope[l, blk, :, cols].astype(F32)).astype(BF)

            def make(b):
                return dot_cols(r.du[blk], wref("u")[l, b].reshape(256, D))

            rs_put("dh2" + str(l), k, blk, make)

        def tile(ref):
            return lambda b: flat(ref[:, :, pl.ds(pl.multiple_of(b * 256, 256), 256)])

        def cols_of(ref):
            return lambda cols: flat(ref[:, :, cols])

        g_l, h2_l, dm_l = r.g.at[l], r.h2.at[l], r.dm.at[l]
        grad_first("d", l, tile(g_l), cols_of(dm_l))
        grad_first("u", l, tile(h2_l), cols_of(r.du))
        gap_b()
        dh2 = rs_sum("dh2" + str(l))
        dn, dg2 = norm_back(dh2, r.y1[l], gain(l, 2))
        r.vgrad[4 * l + 2 : 4 * l + 3, :] = dg2
        dy1 = r.dy1[...] + dn
        r.dy1[...] = dy1
        r.da[...] = (gain(l, 1) * dy1).astype(BF)
        for b in range(4):
            w = wref("o")[l, b].reshape(256, D)
            r.dosend[l, b] = dot_cols(r.da[...], w).astype(BF)
        for k in (1, 2, 3):
            push("do" + str(l), k - 1, r.dosend.at[l, (z + k) % 4], r.dojoin.at[l, z], zpeer(k))
        r.dojoin[l, z] = r.dosend[l, z]
        r.vgrad[4 * l + 1 : 4 * l + 2, :] = jnp.sum(dy1 * r.a[l], axis=0, keepdims=True)
        grad_second("d", l, tile(g_l), cols_of(dm_l))
        grad_second("u", l, tile(h2_l), cols_of(r.du))

    def attn_backward(l, gap_a, gap_b):
        gap_a()
        for k in (1, 2, 3):
            arrived("do" + str(l), k - 1, r.dojoin.at[l, (z + 4 - k) % 4])

        @pl.loop(0, 2)
        def _(pair):
            base = pl.multiple_of(pair * 384, 128)
            c_k = pl.ds(pl.multiple_of(base + 128, 128), 128)
            c_v = pl.ds(pl.multiple_of(base + 256, 128), 128)
            q = flat(r.qkv[l, :, :, pl.ds(base, 128)]) * jnp.asarray(0.125, BF)
            kk = flat(r.qkv[l, :, :, c_k])
            vv = flat(r.qkv[l, :, :, c_v])
            do = flat(r.dojoin[l, :, :, pl.ds(pl.multiple_of(pair * 128, 128), 128)])
            dq, dk, dv = [], [], []
            for head in range(2):
                pb = r.prob[l, 2 * pair + head]
                pf = pb.astype(F32)
                dp = dot_cols(mask_head(do, head), vv)
                dv.append(dot_rows(pb, do))
                ds = (pf * (dp - jnp.sum(pf * dp, axis=-1, keepdims=True))).astype(BF)
                dq.append(dot(ds, kk))
                dk.append(dot_rows(ds, q))

            def put(cols, both, scale):
                val = jnp.where(low_lanes, both[0], both[1])
                if scale is not None:
                    val = val * scale
                r.dqkv[:, :, cols] = val.astype(BF).reshape(4, ROWS, 128)

            put(pl.ds(base, 128), dq, 0.125)
            put(c_k, dk, None)
            put(c_v, dv, None)

        @pl.loop(0, 4)
        def _(k):
            blk = (z + 4 - k) % 4

            def make(b):
                return dot_cols(r.dqkv[blk], wref("q")[l, b].reshape(256, 768))

            rs_put("dh1" + str(l), k, blk, make)

        def left_q(b):
            return flat(r.h1[l, :, :, pl.ds(pl.multiple_of(b * 256, 256), 256)])

        def right_q(cols):
            return flat(r.dqkv[:, :, cols])

        def left_o(b):
            return r.ojoin[l, b]

        def right_o(cols):
            return r.da[:, cols]

        grad_first("q", l, left_q, right_q)
        grad_first("o", l, left_o, right_o)
        gap_b()
        grad_second("q", l, left_q, right_q)
        grad_second("o", l, left_o, right_o)
        dh1 = rs_sum("dh1" + str(l))
        xin = (r.x[...] if l == 0 else r.zout[0]).astype(F32)
        dn, dg1 = norm_back(dh1, xin, gain(l, 0))
        r.vgrad[4 * l : 4 * l + 1, :] = dg1
        dx = (r.dy1[...] + dn).astype(BF)
        r.gout[l] = dx
        return dx

    r.x[...] = x_in[...]

    def gap_f0a():
        weight_c("o", 0)
        weight_d("q", 0)
        weight_c("u", 0)
        weight_c("d", 0)

    def gap_f0b():
        weight_d("o", 0)
        weight_b("q", 1)
        weight_b("o", 1)

    attn_forward(0, xhat0, None, gap_f0a, gap_f0b)
    weight_d("u", 0)
    weight_b("u", 1)
    weight_b("d", 1)
    out_proj(0, x_in[...].astype(F32))

    def gap_f0c():
        weight_d("d", 0)
        weight_c("q", 1)
        weight_c("o", 1)

    mlp_forward(0, gap_f0c)
    weight_d("q", 1)
    weight_c("u", 1)
    weight_c("d", 1)
    finish_layer(0)
    x1 = r.zout[0].astype(F32)
    xhat1, _ = normalise(x1)

    def gap_f1b():
        weight_d("o", 1)

    attn_forward(1, xhat1, None, lambda: None, gap_f1b)
    weight_d("u", 1)
    out_proj(1, r.zout[0].astype(F32))

    def gap_f1c():
        weight_d("d", 1)

    mlp_forward(1, gap_f1c)
    finish_layer(1)
    push("zo", 0, r.zout.at[1 - c], r.zother, sib)

    rs_sent("m0")
    mlp_backward(1, dz_in[...].astype(F32), lambda: None, lambda: None)
    rs_sent("m1")

    def gap_b1b():
        grad_third("d", 1)
        grad_third("u", 1)

    attn_backward(1, lambda: None, gap_b1b)
    for t in "qoud":
        sent("ga" + t + "1")
    rs_sent("dh21")

    def gap_b0a():
        grad_fourth("d", 1)
        grad_fourth("u", 1)

    def gap_b0b():
        grad_third("q", 1)
        grad_third("o", 1)

    mlp_backward(0, r.gout[1].astype(F32), gap_b0a, gap_b0b)
    rs_sent("dh11")

    def gap_b0c():
        grad_fourth("q", 1)
        grad_fourth("o", 1)

    def gap_b0d():
        grad_third("d", 0)
        grad_third("u", 0)

    attn_backward(0, gap_b0c, gap_b0d)

    push("go", 0, r.gout.at[1 - c], r.gother, sib)
    gv = r.vgrad[...]
    r.vsend[2] = gv
    push("ga", 0, r.vsend.at[2], r.vrecv.at[7], sib)
    grad_fourth("d", 0)
    grad_fourth("u", 0)
    arrived("ga", 0, r.vrecv.at[7])
    gv = gv + r.vrecv[7]
    spread("gx", 3, 8, gv, xpeer)
    grad_third("q", 0)
    grad_third("o", 0)
    gv = gathered("gx", 8, gv)
    spread("gy", 4, 11, gv, ypeer)
    grad_fourth("q", 0)
    grad_fourth("o", 0)
    gv = gathered("gy", 11, gv)
    spread("gz", 5, 14, gv, zpeer)
    for l in (1, 0):
        for t in "duqo":
            grad_done(t, l)
    push("fo", 0, r.fin.at[1 - c], r.fother, sib)
    arrived("zo", 0, r.zother)
    lo_ref[c] = r.zout[c, :TOK]
    lo_ref[1 - c] = r.zother[:TOK]
    arrived("go", 0, r.gother)
    gi_ref[c] = r.gout[c, :TOK]
    gi_ref[1 - c] = r.gother[:TOK]
    gv_ref[...] = gathered("gz", 14, gv)

    def assemble(get, which):
        for zz in range(4):
            for t in range(3):
                col = pl.multiple_of(t * 1024 + zz * 256 + which * 128, 128)
                gq_ref[:, pl.ds(col, 128)] = get(zz, t * 128, 128).astype(F32)
            gd_ref[64 * zz : 64 * zz + 64, half(512, which)] = get(zz, 1408, 512).astype(F32)
        total = get(0, 384, 512).astype(F32)
        for zz in range(1, 4):
            total = total + get(zz, 384, 512).astype(F32)
        go_ref[:, half(512, which)] = total
        ups = [get(zz, 896, 512).astype(F32) for zz in range(4)]
        for j in range(8):
            row = jnp.concatenate([u[:, 64 * j : 64 * j + 64] for u in ups], axis=1)
            gu_ref[:, pl.ds(pl.multiple_of((which * 8 + j) * 256, 256), 256)] = row

    assemble(lambda zz, at, n: r.fin[c, zz, :, at : at + n], c)
    arrived("fo", 0, r.fother)
    assemble(lambda zz, at, n: r.fother[zz, :, at : at + n], 1 - c)
    rs_sent("dh20")
    rs_sent("dh10")
    for group in {k[0]: None for k in list(pending)}:
        sent(group)


def local(acts_in, cotangent, qkv_weight, out_weight, up_weight, down_weight, vectors, image_ids):
    c = lax.axis_index("section")
    z = lax.axis_index("seq")
    p = lax.axis_index("shard")

    def halves(w):
        n = w.shape[1] // 2
        return w.reshape(64, 2, n).transpose(1, 0, 2)

    qkv = lax.dynamic_index_in_dim(qkv_weight[0].reshape(64, 3, 4, 2, 128), z, 2, False)
    qkv = qkv.transpose(2, 0, 1, 3).reshape(2, 64, 384)
    up = lax.dynamic_index_in_dim(up_weight[0].reshape(64, 16, 4, 64), z, 2, False).reshape(64, D)
    down = lax.dynamic_index_in_dim(down_weight[0].reshape(4, 64, D), z, 0, False)
    wown = jnp.concatenate([qkv, halves(out_weight[0]), halves(up), halves(down)], axis=2)
    vin = lax.dynamic_update_slice(
        jnp.zeros((8, D), F32), vectors[0].astype(F32), (4 * c, 64 * p)
    )

    def mine(a):
        a = lax.dynamic_index_in_dim(a, c, 0, False)[0]
        return jnp.pad(a, ((0, ROWS - TOK), (0, 0)))

    ids = lax.dynamic_index_in_dim(image_ids, c, 0, False)[0]
    ids = jnp.pad(ids.reshape(4, TOK), ((0, 0), (0, ROWS - TOK)), constant_values=-1).reshape(N)
    vmem = pl.BlockSpec(memory_space=pltpu.VMEM)
    out = pl.pallas_call(
        kernel,
        out_shape=(
            jax.ShapeDtypeStruct((2, TOK, D), BF),
            jax.ShapeDtypeStruct((2, TOK, D), BF),
            jax.ShapeDtypeStruct((64, 3072), F32),
            jax.ShapeDtypeStruct((64, D), F32),
            jax.ShapeDtypeStruct((64, 4096), F32),
            jax.ShapeDtypeStruct((256, D), F32),
            jax.ShapeDtypeStruct((8, D), F32),
        ),
        in_specs=[vmem, vmem, pl.BlockSpec(memory_space=pl.ANY), vmem, vmem, vmem],
        out_specs=(vmem,) * 7,
        scratch_shapes=[pltpu.VMEM(s, t) for s, t in SCRATCH.values()]
        + [pltpu.SemaphoreType.DMA((len(GROUP), 3)), pltpu.SemaphoreType.DMA((len(GROUP), 3))],
        compiler_params=pltpu.CompilerParams(
            collective_id=0, has_side_effects=True, vmem_limit_bytes=64 * 1024 * 1024 - 65536
        ),
    )(mine(acts_in), mine(cotangent), wown, vin, ids[:, None], ids[None, :])
    gv = lax.dynamic_slice(out[6], (4 * c, 64 * p), (4, 64))
    return (
        out[0][None, :, None],
        out[1][None, :, None],
        out[2][None],
        out[3][None],
        out[4][None],
        out[5][None],
        gv[None],
    )


def solution(mesh):
    placed = (
        P(None, "shard", "seq", None),
        P(None, "shard", "seq", None),
        P("section", "shard", None),
        P("section", "shard", None),
        P("section", "shard", None),
        P("section", "shard", None),
        P("section", None, "shard"),
        P(None, "shard", None),
    )
    return jax.shard_map(
        local,
        mesh=mesh,
        in_specs=placed,
        out_specs=(
            P("section", None, "shard", "seq", None),
            P("section", None, "shard", "seq", None),
            P("section", "shard", None),
            P("section", "shard", None),
            P("section", "shard", None),
            P("section", "shard", None),
            P("section", None, "shard"),
        ),
        check_vma=False,
    )
```

```python
import jax
import jax.numpy as jnp
from jax import lax
from jax.experimental import pallas as pl
from jax.experimental.pallas import tpu as pltpu
from jax.sharding import PartitionSpec as P

EPS = 1e-06
NEG = -1e30
BF = jnp.bfloat16
F32 = jnp.float32
MESH = pl.DeviceIdType.MESH
D = 1024
ROWS = 72
N = 4 * ROWS
TENSORS = {"q": (0, 384, True), "o": (384, 512, False), "u": (896, 512, True), "d": (1408, 512, False)}
HALF = 1920


def dot(a, b):
    return lax.dot_general(a, b, (((1,), (0,)), ((), ())), preferred_element_type=F32)


def dot_rows(a, b):
    return lax.dot_general(a, b, (((0,), (0,)), ((), ())), preferred_element_type=F32)


def dot_cols(a, b):
    return lax.dot_general(a, b, (((1,), (1,)), ((), ())), preferred_element_type=F32)


def normalise(values):
    centre = values - jnp.mean(values, axis=-1, keepdims=True)
    scale = lax.rsqrt(jnp.mean(centre * centre, axis=-1, keepdims=True) + EPS)
    return centre * scale, scale


def norm_back(grad, values, gain):
    xhat, scale = normalise(values)
    f = grad * gain
    dv = scale * (
        f
        - jnp.mean(f, axis=-1, keepdims=True)
        - xhat * jnp.mean(f * xhat, axis=-1, keepdims=True)
    )
    return dv, jnp.sum(grad * xhat, axis=0, keepdims=True)


def gelu_parts(u):
    cdf = 0.5 * (1.0 + lax.erf(u * 0.7071067811865476))
    slope = cdf + u * jnp.exp(-0.5 * u * u) * 0.3989422804014327
    return u * cdf, slope


SCRATCH = dict(
    ustage=((16, 64, 128), BF),
    usend=((64, 512), BF),
    xin=((ROWS, D), BF),
    dzin=((ROWS, D), BF),
    vsend=((7, 8, D), F32),
    vrecv=((17, 8, D), F32),
    vec=((8, D), F32),
    vgrad=((8, D), F32),
    h1=((2, 4, ROWS, D), BF),
    qkv=((2, 4, ROWS, 768), BF),
    prob=((2, 4, N, N), BF),
    osend=((2, 4, ROWS, 256), BF),
    ojoin=((2, 4, ROWS, 256), BF),
    a=((2, ROWS, D), F32),
    y1=((2, ROWS, D), F32),
    h2=((2, 4, ROWS, D), BF),
    slope=((2, 4, ROWS, D), BF),
    g=((2, 4, ROWS, D), BF),
    stage=((2, 4, ROWS, D), BF),
    part=((6, 3, ROWS, D), BF),
    mine=((ROWS, D), F32),
    m=((2, ROWS, D), F32),
    dm=((2, 4, ROWS, D), BF),
    du=((4, ROWS, D), BF),
    dy1=((ROWS, D), F32),
    da=((ROWS, D), BF),
    dosend=((2, 4, ROWS, 256), BF),
    dojoin=((2, 4, ROWS, 256), BF),
    dqkv=((4, ROWS, 768), BF),
    zout=((2, ROWS, D), BF),
    gout=((2, ROWS, D), BF),
    zother=((ROWS, D), BF),
    gother=((ROWS, D), BF),
    fin=((2, 4, 64, HALF), BF),
    fother=((4, 64, HALF), BF),
)
for _t, (_, _h, _x) in TENSORS.items():
    SCRATCH["own" + _t] = ((2, 64, _h), BF)
    SCRATCH["w" + _t] = ((2, 2, 4, 4, 64, _h), BF)
    SCRATCH["gs" + _t] = ((4, 4, 64, _h), BF)
    SCRATCH["ra" + _t] = ((2, 4, 4, 64, _h), BF)
    SCRATCH["rb" + _t] = ((2, 3, 4, 64, _h), BF)
    SCRATCH["rc" + _t] = ((2, 3, 64, _h), BF)

GROUPS = (
    ["x", "dz", "us", "va", "vx", "vy", "ga", "gx", "gy", "gz", "zo", "go", "fo"]
    + [n + t + str(l) for n in ("A", "L", "B", "Bl", "C", "D", "ga", "gb", "gc", "ge") for t in "qoud" for l in (0, 1)]
    + [n + str(l) for n in ("h1", "h2", "o", "m", "dm", "dh2", "do", "dh1") for l in (0, 1)]
)
GROUP = {n: i for i, n in enumerate(dict.fromkeys(GROUPS))}


class Refs:
    pass


def kernel(acts, cot, wq, wo, wu, wd, vectors, ids, fin_ref, fother_ref, lo_ref, gi_ref, gv_ref, *scratch):
    r = Refs()
    for name, ref in zip(SCRATCH, scratch):
        setattr(r, name, ref)
    ssem, rsem = scratch[len(SCRATCH) :]
    c = lax.axis_index("section")
    z = lax.axis_index("seq")
    p = lax.axis_index("shard")
    y, x = p // 4, p % 4
    sib = {"section": 1 - c}

    def zpeer(k):
        return {"seq": (z + k) % 4}

    def xpeer(k):
        return {"shard": y * 4 + (x + k) % 4}

    def ypeer(k):
        return {"shard": ((y + k) % 4) * 4 + x}

    pending = {}

    def copy(group, slot, src, dst, dev):
        return pltpu.make_async_remote_copy(
            src_ref=src,
            dst_ref=dst,
            send_sem=ssem.at[GROUP[group], slot],
            recv_sem=rsem.at[GROUP[group], slot],
            device_id=dev,
            device_id_type=MESH,
        )

    def push(group, slot, src, dst, dev):
        copy(group, slot, src, dst, dev).start()
        pending[(group, slot)] = (src, dev)

    def sent(group):
        for key in [k for k in pending if k[0] == group]:
            src, dev = pending.pop(key)
            copy(group, key[1], src, src, dev).wait_send()

    def arrived(group, slot, dst):
        copy(group, slot, dst, dst, sib).wait_recv()

    def local_start(group, slot, src, dst):
        pltpu.make_async_copy(src, dst, ssem.at[GROUP[group], slot]).start()

    def local_wait(group, slot, dst):
        pltpu.make_async_copy(dst, dst, ssem.at[GROUP[group], slot]).wait()

    def piece(t, which):
        if t == "q":
            return [
                (wq.at[0, :, pl.ds(pl.multiple_of(n * 1024 + z * 256 + which * 128, 128), 128)], n * 128, 128)
                for n in range(3)
            ]
        cols = pl.ds(pl.multiple_of(which * 512, 512), 512)
        if t == "o":
            return [(wo.at[0, :, cols], 0, 512)]
        return [(wd.at[0, pl.ds(pl.multiple_of(z * 64, 64), 64), cols], 0, 512)]

    def own(t):
        return getattr(r, "own" + t)

    local_start("x", 0, acts.at[c, 0], r.xin)

    @pl.loop(0, 16)
    def _(n):
        col = pl.multiple_of(n * 256 + (z // 2) * 128, 128)
        local_start("us", 0, wu.at[0, :, pl.ds(col, 128)], r.ustage.at[n])

    for t in "qod":
        for n, (src, at, width) in enumerate(piece(t, c)):
            local_start("L" + t + "0", n, src, own(t).at[c, :, pl.ds(at, width)])
    local_start("dz", 0, cot.at[c, 0], r.dzin)

    barrier = pltpu.get_barrier_semaphore()
    for dev in [sib] + [f(k) for f in (xpeer, ypeer, zpeer) for k in (1, 2, 3)]:
        pl.semaphore_signal(barrier, inc=1, device_id=dev, device_id_type=MESH)
    rows8 = lax.broadcasted_iota(jnp.int32, (8, 128), 0)
    lanes8 = lax.broadcasted_iota(jnp.int32, (8, 128), 1)
    vown = vectors[0].astype(F32)
    vown = jnp.concatenate([vown, vown], axis=0)
    vown = jnp.concatenate([vown, vown], axis=1)
    keep = jnp.logical_and(rows8 // 4 == c, lanes8 // 64 == p % 2)
    r.vsend[6] = jnp.zeros((8, D), F32)
    r.vsend[6, :, pl.ds(pl.multiple_of((p // 2) * 128, 128), 128)] = jnp.where(keep, vown, 0.0)
    pl.semaphore_wait(barrier, 10)

    def half(h, which):
        return pl.ds(pl.multiple_of(which * h, 128), h)

    for t in "qod":
        for n, (src, at, width) in enumerate(piece(t, 1 - c)):
            push("A" + t + "0", n, src, own(t).at[c, :, pl.ds(at, width)], sib)
    push("va", 0, r.vsend.at[6], r.vrecv.at[0], sib)
    local_wait("us", 0, r.ustage)

    def up_half(which):
        lower = lax.broadcasted_iota(jnp.int32, (64, 128), 1) < 64
        tiles = []
        for n in range(4):
            first = r.ustage[8 * which + 2 * n].astype(F32)
            second = r.ustage[8 * which + 2 * n + 1].astype(F32)
            even = jnp.where(lower, first, pltpu.roll(second, 64, 1))
            odd = jnp.where(lower, pltpu.roll(first, 64, 1), second)
            tiles.append(jnp.where(z % 2 == 0, even, odd).astype(BF))
        return jnp.concatenate(tiles, axis=1)

    r.usend[...] = up_half(1 - c)
    push("Au0", 0, r.usend, own("u").at[c], sib)
    r.ownu[c] = up_half(c)

    def own_ready(t):
        for n, (_, at, width) in enumerate(piece(t, c) if t != "u" else [(None, 0, 512)]):
            if t != "u":
                local_wait("L" + t + "0", n, own(t).at[c, :, pl.ds(at, width)])
            arrived("A" + t + "0", n, own(t).at[1 - c, :, pl.ds(at, width)])

    def wref(t):
        return getattr(r, "w" + t)

    def local_copy(t, l):
        return pltpu.make_async_copy(
            own(t).at[l], wref(t).at[l, c, y, x], ssem.at[GROUP["Bl" + t + str(l)], 0]
        )

    def weight_b(t, l):
        _, h, xfirst = TENSORS[t]
        peer = xpeer if xfirst else ypeer
        for k in (1, 3, 2):
            push("B" + t + str(l), k - 1, own(t).at[l], wref(t).at[l, c, y, x], peer(k))
        local_copy(t, l).start()

    def weight_c(t, l):
        _, h, xfirst = TENSORS[t]
        local_copy(t, l).wait()
        for k in (1, 2, 3):
            if xfirst:
                arrived("B" + t + str(l), k - 1, wref(t).at[l, c, y, (x + 4 - k) % 4])
            else:
                arrived("B" + t + str(l), k - 1, wref(t).at[l, c, (y + 4 - k) % 4, x])
        line = wref(t).at[l, c, y] if xfirst else wref(t).at[l, c, :, x]
        peer = ypeer if xfirst else xpeer
        for k in (1, 3, 2):
            push("C" + t + str(l), k - 1, line, line, peer(k))

    def weight_d(t, l):
        _, h, xfirst = TENSORS[t]
        for k in (1, 2, 3):
            if xfirst:
                line = wref(t).at[l, c, (y + 4 - k) % 4]
            else:
                line = wref(t).at[l, c, :, (x + 4 - k) % 4]
            arrived("C" + t + str(l), k - 1, line)
        mine = wref(t).at[l, c]
        push("D" + t + str(l), 0, mine, mine, sib)

    def weight_done(t, l):
        arrived("D" + t + str(l), 0, wref(t).at[l, 1 - c])

    def spread(group, at, slots, value, peer):
        r.vsend[at] = value
        for k in (1, 2, 3):
            push(group, k - 1, r.vsend.at[at], r.vrecv.at[slots + k - 1], peer(k))

    def gathered(group, slots, value):
        for k in (1, 2, 3):
            arrived(group, k - 1, r.vrecv.at[slots + k - 1])
        return value + (r.vrecv[slots] + (r.vrecv[slots + 1] + r.vrecv[slots + 2]))

    own_ready("q")
    weight_b("q", 0)
    arrived("va", 0, r.vrecv.at[0])
    v = r.vsend[6] + r.vrecv[0]
    spread("vx", 0, 1, v, xpeer)
    own_ready("o")
    weight_b("o", 0)
    own_ready("u")
    weight_b("u", 0)
    own_ready("d")
    weight_b("d", 0)
    local_wait("x", 0, r.xin)
    xhat0, _ = normalise(r.xin[...].astype(F32))
    v = gathered("vx", 1, v)
    spread("vy", 1, 4, v, ypeer)
    weight_c("q", 0)
    v = gathered("vy", 4, v)
    r.vec[...] = v

    def gain(l, row):
        return r.vec[4 * l + row : 4 * l + row + 1, :]

    def send_block(group, ref):
        for k in (1, 2, 3):
            push(group, k - 1, ref.at[z], ref.at[z], zpeer(k))

    def flat(value):
        return value.reshape(N, value.shape[-1])

    def weight(t, l, j):
        return wref(t)[l, j // 2, :, :, :, 256 * (j % 2) : 256 * (j % 2) + 256].reshape(D, 256)

    def dot_weight_rows(rows, t, l, b):
        _, h, _ = TENSORS[t]
        first = dot_cols(rows[:, :h], wref(t)[l, 0, b].reshape(256, h))
        return first + dot_cols(rows[:, h:], wref(t)[l, 1, b].reshape(256, h))

    def image(axis):
        row = ids[c]
        place = lax.broadcasted_iota(jnp.int32, (N, 1) if axis == 0 else (1, N), axis)
        one = jnp.sum((row < 1).astype(jnp.int32), axis=1, keepdims=True)
        two = jnp.sum((row < 2).astype(jnp.int32), axis=1, keepdims=True)
        return (place >= one).astype(jnp.int32) + (place >= two).astype(jnp.int32)

    lanes = lax.broadcasted_iota(jnp.int32, (1, 128), 1)
    low_lanes = lanes < 64

    def mask_head(value, head):
        keep = low_lanes if head == 0 else jnp.logical_not(low_lanes)
        return jnp.where(keep, value, jnp.zeros_like(value))

    RS = {"m0": 0, "m1": 1, "dh21": 2, "dh11": 3, "dh20": 4, "dh10": 5}

    def rs_slot(group, k, blk, start):
        i = RS[group]
        return copy(
            group, 3 - k,
            r.stage.at[i % 2, blk], r.part.at[i, 3 - k],
            {"seq": blk},
        )

    def rs_put(group, k, blk, make):
        i = RS[group]
        for j in range(4):
            val = make(j)

            @pl.when(k == 0)
            def _():
                r.mine[:, 256 * j : 256 * j + 256] = val

            @pl.when(k > 0)
            def _():
                r.stage[i % 2, blk, :, 256 * j : 256 * j + 256] = val.astype(BF)

        @pl.when(k > 0)
        def _():
            rs_slot(group, k, blk, True).start()

    def rs_sum(group):
        i = RS[group]
        for s in range(3):
            arrived(group, s, r.part.at[i, s])
        return r.mine[...] + (
            r.part[i, 0].astype(F32) + (r.part[i, 1].astype(F32) + r.part[i, 2].astype(F32))
        )

    def rs_sent(group):
        i = RS[group]
        for k in (1, 2, 3):
            rs_slot(group, k, (z + 4 - k) % 4, False).wait_send()

    def ag_wait(group, ref, k, blk):
        @pl.when(k > 0)
        def _():
            copy(group, k - 1, ref.at[blk], ref.at[blk], sib).wait_recv()

    def attn_forward(l, xhat, gap_a, gap_b):
        r.h1[l, z] = (xhat * gain(l, 0)).astype(BF)
        send_block("h1" + str(l), r.h1.at[l])
        gap_a()
        weight_done("q", l)

        @pl.loop(0, 4)
        def _(k):
            blk = (z + 4 - k) % 4
            ag_wait("h1" + str(l), r.h1.at[l], k, blk)
            for j in range(2):
                w = wref("q")[l, j].reshape(D, 384)
                r.qkv[l, blk, :, 384 * j : 384 * j + 384] = dot(r.h1[l, blk], w).astype(BF)

        gap_b()
        same = image(0) == image(1)

        @pl.loop(0, 2)
        def _(pair):
            base = pl.multiple_of(pair * 384, 128)
            q = flat(r.qkv[l, :, :, pl.ds(base, 128)])
            kk = flat(r.qkv[l, :, :, pl.ds(pl.multiple_of(base + 128, 128), 128)])
            vv = flat(r.qkv[l, :, :, pl.ds(pl.multiple_of(base + 256, 128), 128)])
            q = q * jnp.asarray(0.125, BF)
            res = []
            for head in range(2):
                s = dot_cols(mask_head(q, head), kk)
                s = jnp.where(same, s, NEG)
                e = jnp.exp(s - jnp.max(s, axis=-1, keepdims=True))
                pb = (e * (1.0 / jnp.sum(e, axis=-1, keepdims=True))).astype(BF)
                r.prob[l, 2 * pair + head] = pb
                res.append(dot(pb, vv))
            o = jnp.where(low_lanes, res[0], res[1]).astype(BF)
            r.osend[l, :, :, pl.ds(pl.multiple_of(pair * 128, 128), 128)] = o.reshape(4, ROWS, 128)

        for k in (1, 2, 3):
            blk = (z + k) % 4
            push("o" + str(l), k - 1, r.osend.at[l, blk], r.ojoin.at[l, z], zpeer(k))
        r.ojoin[l, z] = r.osend[l, z]

    def out_proj(l, xin):
        weight_done("o", l)
        for k in (1, 2, 3):
            arrived("o" + str(l), k - 1, r.ojoin.at[l, (z + 4 - k) % 4])
        for j in range(4):
            cols = pl.ds(256 * j, 256)
            acc = None
            for b in range(4):
                w = wref("o")[l, j // 2, b, :, :, 256 * (j % 2) : 256 * (j % 2) + 256].reshape(256, 256)
                term = dot(r.ojoin[l, b], w)
                acc = term if acc is None else acc + term
            r.a[l, :, cols] = acc
        y1 = xin + gain(l, 1) * r.a[l]
        r.y1[l] = y1
        yhat, _ = normalise(y1)
        r.h2[l, z] = (yhat * gain(l, 2)).astype(BF)
        send_block("h2" + str(l), r.h2.at[l])

    def mlp_forward(l, gap_a):
        gap_a()
        weight_done("u", l)
        weight_done("d", l)

        @pl.loop(0, 4)
        def _(k):
            blk = (z + 4 - k) % 4
            ag_wait("h2" + str(l), r.h2.at[l], k, blk)
            for j in range(4):
                cols = pl.ds(256 * j, 256)
                u = dot(r.h2[l, blk], weight("u", l, j))
                g, slope = gelu_parts(u)
                r.g[l, blk, :, cols] = g.astype(BF)
                r.slope[l, blk, :, cols] = slope.astype(BF)

            def make(j):
                return dot(r.g[l, blk], weight("d", l, j))

            rs_put("m" + str(l), k, blk, make)

    def finish_layer(l):
        m = rs_sum("m" + str(l))
        r.m[l] = m
        r.zout[l] = (r.y1[l] + gain(l, 3) * m).astype(BF)

    def grad_first(t, l, left, right):
        _, h, _ = TENSORS[t]
        gs = getattr(r, "gs" + t)

        @pl.loop(0, 4)
        def _(b):
            gs[b] = dot_rows(left(b), right(half(h, 1 - c))).astype(BF).reshape(4, 64, h)

        push("ga" + t + str(l), 0, gs, getattr(r, "ra" + t).at[l], sib)

    def grad_second(t, l, left, right):
        _, h, xfirst = TENSORS[t]
        ra = getattr(r, "ra" + t)
        arrived("ga" + t + str(l), 0, ra.at[l])

        @pl.loop(0, 4)
        def _(b):
            val = dot_rows(left(b), right(half(h, c))).reshape(4, 64, h)
            ra[l, b] = (val + ra[l, b].astype(F32)).astype(BF)

        for k in (1, 2, 3):
            if xfirst:
                src, dev = ra.at[l, (y + k) % 4], ypeer(k)
            else:
                src, dev = ra.at[l, :, (x + k) % 4], xpeer(k)
            push("gb" + t + str(l), k - 1, src, getattr(r, "rb" + t).at[l, k - 1], dev)

    def grad_third(t, l):
        _, h, xfirst = TENSORS[t]
        ra, rb = getattr(r, "ra" + t), getattr(r, "rb" + t)
        for k in (1, 2, 3):
            arrived("gb" + t + str(l), k - 1, rb.at[l, k - 1])

        @pl.loop(0, 4)
        def _(i):
            yy, xx = (y, i) if xfirst else (i, x)
            val = ra[l, yy, xx].astype(F32) + rb[l, 0, i].astype(F32)
            val = val + (rb[l, 1, i].astype(F32) + rb[l, 2, i].astype(F32))
            ra[l, yy, xx] = val.astype(BF)

        for k in (1, 2, 3):
            if xfirst:
                src, dev = ra.at[l, y, (x + k) % 4], xpeer(k)
            else:
                src, dev = ra.at[l, (y + k) % 4, x], ypeer(k)
            push("gc" + t + str(l), k - 1, src, getattr(r, "rc" + t).at[l, k - 1], dev)

    def grad_fourth(t, l):
        off, h, xfirst = TENSORS[t]
        ra, rc = getattr(r, "ra" + t), getattr(r, "rc" + t)
        for k in (1, 2, 3):
            arrived("gc" + t + str(l), k - 1, rc.at[l, k - 1])
        val = ra[l, y, x].astype(F32) + rc[l, 0].astype(F32)
        val = val + (rc[l, 1].astype(F32) + rc[l, 2].astype(F32))
        r.fin[l, z, :, off : off + h] = val.astype(BF)
        block = r.fin.at[l, z, :, pl.ds(off, h)]
        for k in (1, 2, 3):
            push("ge" + t + str(l), k - 1, block, block, zpeer(k))

    def grad_done(t, l):
        off, h, _ = TENSORS[t]
        for k in (1, 2, 3):
            arrived("ge" + t + str(l), k - 1, r.fin.at[l, (z + 4 - k) % 4, :, pl.ds(off, h)])

    def mlp_backward(l, dz, gap_a, gap_b):
        r.dm[l, z] = (gain(l, 3) * dz).astype(BF)
        send_block("dm" + str(l), r.dm.at[l])
        r.vgrad[4 * l + 3 : 4 * l + 4, :] = jnp.sum(dz * r.m[l], axis=0, keepdims=True)
        r.dy1[...] = dz
        gap_a()

        @pl.loop(0, 4)
        def _(k):
            blk = (z + 4 - k) % 4
            ag_wait("dm" + str(l), r.dm.at[l], k, blk)
            for b in range(4):
                cols = pl.ds(256 * b, 256)
                grad = dot_weight_rows(r.dm[l, blk], "d", l, b)
                r.du[blk, :, cols] = (grad * r.slope[l, blk, :, cols].astype(F32)).astype(BF)

            def make(b):
                return dot_weight_rows(r.du[blk], "u", l, b)

            rs_put("dh2" + str(l), k, blk, make)

        def tile(ref):
            return lambda b: flat(ref[:, :, pl.ds(pl.multiple_of(b * 256, 256), 256)])

        def cols_of(ref):
            return lambda cols: flat(ref[:, :, cols])

        g_l, h2_l, dm_l = r.g.at[l], r.h2.at[l], r.dm.at[l]
        grad_first("d", l, tile(g_l), cols_of(dm_l))
        grad_first("u", l, tile(h2_l), cols_of(r.du))
        gap_b()
        dh2 = rs_sum("dh2" + str(l))
        dn, dg2 = norm_back(dh2, r.y1[l], gain(l, 2))
        r.vgrad[4 * l + 2 : 4 * l + 3, :] = dg2
        dy1 = r.dy1[...] + dn
        r.dy1[...] = dy1
        r.da[...] = (gain(l, 1) * dy1).astype(BF)
        for b in range(4):
            r.dosend[l, b] = dot_weight_rows(r.da[...], "o", l, b).astype(BF)
        for k in (1, 2, 3):
            push("do" + str(l), k - 1, r.dosend.at[l, (z + k) % 4], r.dojoin.at[l, z], zpeer(k))
        r.dojoin[l, z] = r.dosend[l, z]
        r.vgrad[4 * l + 1 : 4 * l + 2, :] = jnp.sum(dy1 * r.a[l], axis=0, keepdims=True)
        grad_second("d", l, tile(g_l), cols_of(dm_l))
        grad_second("u", l, tile(h2_l), cols_of(r.du))

    def attn_backward(l, gap_a, gap_b):
        gap_a()
        for k in (1, 2, 3):
            arrived("do" + str(l), k - 1, r.dojoin.at[l, (z + 4 - k) % 4])

        @pl.loop(0, 2)
        def _(pair):
            base = pl.multiple_of(pair * 384, 128)
            c_k = pl.ds(pl.multiple_of(base + 128, 128), 128)
            c_v = pl.ds(pl.multiple_of(base + 256, 128), 128)
            q = flat(r.qkv[l, :, :, pl.ds(base, 128)]) * jnp.asarray(0.125, BF)
            kk = flat(r.qkv[l, :, :, c_k])
            vv = flat(r.qkv[l, :, :, c_v])
            do = flat(r.dojoin[l, :, :, pl.ds(pl.multiple_of(pair * 128, 128), 128)])
            dq, dk, dv = [], [], []
            for head in range(2):
                pb = r.prob[l, 2 * pair + head]
                pf = pb.astype(F32)
                dp = dot_cols(mask_head(do, head), vv)
                dv.append(dot_rows(pb, do))
                ds = (pf * (dp - jnp.sum(pf * dp, axis=-1, keepdims=True))).astype(BF)
                dq.append(dot(ds, kk))
                dk.append(dot_rows(ds, q))

            def put(cols, both, scale):
                val = jnp.where(low_lanes, both[0], both[1])
                if scale is not None:
                    val = val * scale
                r.dqkv[:, :, cols] = val.astype(BF).reshape(4, ROWS, 128)

            put(pl.ds(base, 128), dq, 0.125)
            put(c_k, dk, None)
            put(c_v, dv, None)

        @pl.loop(0, 4)
        def _(k):
            blk = (z + 4 - k) % 4

            def make(b):
                return dot_weight_rows(r.dqkv[blk], "q", l, b)

            rs_put("dh1" + str(l), k, blk, make)

        def left_q(b):
            return flat(r.h1[l, :, :, pl.ds(pl.multiple_of(b * 256, 256), 256)])

        def right_q(cols):
            return flat(r.dqkv[:, :, cols])

        def left_o(b):
            return r.ojoin[l, b]

        def right_o(cols):
            return r.da[:, cols]

        grad_first("q", l, left_q, right_q)
        grad_first("o", l, left_o, right_o)
        gap_b()
        grad_second("q", l, left_q, right_q)
        grad_second("o", l, left_o, right_o)
        dh1 = rs_sum("dh1" + str(l))
        xin = (r.xin[...] if l == 0 else r.zout[0]).astype(F32)
        dn, dg1 = norm_back(dh1, xin, gain(l, 0))
        r.vgrad[4 * l : 4 * l + 1, :] = dg1
        dx = (r.dy1[...] + dn).astype(BF)
        r.gout[l] = dx
        return dx

    def gap_f0a():
        weight_c("o", 0)
        weight_d("q", 0)
        weight_c("u", 0)
        weight_c("d", 0)

    def gap_f0b():
        weight_d("o", 0)

    attn_forward(0, xhat0, gap_f0a, gap_f0b)
    weight_b("q", 1)
    weight_b("o", 1)
    out_proj(0, r.xin[...].astype(F32))

    def gap_f0c():
        weight_d("u", 0)
        weight_d("d", 0)
        weight_c("q", 1)
        weight_c("o", 1)
        weight_b("u", 1)
        weight_b("d", 1)

    mlp_forward(0, gap_f0c)
    weight_d("q", 1)
    weight_d("o", 1)
    weight_c("u", 1)
    weight_c("d", 1)
    finish_layer(0)
    xhat1, _ = normalise(r.zout[0].astype(F32))
    attn_forward(1, xhat1, lambda: None, lambda: None)
    out_proj(1, r.zout[0].astype(F32))

    def gap_f1c():
        weight_d("u", 1)
        weight_d("d", 1)

    mlp_forward(1, gap_f1c)
    finish_layer(1)
    push("zo", 0, r.zout.at[1 - c], r.zother, sib)

    rs_sent("m0")
    local_wait("dz", 0, r.dzin)
    mlp_backward(1, r.dzin[...].astype(F32), lambda: None, lambda: None)
    rs_sent("m1")

    def gap_b1b():
        grad_third("d", 1)
        grad_third("u", 1)

    attn_backward(1, lambda: None, gap_b1b)
    for t in "qoud":
        sent("ga" + t + "1")
    rs_sent("dh21")

    def gap_b0a():
        grad_fourth("d", 1)
        grad_fourth("u", 1)

    def gap_b0b():
        grad_third("q", 1)
        grad_third("o", 1)

    mlp_backward(0, r.gout[1].astype(F32), gap_b0a, gap_b0b)
    rs_sent("dh11")

    def gap_b0c():
        grad_fourth("q", 1)
        grad_fourth("o", 1)

    def gap_b0d():
        grad_third("d", 0)
        grad_third("u", 0)

    attn_backward(0, gap_b0c, gap_b0d)

    push("go", 0, r.gout.at[1 - c], r.gother, sib)
    gv = r.vgrad[...]
    r.vsend[2] = gv
    push("ga", 0, r.vsend.at[2], r.vrecv.at[7], sib)
    grad_fourth("d", 0)
    grad_fourth("u", 0)
    arrived("ga", 0, r.vrecv.at[7])
    gv = gv + r.vrecv[7]
    spread("gx", 3, 8, gv, xpeer)
    grad_third("q", 0)
    grad_third("o", 0)
    gv = gathered("gx", 8, gv)
    spread("gy", 4, 11, gv, ypeer)
    grad_fourth("q", 0)
    grad_fourth("o", 0)
    gv = gathered("gy", 11, gv)
    spread("gz", 5, 14, gv, zpeer)
    for l in (1, 0):
        for t in "duqo":
            grad_done(t, l)
    push("fo", 0, r.fin.at[1 - c], r.fother, sib)
    arrived("zo", 0, r.zother)
    lo_ref[c] = r.zout[c]
    lo_ref[1 - c] = r.zother[...]
    arrived("go", 0, r.gother)
    gi_ref[c] = r.gout[c]
    gi_ref[1 - c] = r.gother[...]
    fin_ref[...] = r.fin[c]
    gv_ref[...] = gathered("gz", 14, gv)
    arrived("fo", 0, r.fother)
    fother_ref[...] = r.fother[...]
    rs_sent("dh20")
    rs_sent("dh10")
    for group in {k[0]: None for k in list(pending)}:
        sent(group)


def assemble(fin, fother, lo, gi, gv, lo_ref, gi_ref, gq_ref, go_ref, gu_ref, gd_ref, gv_ref):
    c = lax.axis_index("section")
    p = lax.axis_index("shard")
    for m in range(2):
        lo_ref[0, m, 0] = lo[m]
        gi_ref[0, m, 0] = gi[m]
    both = gv[:, pl.ds(pl.multiple_of((p // 2) * 128, 128), 128)]
    both = jnp.where(c == 0, both[:4], both[4:])
    gv_ref[0] = jnp.where(p % 2 == 0, both[:, :64], both[:, 64:])
    for ref, which in ((fin, c), (fother, 1 - c)):
        wide = pl.ds(pl.multiple_of(which * 512, 512), 512)
        for zz in range(4):
            for t in range(3):
                col = pl.multiple_of(t * 1024 + zz * 256 + which * 128, 128)
                gq_ref[0, :, pl.ds(col, 128)] = ref[zz, :, t * 128 : t * 128 + 128].astype(F32)
            gd_ref[0, 64 * zz : 64 * zz + 64, wide] = ref[zz, :, 1408:1920].astype(F32)
        total = ref[0, :, 384:896].astype(F32)
        for zz in range(1, 4):
            total = total + ref[zz, :, 384:896].astype(F32)
        go_ref[0, :, wide] = total
        ups = [ref[zz, :, 896:1408].astype(F32) for zz in range(4)]
        for n in range(8):
            row = jnp.concatenate([u[:, 64 * n : 64 * n + 64] for u in ups], axis=1)
            gu_ref[0, :, pl.ds(pl.multiple_of((which * 8 + n) * 256, 256), 256)] = row


def local(acts_in, cotangent, qkv_weight, out_weight, up_weight, down_weight, vectors, image_ids):
    vmem = pl.BlockSpec(memory_space=pltpu.VMEM)
    hbm = pl.BlockSpec(memory_space=pl.ANY)
    out = pl.pallas_call(
        kernel,
        out_shape=(
            jax.ShapeDtypeStruct((4, 64, HALF), BF),
            jax.ShapeDtypeStruct((4, 64, HALF), BF),
            jax.ShapeDtypeStruct((2, ROWS, D), BF),
            jax.ShapeDtypeStruct((2, ROWS, D), BF),
            jax.ShapeDtypeStruct((8, D), F32),
        ),
        in_specs=[hbm] * 6 + [vmem] * 2,
        out_specs=(vmem,) * 5,
        scratch_shapes=[pltpu.VMEM(s, t) for s, t in SCRATCH.values()]
        + [pltpu.SemaphoreType.DMA((len(GROUP), 3)), pltpu.SemaphoreType.DMA((len(GROUP), 3))],
        compiler_params=pltpu.CompilerParams(
            collective_id=0, has_side_effects=True, vmem_limit_bytes=64 * 1024 * 1024 - 65536
        ),
    )(acts_in, cotangent, qkv_weight, out_weight, up_weight, down_weight, vectors, image_ids)
    return pl.pallas_call(
        assemble,
        out_shape=(
            jax.ShapeDtypeStruct((1, 2, 1, ROWS, D), BF),
            jax.ShapeDtypeStruct((1, 2, 1, ROWS, D), BF),
            jax.ShapeDtypeStruct((1, 64, 3072), F32),
            jax.ShapeDtypeStruct((1, 64, D), F32),
            jax.ShapeDtypeStruct((1, 64, 4096), F32),
            jax.ShapeDtypeStruct((1, 256, D), F32),
            jax.ShapeDtypeStruct((1, 4, 64), F32),
        ),
        in_specs=[vmem] * 5,
        out_specs=(vmem,) * 7,
        compiler_params=pltpu.CompilerParams(vmem_limit_bytes=32 * 1024 * 1024),
    )(*out)


def solution(mesh):
    placed = (
        P(None, "shard", "seq", None),
        P(None, "shard", "seq", None),
        P("section", "shard", None),
        P("section", "shard", None),
        P("section", "shard", None),
        P("section", "shard", None),
        P("section", None, "shard"),
        P(None, "shard", None),
    )
    return jax.shard_map(
        local,
        mesh=mesh,
        in_specs=placed,
        out_specs=(
            P("section", None, "shard", "seq", None),
            P("section", None, "shard", "seq", None),
            P("section", "shard", None),
            P("section", "shard", None),
            P("section", "shard", None),
            P("section", "shard", None),
            P("section", None, "shard"),
        ),
        check_vma=False,
    )
```

```python
import jax
import jax.numpy as jnp
from jax import lax
from jax.experimental import pallas as pl
from jax.experimental.pallas import tpu as pltpu
from jax.sharding import PartitionSpec as P

EPS = 1e-06
NEG = -1e30
BF = jnp.bfloat16
F32 = jnp.float32
MESH = pl.DeviceIdType.MESH
D = 1024
ROWS = 72
N = 4 * ROWS
TENSORS = {"q": (0, 384, True), "o": (384, 512, False), "u": (896, 512, True), "d": (1408, 512, False)}
HALF = 1920


def dot(a, b):
    return lax.dot_general(a, b, (((1,), (0,)), ((), ())), preferred_element_type=F32)


def dot_rows(a, b):
    return lax.dot_general(a, b, (((0,), (0,)), ((), ())), preferred_element_type=F32)


def dot_cols(a, b):
    return lax.dot_general(a, b, (((1,), (1,)), ((), ())), preferred_element_type=F32)


def normalise(values):
    centre = values - jnp.mean(values, axis=-1, keepdims=True)
    scale = lax.rsqrt(jnp.mean(centre * centre, axis=-1, keepdims=True) + EPS)
    return centre * scale, scale


def norm_back(grad, values, gain):
    xhat, scale = normalise(values)
    f = grad * gain
    dv = scale * (
        f
        - jnp.mean(f, axis=-1, keepdims=True)
        - xhat * jnp.mean(f * xhat, axis=-1, keepdims=True)
    )
    return dv, jnp.sum(grad * xhat, axis=0, keepdims=True)


def gelu_parts(u):
    cdf = 0.5 * (1.0 + lax.erf(u * 0.7071067811865476))
    slope = cdf + u * jnp.exp(-0.5 * u * u) * 0.3989422804014327
    return u * cdf, slope


SCRATCH = dict(
    vectors=((1, 4, 64), BF),
    ids=((1, N), jnp.int32),
    ustage=((16, 64, 128), BF),
    usend=((64, 512), BF),
    xin=((ROWS, D), BF),
    dzin=((ROWS, D), BF),
    vsend=((7, 8, D), F32),
    vrecv=((17, 8, D), F32),
    vec=((8, D), F32),
    vgrad=((8, D), F32),
    h1=((2, 4, ROWS, D), BF),
    qkv=((2, 4, ROWS, 768), BF),
    prob=((2, 4, N, N), BF),
    wqt=((2, 768, D), BF),
    osend=((2, 4, ROWS, 256), BF),
    ojoin=((2, 4, ROWS, 256), BF),
    a=((2, ROWS, D), F32),
    y1=((2, ROWS, D), F32),
    h2=((2, 4, ROWS, D), BF),
    slope=((2, 4, ROWS, D), BF),
    g=((2, 4, ROWS, D), BF),
    stage=((2, 4, ROWS, D), BF),
    part=((6, 3, ROWS, D), BF),
    mine=((ROWS, D), F32),
    m=((2, ROWS, D), F32),
    dm=((2, 4, ROWS, D), BF),
    du=((4, ROWS, D), BF),
    dy1=((ROWS, D), F32),
    da=((ROWS, D), BF),
    dosend=((2, 4, ROWS, 256), BF),
    dojoin=((2, 4, ROWS, 256), BF),
    dqkv=((4, ROWS, 768), BF),
    zout=((2, ROWS, D), BF),
    gout=((2, ROWS, D), BF),
    fin=((2, 4, 64, HALF), BF),
)
for _t, (_, _h, _x) in TENSORS.items():
    SCRATCH["own" + _t] = ((2, 64, _h), BF)
    SCRATCH["w" + _t] = ((2, 2, 4, 4, 64, _h), BF)
    SCRATCH["lt" + _t] = ((4, 256, 4 * ROWS), BF)
    SCRATCH["gs" + _t] = ((4, 4, 64, _h), BF)
    SCRATCH["ra" + _t] = ((2, 4, 4, 64, _h), BF)
    SCRATCH["rb" + _t] = ((2, 3, 4, 64, _h), BF)
    SCRATCH["rc" + _t] = ((2, 3, 64, _h), BF)

GROUPS = (
    ["x", "dz", "us", "vin", "iin", "out", "out2", "out3", "va", "vx", "vy", "ga", "gx", "gy", "gz", "zo", "go", "fo"]
    + [n + t + str(l) for n in ("A", "L", "B", "Bl", "C", "E", "D", "ga", "gb", "gc", "ge") for t in "qoud" for l in (0, 1)]
    + [n + str(l) for n in ("h1", "h2", "o", "m", "dm", "dh2", "do", "dh1") for l in (0, 1)]
)
GROUP = {n: i for i, n in enumerate(dict.fromkeys(GROUPS))}


class Refs:
    pass


def kernel(acts, cot, wq, wo, wu, wd, vectors_in, ids_in, fin_ref, fother_ref, lo_ref, gi_ref, gv_ref, *scratch):
    r = Refs()
    for name, ref in zip(SCRATCH, scratch):
        setattr(r, name, ref)
    ssem, rsem = scratch[len(SCRATCH) :]
    c = lax.axis_index("section")
    z = lax.axis_index("seq")
    p = lax.axis_index("shard")
    y, x = p // 4, p % 4
    sib = {"section": 1 - c}

    def zpeer(k):
        return {"seq": (z + k) % 4}

    def xpeer(k):
        return {"shard": y * 4 + (x + k) % 4}

    def ypeer(k):
        return {"shard": ((y + k) % 4) * 4 + x}

    pending = {}

    def copy(group, slot, src, dst, dev):
        return pltpu.make_async_remote_copy(
            src_ref=src,
            dst_ref=dst,
            send_sem=ssem.at[GROUP[group], slot],
            recv_sem=rsem.at[GROUP[group], slot],
            device_id=dev,
            device_id_type=MESH,
        )

    def push(group, slot, src, dst, dev):
        copy(group, slot, src, dst, dev).start()
        pending[(group, slot)] = (src, dev)

    def sent(group):
        for key in [k for k in pending if k[0] == group]:
            src, dev = pending.pop(key)
            copy(group, key[1], src, src, dev).wait_send()

    def arrived(group, slot, dst):
        copy(group, slot, dst, dst, sib).wait_recv()

    def local_start(group, slot, src, dst):
        pltpu.make_async_copy(src, dst, ssem.at[GROUP[group], slot]).start()

    def local_wait(group, slot, dst):
        pltpu.make_async_copy(dst, dst, ssem.at[GROUP[group], slot]).wait()

    def piece(t, which):
        if t == "q":
            return [
                (wq.at[0, :, pl.ds(pl.multiple_of(n * 1024 + z * 256 + which * 128, 128), 128)], n * 128, 128)
                for n in range(3)
            ]
        cols = pl.ds(pl.multiple_of(which * 512, 512), 512)
        if t == "o":
            return [(wo.at[0, :, cols], 0, 512)]
        return [(wd.at[0, pl.ds(pl.multiple_of(z * 64, 64), 64), cols], 0, 512)]

    def own(t):
        return getattr(r, "own" + t)

    local_start("vin", 0, vectors_in, r.vectors)
    local_start("iin", 0, ids_in.at[c], r.ids)
    local_start("x", 0, acts.at[c, 0], r.xin)

    @pl.loop(0, 16)
    def _(n):
        col = pl.multiple_of(n * 256 + (z // 2) * 128, 128)
        local_start("us", 0, wu.at[0, :, pl.ds(col, 128)], r.ustage.at[n])

    for t in "qod":
        for n, (src, at, width) in enumerate(piece(t, c)):
            local_start("L" + t + "0", n, src, own(t).at[c, :, pl.ds(at, width)])
    local_start("dz", 0, cot.at[c, 0], r.dzin)

    barrier = pltpu.get_barrier_semaphore()
    for dev in [sib] + [f(k) for f in (xpeer, ypeer, zpeer) for k in (1, 2, 3)]:
        pl.semaphore_signal(barrier, inc=1, device_id=dev, device_id_type=MESH)
    rows8 = lax.broadcasted_iota(jnp.int32, (8, 128), 0)
    lanes8 = lax.broadcasted_iota(jnp.int32, (8, 128), 1)
    local_wait("vin", 0, r.vectors)
    vown = r.vectors[0].astype(F32)
    vown = jnp.concatenate([vown, vown], axis=0)
    vown = jnp.concatenate([vown, vown], axis=1)
    keep = jnp.logical_and(rows8 // 4 == c, lanes8 // 64 == p % 2)
    r.vsend[6] = jnp.zeros((8, D), F32)
    r.vsend[6, :, pl.ds(pl.multiple_of((p // 2) * 128, 128), 128)] = jnp.where(keep, vown, 0.0)
    pl.semaphore_wait(barrier, 10)

    def half(h, which):
        return pl.ds(pl.multiple_of(which * h, 128), h)

    for t in "qod":
        for n, (src, at, width) in enumerate(piece(t, 1 - c)):
            push("A" + t + "0", n, src, own(t).at[c, :, pl.ds(at, width)], sib)
    push("va", 0, r.vsend.at[6], r.vrecv.at[0], sib)
    local_wait("us", 0, r.ustage)

    def up_half(which):
        lower = lax.broadcasted_iota(jnp.int32, (64, 128), 1) < 64
        tiles = []
        for n in range(4):
            first = r.ustage[8 * which + 2 * n].astype(F32)
            second = r.ustage[8 * which + 2 * n + 1].astype(F32)
            even = jnp.where(lower, first, pltpu.roll(second, 64, 1))
            odd = jnp.where(lower, pltpu.roll(first, 64, 1), second)
            tiles.append(jnp.where(z % 2 == 0, even, odd).astype(BF))
        return jnp.concatenate(tiles, axis=1)

    r.usend[...] = up_half(1 - c)
    push("Au0", 0, r.usend, own("u").at[c], sib)
    r.ownu[c] = up_half(c)

    def own_ready(t):
        for n, (_, at, width) in enumerate(piece(t, c) if t != "u" else [(None, 0, 512)]):
            if t != "u":
                local_wait("L" + t + "0", n, own(t).at[c, :, pl.ds(at, width)])
            arrived("A" + t + "0", n, own(t).at[1 - c, :, pl.ds(at, width)])

    def wref(t):
        return getattr(r, "w" + t)

    def local_copy(t, l):
        return pltpu.make_async_copy(
            own(t).at[l], wref(t).at[l, c, y, x], ssem.at[GROUP["Bl" + t + str(l)], 0]
        )

    def weight_b(t, l):
        _, h, xfirst = TENSORS[t]
        peer = xpeer if xfirst else ypeer
        for k in (1, 3, 2):
            push("B" + t + str(l), k - 1, own(t).at[l], wref(t).at[l, c, y, x], peer(k))
        local_copy(t, l).start()

    def weight_c(t, l):
        _, h, xfirst = TENSORS[t]
        local_copy(t, l).wait()
        for k in (1, 2, 3):
            if xfirst:
                arrived("B" + t + str(l), k - 1, wref(t).at[l, c, y, (x + 4 - k) % 4])
            else:
                arrived("B" + t + str(l), k - 1, wref(t).at[l, c, (y + 4 - k) % 4, x])
        line = wref(t).at[l, c, y] if xfirst else wref(t).at[l, c, :, x]
        peer = ypeer if xfirst else xpeer
        for k in (1, 3):
            push("C" + t + str(l), k - 1, line, line, peer(k))

    def line_of(t, l, back, part=None):
        if TENSORS[t][2]:
            ref = wref(t).at[l, c, (y + 4 - back) % 4]
            return ref if part is None else ref.at[pl.ds(2 * part, 2)]
        if part is None:
            return wref(t).at[l, c, :, (x + 4 - back) % 4]
        return wref(t).at[l, c, pl.ds(2 * part, 2), (x + 4 - back) % 4]

    def weight_e(t, l):
        peer = ypeer if TENSORS[t][2] else xpeer
        for k, part in ((1, 0), (3, 1)):
            arrived("C" + t + str(l), k - 1, line_of(t, l, k))
            push("E" + t + str(l), k - 1, line_of(t, l, k, part), line_of(t, l, k, part), peer(k))

    def weight_d(t, l):
        for k, part in ((1, 0), (3, 1)):
            arrived("E" + t + str(l), k - 1, line_of(t, l, 2, part))
        mine = wref(t).at[l, c]
        push("D" + t + str(l), 0, mine, mine, sib)

    def weight_done(t, l):
        arrived("D" + t + str(l), 0, wref(t).at[l, 1 - c])

    def spread(group, at, slots, value, peer):
        r.vsend[at] = value
        for k in (1, 2, 3):
            push(group, k - 1, r.vsend.at[at], r.vrecv.at[slots + k - 1], peer(k))

    def gathered(group, slots, value):
        for k in (1, 2, 3):
            arrived(group, k - 1, r.vrecv.at[slots + k - 1])
        return value + (r.vrecv[slots] + (r.vrecv[slots + 1] + r.vrecv[slots + 2]))

    own_ready("q")
    weight_b("q", 0)
    arrived("va", 0, r.vrecv.at[0])
    v = r.vsend[6] + r.vrecv[0]
    spread("vx", 0, 1, v, xpeer)
    own_ready("o")
    weight_b("o", 0)
    own_ready("u")
    weight_b("u", 0)
    own_ready("d")
    weight_b("d", 0)
    local_wait("x", 0, r.xin)
    local_wait("iin", 0, r.ids)
    xhat0, _ = normalise(r.xin[...].astype(F32))
    v = gathered("vx", 1, v)
    spread("vy", 1, 4, v, ypeer)
    weight_c("q", 0)
    v = gathered("vy", 4, v)
    r.vec[...] = v

    def gain(l, row):
        return r.vec[4 * l + row : 4 * l + row + 1, :]

    def send_block(group, ref):
        for k in (1, 2, 3):
            push(group, k - 1, ref.at[z], ref.at[z], zpeer(k))

    def flat(value):
        return value.reshape(N, value.shape[-1])

    def weight(t, l, j):
        return wref(t)[l, j // 2, :, :, :, 256 * (j % 2) : 256 * (j % 2) + 256].reshape(D, 256)

    def turn(t, l):
        for n in "CED":
            sent(n + t + str(l))

        def tile(a, b):
            return wref(t).at[l, b // 2, a, :, :, pl.ds(256 * (b % 2), 256)]

        for a in range(4):
            for b in range(a, 4):
                upper = tile(a, b)[...].reshape(256, 256)
                if a < b:
                    lower = tile(b, a)[...].reshape(256, 256)
                    tile(a, b)[...] = lower.T.reshape(4, 64, 256)
                tile(b, a)[...] = upper.T.reshape(4, 64, 256)

    def turn_qkv(l):
        for h in range(2):
            for n in range(3):
                for a in range(4):
                    w = wref("q")[l, h, a, :, :, 128 * n : 128 * n + 128].reshape(256, 128)
                    r.wqt[l, 384 * h + 128 * n : 384 * h + 128 * n + 128, 256 * a : 256 * a + 256] = w.T

    def image(axis):
        row = r.ids[...]
        place = lax.broadcasted_iota(jnp.int32, (N, 1) if axis == 0 else (1, N), axis)
        one = jnp.sum((row < 1).astype(jnp.int32), axis=1, keepdims=True)
        two = jnp.sum((row < 2).astype(jnp.int32), axis=1, keepdims=True)
        return (place >= one).astype(jnp.int32) + (place >= two).astype(jnp.int32)

    lanes = lax.broadcasted_iota(jnp.int32, (1, 128), 1)
    low_lanes = lanes < 64

    def mask_head(value, head):
        keep = low_lanes if head == 0 else jnp.logical_not(low_lanes)
        return jnp.where(keep, value, jnp.zeros_like(value))

    RS = {"m0": 0, "m1": 1, "dh21": 2, "dh11": 3, "dh20": 4, "dh10": 5}

    def rs_slot(group, k, blk, start):
        i = RS[group]
        return copy(
            group, 3 - k,
            r.stage.at[i % 2, blk], r.part.at[i, 3 - k],
            {"seq": blk},
        )

    def rs_put(group, k, blk, make):
        i = RS[group]
        for j in range(4):
            val = make(j)

            @pl.when(k == 0)
            def _():
                r.mine[:, 256 * j : 256 * j + 256] = val

            @pl.when(k > 0)
            def _():
                r.stage[i % 2, blk, :, 256 * j : 256 * j + 256] = val.astype(BF)

        @pl.when(k > 0)
        def _():
            rs_slot(group, k, blk, True).start()

    def rs_sum(group):
        i = RS[group]
        for s in range(3):
            arrived(group, s, r.part.at[i, s])
        return r.mine[...] + (
            r.part[i, 0].astype(F32) + (r.part[i, 1].astype(F32) + r.part[i, 2].astype(F32))
        )

    def rs_sent(group):
        i = RS[group]
        for k in (1, 2, 3):
            rs_slot(group, k, (z + 4 - k) % 4, False).wait_send()

    def ag_wait(group, ref, k, blk):
        @pl.when(k > 0)
        def _():
            copy(group, k - 1, ref.at[blk], ref.at[blk], sib).wait_recv()

    def attn_forward(l, xhat, gap_a, gap_b):
        r.h1[l, z] = (xhat * gain(l, 0)).astype(BF)
        send_block("h1" + str(l), r.h1.at[l])
        gap_a()
        weight_done("q", l)

        @pl.loop(0, 4)
        def _(k):
            blk = (z + 4 - k) % 4
            ag_wait("h1" + str(l), r.h1.at[l], k, blk)
            for j in range(2):
                w = wref("q")[l, j].reshape(D, 384)
                r.qkv[l, blk, :, 384 * j : 384 * j + 384] = dot(r.h1[l, blk], w).astype(BF)

        gap_b()
        same = image(0) == image(1)

        @pl.loop(0, 2)
        def _(pair):
            base = pl.multiple_of(pair * 384, 128)
            q = flat(r.qkv[l, :, :, pl.ds(base, 128)])
            kk = flat(r.qkv[l, :, :, pl.ds(pl.multiple_of(base + 128, 128), 128)])
            vv = flat(r.qkv[l, :, :, pl.ds(pl.multiple_of(base + 256, 128), 128)])
            q = q * jnp.asarray(0.125, BF)
            res = []
            for head in range(2):
                s = dot_cols(mask_head(q, head), kk)
                s = jnp.where(same, s, NEG)
                e = jnp.exp(s - jnp.max(s, axis=-1, keepdims=True))
                pb = (e * (1.0 / jnp.sum(e, axis=-1, keepdims=True))).astype(BF)
                r.prob[l, 2 * pair + head] = pb
                res.append(dot(pb, vv))
            o = jnp.where(low_lanes, res[0], res[1]).astype(BF)
            r.osend[l, :, :, pl.ds(pl.multiple_of(pair * 128, 128), 128)] = o.reshape(4, ROWS, 128)

        for k in (1, 2, 3):
            blk = (z + k) % 4
            push("o" + str(l), k - 1, r.osend.at[l, blk], r.ojoin.at[l, z], zpeer(k))
        r.ojoin[l, z] = r.osend[l, z]

    def out_proj(l, xin):
        weight_done("o", l)
        for k in (1, 2, 3):
            arrived("o" + str(l), k - 1, r.ojoin.at[l, (z + 4 - k) % 4])
        for j in range(4):
            cols = pl.ds(256 * j, 256)
            acc = None
            for b in range(4):
                w = wref("o")[l, j // 2, b, :, :, 256 * (j % 2) : 256 * (j % 2) + 256].reshape(256, 256)
                term = dot(r.ojoin[l, b], w)
                acc = term if acc is None else acc + term
            r.a[l, :, cols] = acc
        y1 = xin + gain(l, 1) * r.a[l]
        r.y1[l] = y1
        yhat, _ = normalise(y1)
        r.h2[l, z] = (yhat * gain(l, 2)).astype(BF)
        send_block("h2" + str(l), r.h2.at[l])

    def mlp_forward(l, gap_a):
        gap_a()
        weight_done("u", l)
        weight_done("d", l)

        @pl.loop(0, 4)
        def _(k):
            blk = (z + 4 - k) % 4
            ag_wait("h2" + str(l), r.h2.at[l], k, blk)
            for j in range(4):
                cols = pl.ds(256 * j, 256)
                u = dot(r.h2[l, blk], weight("u", l, j))
                g, slope = gelu_parts(u)
                r.g[l, blk, :, cols] = g.astype(BF)
                r.slope[l, blk, :, cols] = slope.astype(BF)

            def make(j):
                return dot(r.g[l, blk], weight("d", l, j))

            rs_put("m" + str(l), k, blk, make)

    def finish_layer(l):
        m = rs_sum("m" + str(l))
        r.m[l] = m
        r.zout[l] = (r.y1[l] + gain(l, 3) * m).astype(BF)

    def grad_first(t, l, left, right):
        _, h, _ = TENSORS[t]
        gs, lt = getattr(r, "gs" + t), getattr(r, "lt" + t)

        @pl.loop(0, 4)
        def _(b):
            turned = left(b).T
            lt[b, :, : turned.shape[1]] = turned
            gs[b] = dot(turned, right(half(h, 1 - c))).astype(BF).reshape(4, 64, h)

        push("ga" + t + str(l), 0, gs, getattr(r, "ra" + t).at[l], sib)

    def grad_second(t, l, right):
        _, h, xfirst = TENSORS[t]
        ra, lt = getattr(r, "ra" + t), getattr(r, "lt" + t)
        depth = ROWS if t == "o" else N
        arrived("ga" + t + str(l), 0, ra.at[l])

        @pl.loop(0, 4)
        def _(b):
            val = dot(lt[b, :, :depth], right(half(h, c))).reshape(4, 64, h)
            ra[l, b] = (val + ra[l, b].astype(F32)).astype(BF)

        for k in (1, 2, 3):
            if xfirst:
                src, dev = ra.at[l, (y + k) % 4], ypeer(k)
            else:
                src, dev = ra.at[l, :, (x + k) % 4], xpeer(k)
            push("gb" + t + str(l), k - 1, src, getattr(r, "rb" + t).at[l, k - 1], dev)

    def grad_third(t, l):
        _, h, xfirst = TENSORS[t]
        ra, rb = getattr(r, "ra" + t), getattr(r, "rb" + t)
        for k in (1, 2, 3):
            arrived("gb" + t + str(l), k - 1, rb.at[l, k - 1])

        @pl.loop(0, 4)
        def _(i):
            yy, xx = (y, i) if xfirst else (i, x)
            val = ra[l, yy, xx].astype(F32) + rb[l, 0, i].astype(F32)
            val = val + (rb[l, 1, i].astype(F32) + rb[l, 2, i].astype(F32))
            ra[l, yy, xx] = val.astype(BF)

        for k in (1, 2, 3):
            if xfirst:
                src, dev = ra.at[l, y, (x + k) % 4], xpeer(k)
            else:
                src, dev = ra.at[l, (y + k) % 4, x], ypeer(k)
            push("gc" + t + str(l), k - 1, src, getattr(r, "rc" + t).at[l, k - 1], dev)

    def grad_fourth(t, l):
        off, h, xfirst = TENSORS[t]
        ra, rc = getattr(r, "ra" + t), getattr(r, "rc" + t)
        for k in (1, 2, 3):
            arrived("gc" + t + str(l), k - 1, rc.at[l, k - 1])
        val = ra[l, y, x].astype(F32) + rc[l, 0].astype(F32)
        val = val + (rc[l, 1].astype(F32) + rc[l, 2].astype(F32))
        r.fin[l, z, :, off : off + h] = val.astype(BF)
        block = r.fin.at[l, z, :, pl.ds(off, h)]
        for k in (1, 2, 3):
            push("ge" + t + str(l), k - 1, block, block, zpeer(k))

    def grad_done(t, l):
        off, h, _ = TENSORS[t]
        for k in (1, 2, 3):
            arrived("ge" + t + str(l), k - 1, r.fin.at[l, (z + 4 - k) % 4, :, pl.ds(off, h)])

    def mlp_backward(l, dz, gap_a, gap_b):
        r.dm[l, z] = (gain(l, 3) * dz).astype(BF)
        send_block("dm" + str(l), r.dm.at[l])
        r.vgrad[4 * l + 3 : 4 * l + 4, :] = jnp.sum(dz * r.m[l], axis=0, keepdims=True)
        r.dy1[...] = dz
        gap_a()

        @pl.loop(0, 4)
        def _(k):
            blk = (z + 4 - k) % 4
            ag_wait("dm" + str(l), r.dm.at[l], k, blk)
            for b in range(4):
                cols = pl.ds(256 * b, 256)
                grad = dot(r.dm[l, blk], weight("d", l, b))
                r.du[blk, :, cols] = (grad * r.slope[l, blk, :, cols].astype(F32)).astype(BF)

            def make(b):
                return dot(r.du[blk], weight("u", l, b))

            rs_put("dh2" + str(l), k, blk, make)

        def tile(ref):
            return lambda b: flat(ref[:, :, pl.ds(pl.multiple_of(b * 256, 256), 256)])

        def cols_of(ref):
            return lambda cols: flat(ref[:, :, cols])

        g_l, h2_l, dm_l = r.g.at[l], r.h2.at[l], r.dm.at[l]
        grad_first("d", l, tile(g_l), cols_of(dm_l))
        grad_first("u", l, tile(h2_l), cols_of(r.du))
        gap_b()
        dh2 = rs_sum("dh2" + str(l))
        dn, dg2 = norm_back(dh2, r.y1[l], gain(l, 2))
        r.vgrad[4 * l + 2 : 4 * l + 3, :] = dg2
        dy1 = r.dy1[...] + dn
        r.dy1[...] = dy1
        r.da[...] = (gain(l, 1) * dy1).astype(BF)
        for b in range(4):
            r.dosend[l, b] = dot(r.da[...], weight("o", l, b)).astype(BF)
        for k in (1, 2, 3):
            push("do" + str(l), k - 1, r.dosend.at[l, (z + k) % 4], r.dojoin.at[l, z], zpeer(k))
        r.dojoin[l, z] = r.dosend[l, z]
        r.vgrad[4 * l + 1 : 4 * l + 2, :] = jnp.sum(dy1 * r.a[l], axis=0, keepdims=True)
        grad_second("d", l, cols_of(dm_l))
        grad_second("u", l, cols_of(r.du))

    def attn_backward(l, gap_a, gap_b):
        gap_a()
        for k in (1, 2, 3):
            arrived("do" + str(l), k - 1, r.dojoin.at[l, (z + 4 - k) % 4])

        @pl.loop(0, 2)
        def _(pair):
            base = pl.multiple_of(pair * 384, 128)
            c_k = pl.ds(pl.multiple_of(base + 128, 128), 128)
            c_v = pl.ds(pl.multiple_of(base + 256, 128), 128)
            q = flat(r.qkv[l, :, :, pl.ds(base, 128)]) * jnp.asarray(0.125, BF)
            kk = flat(r.qkv[l, :, :, c_k])
            vv = flat(r.qkv[l, :, :, c_v])
            do = flat(r.dojoin[l, :, :, pl.ds(pl.multiple_of(pair * 128, 128), 128)])
            dq, dk, dv = [], [], []
            for head in range(2):
                pb = r.prob[l, 2 * pair + head]
                pf = pb.astype(F32)
                dp = dot_cols(mask_head(do, head), vv)
                dv.append(dot_rows(pb, do))
                ds = (pf * (dp - jnp.sum(pf * dp, axis=-1, keepdims=True))).astype(BF)
                dq.append(dot(ds, kk))
                dk.append(dot_rows(ds, q))

            def put(cols, both, scale):
                val = jnp.where(low_lanes, both[0], both[1])
                if scale is not None:
                    val = val * scale
                r.dqkv[:, :, cols] = val.astype(BF).reshape(4, ROWS, 128)

            put(pl.ds(base, 128), dq, 0.125)
            put(c_k, dk, None)
            put(c_v, dv, None)

        @pl.loop(0, 4)
        def _(k):
            blk = (z + 4 - k) % 4

            def make(b):
                return dot(r.dqkv[blk], r.wqt[l, :, 256 * b : 256 * b + 256])

            rs_put("dh1" + str(l), k, blk, make)

        def left_q(b):
            return flat(r.h1[l, :, :, pl.ds(pl.multiple_of(b * 256, 256), 256)])

        def right_q(cols):
            return flat(r.dqkv[:, :, cols])

        def left_o(b):
            return r.ojoin[l, b]

        def right_o(cols):
            return r.da[:, cols]

        grad_first("q", l, left_q, right_q)
        grad_first("o", l, left_o, right_o)
        gap_b()
        grad_second("q", l, right_q)
        grad_second("o", l, right_o)
        dh1 = rs_sum("dh1" + str(l))
        xin = (r.xin[...] if l == 0 else r.zout[0]).astype(F32)
        dn, dg1 = norm_back(dh1, xin, gain(l, 0))
        r.vgrad[4 * l : 4 * l + 1, :] = dg1
        dx = (r.dy1[...] + dn).astype(BF)
        r.gout[l] = dx
        return dx

    def gap_f0a():
        weight_c("o", 0)
        weight_e("q", 0)
        weight_e("o", 0)
        weight_c("u", 0)
        weight_c("d", 0)
        weight_d("q", 0)

    def gap_f0b():
        weight_d("o", 0)

    attn_forward(0, xhat0, gap_f0a, gap_f0b)
    weight_b("q", 1)
    weight_b("o", 1)
    turn_qkv(0)
    weight_e("u", 0)
    weight_e("d", 0)
    out_proj(0, r.xin[...].astype(F32))

    def gap_f0c():
        weight_c("q", 1)
        weight_c("o", 1)
        turn("o", 0)
        weight_d("u", 0)
        weight_d("d", 0)
        weight_b("u", 1)
        weight_b("d", 1)

    mlp_forward(0, gap_f0c)
    weight_e("q", 1)
    weight_e("o", 1)
    weight_c("u", 1)
    weight_c("d", 1)
    turn("u", 0)
    weight_d("q", 1)
    weight_d("o", 1)
    turn("d", 0)
    finish_layer(0)
    xhat1, _ = normalise(r.zout[0].astype(F32))

    def gap_f1b():
        weight_e("u", 1)
        weight_e("d", 1)

    attn_forward(1, xhat1, lambda: None, gap_f1b)
    turn_qkv(1)
    out_proj(1, r.zout[0].astype(F32))

    def gap_f1c():
        turn("o", 1)
        weight_d("u", 1)
        weight_d("d", 1)

    mlp_forward(1, gap_f1c)
    turn("u", 1)
    turn("d", 1)
    finish_layer(1)
    push("zo", 0, r.zout.at[1 - c], lo_ref.at[c], sib)
    local_start("out", 0, r.zout.at[c], lo_ref.at[c])

    rs_sent("m0")
    local_wait("dz", 0, r.dzin)
    mlp_backward(1, r.dzin[...].astype(F32), lambda: None, lambda: None)
    rs_sent("m1")

    def gap_b1b():
        grad_third("d", 1)
        grad_third("u", 1)

    attn_backward(1, lambda: None, gap_b1b)
    for t in "qoud":
        sent("ga" + t + "1")
    rs_sent("dh21")

    def gap_b0a():
        grad_fourth("d", 1)
        grad_fourth("u", 1)

    def gap_b0b():
        grad_third("q", 1)
        grad_third("o", 1)

    mlp_backward(0, r.gout[1].astype(F32), gap_b0a, gap_b0b)
    rs_sent("dh11")

    def gap_b0c():
        grad_fourth("q", 1)
        grad_fourth("o", 1)

    def gap_b0d():
        grad_third("d", 0)
        grad_third("u", 0)

    attn_backward(0, gap_b0c, gap_b0d)

    push("go", 0, r.gout.at[1 - c], gi_ref.at[c], sib)
    local_start("out", 1, r.gout.at[c], gi_ref.at[c])
    gv = r.vgrad[...]
    r.vsend[2] = gv
    push("ga", 0, r.vsend.at[2], r.vrecv.at[7], sib)
    grad_fourth("d", 0)
    grad_fourth("u", 0)
    arrived("ga", 0, r.vrecv.at[7])
    gv = gv + r.vrecv[7]
    spread("gx", 3, 8, gv, xpeer)
    grad_third("q", 0)
    grad_third("o", 0)
    gv = gathered("gx", 8, gv)
    spread("gy", 4, 11, gv, ypeer)
    grad_fourth("q", 0)
    grad_fourth("o", 0)
    gv = gathered("gy", 11, gv)
    spread("gz", 5, 14, gv, zpeer)
    for l in (1, 0):
        for t in "duqo":
            grad_done(t, l)
    push("fo", 0, r.fin.at[1 - c], fother_ref, sib)
    local_start("out", 2, r.fin.at[c], fin_ref)
    r.vgrad[...] = gathered("gz", 14, gv)
    local_start("out2", 0, r.vgrad, gv_ref)
    arrived("zo", 0, lo_ref.at[1 - c])
    arrived("go", 0, gi_ref.at[1 - c])
    arrived("fo", 0, fother_ref)
    local_wait("out", 0, lo_ref.at[c])
    local_wait("out", 1, gi_ref.at[c])
    local_wait("out", 2, fin_ref)
    local_wait("out2", 0, gv_ref)
    rs_sent("dh20")
    rs_sent("dh10")
    for group in {k[0]: None for k in list(pending)}:
        sent(group)


def assemble(fin_in, fother_in, lo, gi, gv_in, lo_ref, gi_ref, gq_ref, go_ref, gu_ref, gd_ref, gv_ref, fin, fother, gv, sem):
    c = lax.axis_index("section")
    p = lax.axis_index("shard")
    pairs = [(fin_in, fin), (fother_in, fother), (gv_in, gv)]
    pairs += [(lo.at[m], lo_ref.at[0, m, 0]) for m in range(2)]
    pairs += [(gi.at[m], gi_ref.at[0, m, 0]) for m in range(2)]
    moves = [pltpu.make_async_copy(a, b, sem.at[n]) for n, (a, b) in enumerate(pairs)]
    for move in moves:
        move.start()
    moves[2].wait()
    both = gv[:, pl.ds(pl.multiple_of((p // 2) * 128, 128), 128)]
    both = jnp.where(c == 0, both[:4], both[4:])
    gv_ref[0] = jnp.where(p % 2 == 0, both[:, :64], both[:, 64:])
    for n, ref, which in ((0, fin, c), (1, fother, 1 - c)):
        moves[n].wait()
        wide = pl.ds(pl.multiple_of(which * 512, 512), 512)
        for zz in range(4):
            for t in range(3):
                col = pl.multiple_of(t * 1024 + zz * 256 + which * 128, 128)
                gq_ref[0, :, pl.ds(col, 128)] = ref[zz, :, t * 128 : t * 128 + 128].astype(F32)
            gd_ref[0, 64 * zz : 64 * zz + 64, wide] = ref[zz, :, 1408:1920].astype(F32)
        total = ref[0, :, 384:896].astype(F32)
        for zz in range(1, 4):
            total = total + ref[zz, :, 384:896].astype(F32)
        go_ref[0, :, wide] = total
        ups = [ref[zz, :, 896:1408].astype(F32) for zz in range(4)]
        for n in range(8):
            row = jnp.concatenate([u[:, 64 * n : 64 * n + 64] for u in ups], axis=1)
            gu_ref[0, :, pl.ds(pl.multiple_of((which * 8 + n) * 256, 256), 256)] = row
    for move in moves[3:]:
        move.wait()


def local(acts_in, cotangent, qkv_weight, out_weight, up_weight, down_weight, vectors, image_ids):
    vmem = pl.BlockSpec(memory_space=pltpu.VMEM)
    hbm = pl.BlockSpec(memory_space=pl.ANY)
    out = pl.pallas_call(
        kernel,
        out_shape=(
            jax.ShapeDtypeStruct((4, 64, HALF), BF),
            jax.ShapeDtypeStruct((4, 64, HALF), BF),
            jax.ShapeDtypeStruct((2, ROWS, D), BF),
            jax.ShapeDtypeStruct((2, ROWS, D), BF),
            jax.ShapeDtypeStruct((8, D), F32),
        ),
        in_specs=[hbm] * 8,
        out_specs=(hbm,) * 5,
        scratch_shapes=[pltpu.VMEM(s, t) for s, t in SCRATCH.values()]
        + [pltpu.SemaphoreType.DMA((len(GROUP), 3)), pltpu.SemaphoreType.DMA((len(GROUP), 3))],
        compiler_params=pltpu.CompilerParams(
            collective_id=0, has_side_effects=True, vmem_limit_bytes=64 * 1024 * 1024 - 65536
        ),
    )(acts_in, cotangent, qkv_weight, out_weight, up_weight, down_weight, vectors, image_ids)
    return pl.pallas_call(
        assemble,
        out_shape=(
            jax.ShapeDtypeStruct((1, 2, 1, ROWS, D), BF),
            jax.ShapeDtypeStruct((1, 2, 1, ROWS, D), BF),
            jax.ShapeDtypeStruct((1, 64, 3072), F32),
            jax.ShapeDtypeStruct((1, 64, D), F32),
            jax.ShapeDtypeStruct((1, 64, 4096), F32),
            jax.ShapeDtypeStruct((1, 256, D), F32),
            jax.ShapeDtypeStruct((1, 4, 64), F32),
        ),
        in_specs=[hbm] * 5,
        out_specs=(hbm,) * 2 + (vmem,) * 5,
        scratch_shapes=[
            pltpu.VMEM((4, 64, HALF), BF),
            pltpu.VMEM((4, 64, HALF), BF),
            pltpu.VMEM((8, D), F32),
            pltpu.SemaphoreType.DMA((7,)),
        ],
        compiler_params=pltpu.CompilerParams(vmem_limit_bytes=32 * 1024 * 1024),
    )(*out)


def solution(mesh):
    placed = (
        P(None, "shard", "seq", None),
        P(None, "shard", "seq", None),
        P("section", "shard", None),
        P("section", "shard", None),
        P("section", "shard", None),
        P("section", "shard", None),
        P("section", None, "shard"),
        P(None, "shard", None),
    )
    return jax.shard_map(
        local,
        mesh=mesh,
        in_specs=placed,
        out_specs=(
            P("section", None, "shard", "seq", None),
            P("section", None, "shard", "seq", None),
            P("section", "shard", None),
            P("section", "shard", None),
            P("section", "shard", None),
            P("section", "shard", None),
            P("section", None, "shard"),
        ),
        check_vma=False,
    )
```

```python
import jax
import jax.numpy as jnp
from jax import lax
from jax.experimental import pallas as pl
from jax.experimental.pallas import tpu as pltpu
from jax.sharding import PartitionSpec as P

EPS = 1e-06
NEG = -1e30
BF = jnp.bfloat16
F32 = jnp.float32
MESH = pl.DeviceIdType.MESH
D = 1024
ROWS = 72
N = 4 * ROWS
TENSORS = {"q": (0, 384, True), "o": (384, 512, False), "u": (896, 512, True), "d": (1408, 512, False)}
HALF = 1920


def dot(a, b):
    return lax.dot_general(a, b, (((1,), (0,)), ((), ())), preferred_element_type=F32)


def dot_rows(a, b):
    return lax.dot_general(a, b, (((0,), (0,)), ((), ())), preferred_element_type=F32)


def dot_cols(a, b):
    return lax.dot_general(a, b, (((1,), (1,)), ((), ())), preferred_element_type=F32)


def normalise(values):
    centre = values - jnp.mean(values, axis=-1, keepdims=True)
    scale = lax.rsqrt(jnp.mean(centre * centre, axis=-1, keepdims=True) + EPS)
    return centre * scale, scale


def norm_back(grad, values, gain):
    xhat, scale = normalise(values)
    f = grad * gain
    dv = scale * (
        f
        - jnp.mean(f, axis=-1, keepdims=True)
        - xhat * jnp.mean(f * xhat, axis=-1, keepdims=True)
    )
    return dv, jnp.sum(grad * xhat, axis=0, keepdims=True)


def gelu_parts(u):
    cdf = 0.5 * (1.0 + lax.erf(u * 0.7071067811865476))
    slope = cdf + u * jnp.exp(-0.5 * u * u) * 0.3989422804014327
    return u * cdf, slope


SCRATCH = dict(
    vectors=((1, 4, 64), BF),
    ids=((1, N), jnp.int32),
    ustage=((16, 64, 128), BF),
    usend=((64, 512), BF),
    xall=((4, ROWS, D), BF),
    rdq=((16, 64, 384), BF),
    dzin=((ROWS, D), BF),
    vsend=((7, 8, D), F32),
    vrecv=((17, 8, D), F32),
    vec=((8, D), F32),
    vgrad=((8, D), F32),
    h1=((2, 4, ROWS, D), BF),
    qkv=((2, 4, ROWS, 768), BF),
    prob=((2, 4, N, N), BF),
    wqt=((2, 768, D), BF),
    osend=((2, 4, ROWS, 256), BF),
    ojoin=((2, 4, ROWS, 256), BF),
    a=((2, ROWS, D), F32),
    y1=((2, ROWS, D), F32),
    h2=((2, 4, ROWS, D), BF),
    slope=((2, 4, ROWS, D), BF),
    g=((2, 4, ROWS, D), BF),
    stage=((2, 4, ROWS, D), BF),
    part=((6, 3, ROWS, D), BF),
    mine=((ROWS, D), F32),
    m=((2, ROWS, D), F32),
    dm=((2, 4, ROWS, D), BF),
    du=((4, ROWS, D), BF),
    dy1=((ROWS, D), F32),
    da=((ROWS, D), BF),
    dosend=((2, 4, ROWS, 256), BF),
    dojoin=((2, 4, ROWS, 256), BF),
    dqkv=((4, ROWS, 768), BF),
    zout=((2, ROWS, D), BF),
    gout=((2, ROWS, D), BF),
    fin=((2, 4, 64, HALF), BF),
)
for _t, (_, _h, _x) in TENSORS.items():
    SCRATCH["own" + _t] = ((2, 64, _h), BF)
    SCRATCH["w" + _t] = ((2, 2, 4, 4, 64, _h), BF)
    SCRATCH["lt" + _t] = ((4, 256, 4 * ROWS), BF)
    SCRATCH["gs" + _t] = ((4, 4, 64, _h), BF)
    SCRATCH["ra" + _t] = ((2, 4, 4, 64, _h), BF)
    SCRATCH["rb" + _t] = ((2, 3, 4, 64, _h), BF)
    SCRATCH["rc" + _t] = ((2, 3, 64, _h), BF)

GROUPS = (
    ["x", "dz", "us", "vin", "iin", "out", "out2", "out3", "va", "vx", "vy", "ga", "gx", "gy", "gz", "zo", "go", "fo"]
    + [n + t + str(l) for n in ("A", "L", "B", "Bl", "C", "E", "D", "ga", "gb", "gc", "ge") for t in "qoud" for l in (0, 1)]
    + [n + str(l) for n in ("h1", "h2", "o", "m", "dm", "dh2", "do", "dh1") for l in (0, 1)]
)
ORDER = (1, 3, 4, 12, 5, 7, 13, 15, 2, 8, 6, 14, 9, 11, 10)
DIRECT = {"Q": 0, "R": 1}
GROUP = {n: i for i, n in enumerate(dict.fromkeys(GROUPS))}


class Refs:
    pass


def kernel(acts, cot, wq, wo, wu, wd, vectors_in, ids_in, fin_ref, fother_ref, lo_ref, gi_ref, gv_ref, *scratch):
    r = Refs()
    for name, ref in zip(SCRATCH, scratch):
        setattr(r, name, ref)
    ssem, rsem, ssem16, rsem16 = scratch[len(SCRATCH) :]
    c = lax.axis_index("section")
    z = lax.axis_index("seq")
    p = lax.axis_index("shard")
    y, x = p // 4, p % 4
    sib = {"section": 1 - c}

    def zpeer(k):
        return {"seq": (z + k) % 4}

    def xpeer(k):
        return {"shard": y * 4 + (x + k) % 4}

    def ypeer(k):
        return {"shard": ((y + k) % 4) * 4 + x}

    def any_peer(n):
        return {"shard": ((y + n // 4) % 4) * 4 + (x + n % 4) % 4}

    pending = {}

    def copy(group, slot, src, dst, dev):
        if group in DIRECT:
            at, send, recv = DIRECT[group], ssem16, rsem16
        else:
            at, send, recv = GROUP[group], ssem, rsem
        return pltpu.make_async_remote_copy(
            src_ref=src,
            dst_ref=dst,
            send_sem=send.at[at, slot],
            recv_sem=recv.at[at, slot],
            device_id=dev,
            device_id_type=MESH,
        )

    def push(group, slot, src, dst, dev):
        copy(group, slot, src, dst, dev).start()
        pending[(group, slot)] = (src, dev)

    def sent(group):
        for key in [k for k in pending if k[0] == group]:
            src, dev = pending.pop(key)
            copy(group, key[1], src, src, dev).wait_send()

    def arrived(group, slot, dst):
        copy(group, slot, dst, dst, sib).wait_recv()

    def local_start(group, slot, src, dst):
        pltpu.make_async_copy(src, dst, ssem.at[GROUP[group], slot]).start()

    def local_wait(group, slot, dst):
        pltpu.make_async_copy(dst, dst, ssem.at[GROUP[group], slot]).wait()

    def piece(t, which):
        if t == "q":
            return [
                (wq.at[0, :, pl.ds(pl.multiple_of(n * 1024 + z * 256 + which * 128, 128), 128)], n * 128, 128)
                for n in range(3)
            ]
        cols = pl.ds(pl.multiple_of(which * 512, 512), 512)
        if t == "o":
            return [(wo.at[0, :, cols], 0, 512)]
        return [(wd.at[0, pl.ds(pl.multiple_of(z * 64, 64), 64), cols], 0, 512)]

    def own(t):
        return getattr(r, "own" + t)

    local_start("vin", 0, vectors_in, r.vectors)
    local_start("iin", 0, ids_in.at[c], r.ids)
    local_start("x", 0, acts.at[c, 0], r.xall.at[z])

    @pl.loop(0, 16)
    def _(n):
        col = pl.multiple_of(n * 256 + (z // 2) * 128, 128)
        local_start("us", 0, wu.at[0, :, pl.ds(col, 128)], r.ustage.at[n])

    for t in "qod":
        for n, (src, at, width) in enumerate(piece(t, c)):
            local_start("L" + t + "0", n, src, own(t).at[c, :, pl.ds(at, width)])
    local_start("dz", 0, cot.at[c, 0], r.dzin)

    barrier = pltpu.get_barrier_semaphore()
    for dev in [sib] + [zpeer(k) for k in (1, 2, 3)] + [any_peer(n) for n in ORDER]:
        pl.semaphore_signal(barrier, inc=1, device_id=dev, device_id_type=MESH)
    rows8 = lax.broadcasted_iota(jnp.int32, (8, 128), 0)
    lanes8 = lax.broadcasted_iota(jnp.int32, (8, 128), 1)
    local_wait("vin", 0, r.vectors)
    vown = r.vectors[0].astype(F32)
    vown = jnp.concatenate([vown, vown], axis=0)
    vown = jnp.concatenate([vown, vown], axis=1)
    keep = jnp.logical_and(rows8 // 4 == c, lanes8 // 64 == p % 2)
    r.vsend[6] = jnp.zeros((8, D), F32)
    r.vsend[6, :, pl.ds(pl.multiple_of((p // 2) * 128, 128), 128)] = jnp.where(keep, vown, 0.0)
    pl.semaphore_wait(barrier, 19)

    def half(h, which):
        return pl.ds(pl.multiple_of(which * h, 128), h)

    def push_own(t):
        for n, (src, at, width) in enumerate(piece(t, 1 - c)):
            push("A" + t + "0", n, src, own(t).at[c, :, pl.ds(at, width)], sib)

    push_own("q")
    for k in (1, 3):
        push("h10", k - 1, acts.at[c, 0], r.xall.at[z], zpeer(k))
    push_own("o")
    push_own("d")
    push("va", 0, r.vsend.at[6], r.vrecv.at[0], sib)
    local_wait("us", 0, r.ustage)

    def up_half(which):
        lower = lax.broadcasted_iota(jnp.int32, (64, 128), 1) < 64
        tiles = []
        for n in range(4):
            first = r.ustage[8 * which + 2 * n].astype(F32)
            second = r.ustage[8 * which + 2 * n + 1].astype(F32)
            even = jnp.where(lower, first, pltpu.roll(second, 64, 1))
            odd = jnp.where(lower, pltpu.roll(first, 64, 1), second)
            tiles.append(jnp.where(z % 2 == 0, even, odd).astype(BF))
        return jnp.concatenate(tiles, axis=1)

    r.usend[...] = up_half(1 - c)
    push("Au0", 0, r.usend, own("u").at[c], sib)
    r.ownu[c] = up_half(c)

    def own_ready(t):
        for n, (_, at, width) in enumerate(piece(t, c) if t != "u" else [(None, 0, 512)]):
            if t != "u":
                local_wait("L" + t + "0", n, own(t).at[c, :, pl.ds(at, width)])
            arrived("A" + t + "0", n, own(t).at[1 - c, :, pl.ds(at, width)])

    def wref(t):
        return getattr(r, "w" + t)

    def local_copy(t, l):
        return pltpu.make_async_copy(
            own(t).at[l], wref(t).at[l, c, y, x], ssem.at[GROUP["Bl" + t + str(l)], 0]
        )

    def weight_b(t, l):
        _, h, xfirst = TENSORS[t]
        peer = xpeer if xfirst else ypeer
        for k in (1, 3, 2):
            push("B" + t + str(l), k - 1, own(t).at[l], wref(t).at[l, c, y, x], peer(k))
        local_copy(t, l).start()

    def weight_c(t, l):
        _, h, xfirst = TENSORS[t]
        local_copy(t, l).wait()
        for k in (1, 2, 3):
            if xfirst:
                arrived("B" + t + str(l), k - 1, wref(t).at[l, c, y, (x + 4 - k) % 4])
            else:
                arrived("B" + t + str(l), k - 1, wref(t).at[l, c, (y + 4 - k) % 4, x])
        line = wref(t).at[l, c, y] if xfirst else wref(t).at[l, c, :, x]
        peer = ypeer if xfirst else xpeer
        for k in (1, 3):
            push("C" + t + str(l), k - 1, line, line, peer(k))

    def line_of(t, l, back, part=None):
        if TENSORS[t][2]:
            ref = wref(t).at[l, c, (y + 4 - back) % 4]
            return ref if part is None else ref.at[pl.ds(2 * part, 2)]
        if part is None:
            return wref(t).at[l, c, :, (x + 4 - back) % 4]
        return wref(t).at[l, c, pl.ds(2 * part, 2), (x + 4 - back) % 4]

    def weight_e(t, l):
        peer = ypeer if TENSORS[t][2] else xpeer
        for k, part in ((1, 0), (3, 1)):
            arrived("C" + t + str(l), k - 1, line_of(t, l, k))
            push("E" + t + str(l), k - 1, line_of(t, l, k, part), line_of(t, l, k, part), peer(k))

    def weight_d(t, l):
        for k, part in ((1, 0), (3, 1)):
            arrived("E" + t + str(l), k - 1, line_of(t, l, 2, part))
        mine = wref(t).at[l, c]
        push("D" + t + str(l), 0, mine, mine, sib)

    def weight_done(t, l):
        arrived("D" + t + str(l), 0, wref(t).at[l, 1 - c])

    def spread(group, at, slots, value, peer):
        r.vsend[at] = value
        for k in (1, 2, 3):
            push(group, k - 1, r.vsend.at[at], r.vrecv.at[slots + k - 1], peer(k))

    def gathered(group, slots, value):
        for k in (1, 2, 3):
            arrived(group, k - 1, r.vrecv.at[slots + k - 1])
        return value + (r.vrecv[slots] + (r.vrecv[slots + 1] + r.vrecv[slots + 2]))

    own_ready("q")
    for n in ORDER:
        push("Q", n, own("q").at[0], wref("q").at[0, c, y, x], any_peer(n))
    local_copy("q", 0).start()
    arrived("va", 0, r.vrecv.at[0])
    v = r.vsend[6] + r.vrecv[0]
    spread("vx", 0, 1, v, xpeer)
    push("h10", 1, acts.at[c, 0], r.xall.at[z], zpeer(2))
    own_ready("o")
    weight_b("o", 0)
    own_ready("u")
    weight_b("u", 0)
    own_ready("d")
    weight_b("d", 0)
    v = gathered("vx", 1, v)
    spread("vy", 1, 4, v, ypeer)
    local_wait("iin", 0, r.ids)
    local_wait("x", 0, r.xall.at[z])
    weight_c("o", 0)
    weight_c("u", 0)
    weight_c("d", 0)
    v = gathered("vy", 4, v)
    r.vec[...] = v

    def first_qkv():
        local_copy("q", 0).wait()
        for n in ORDER:
            arrived("Q", n, wref("q").at[0, c, (y + 4 - n // 4) % 4, (x + 4 - n % 4) % 4])
        mine = wref("q").at[0, c]
        push("Dq0", 0, mine, mine, sib)

    def gain(l, row):
        return r.vec[4 * l + row : 4 * l + row + 1, :]

    def send_block(group, ref):
        for k in (1, 3):
            push(group, k - 1, ref.at[z], ref.at[z], zpeer(k))
        pending[(group, 1)] = (ref.at[z], beyond)

    beyond = zpeer(2)

    def send_beyond(group, ref, k):
        @pl.when(k == 0)
        def _():
            copy(group, 1, ref.at[z], ref.at[z], beyond).start()

    def each_block(body):
        @pl.loop(0, 4)
        def _(n):
            k = jnp.where(n == 2, 3, jnp.where(n == 3, 2, n))
            body(k, (z + 4 - k) % 4)

    def flat(value):
        return value.reshape(N, value.shape[-1])

    def weight(t, l, j):
        return wref(t)[l, j // 2, :, :, :, 256 * (j % 2) : 256 * (j % 2) + 256].reshape(D, 256)

    def turn(t, l):
        for n in "CED":
            sent(n + t + str(l))

        def tile(a, b):
            return wref(t).at[l, b // 2, a, :, :, pl.ds(256 * (b % 2), 256)]

        for a in range(4):
            for b in range(a, 4):
                upper = tile(a, b)[...].reshape(256, 256)
                if a < b:
                    lower = tile(b, a)[...].reshape(256, 256)
                    tile(a, b)[...] = lower.T.reshape(4, 64, 256)
                tile(b, a)[...] = upper.T.reshape(4, 64, 256)

    def turn_qkv(l):
        for h in range(2):
            for n in range(3):
                for a in range(4):
                    w = wref("q")[l, h, a, :, :, 128 * n : 128 * n + 128].reshape(256, 128)
                    r.wqt[l, 384 * h + 128 * n : 384 * h + 128 * n + 128, 256 * a : 256 * a + 256] = w.T

    def image(axis):
        row = r.ids[...]
        place = lax.broadcasted_iota(jnp.int32, (N, 1) if axis == 0 else (1, N), axis)
        one = jnp.sum((row < 1).astype(jnp.int32), axis=1, keepdims=True)
        two = jnp.sum((row < 2).astype(jnp.int32), axis=1, keepdims=True)
        return (place >= one).astype(jnp.int32) + (place >= two).astype(jnp.int32)

    lanes = lax.broadcasted_iota(jnp.int32, (1, 128), 1)
    low_lanes = lanes < 64

    def mask_head(value, head):
        keep = low_lanes if head == 0 else jnp.logical_not(low_lanes)
        return jnp.where(keep, value, jnp.zeros_like(value))

    RS = {"m0": 0, "m1": 1, "dh21": 2, "dh11": 3, "dh20": 4, "dh10": 5}

    def rs_slot(group, k, blk, start):
        i = RS[group]
        return copy(
            group, 3 - k,
            r.stage.at[i % 2, blk], r.part.at[i, 3 - k],
            {"seq": blk},
        )

    def rs_put(group, k, blk, make):
        i = RS[group]
        for j in range(4):
            val = make(j)

            @pl.when(k == 0)
            def _():
                r.mine[:, 256 * j : 256 * j + 256] = val

            @pl.when(k > 0)
            def _():
                r.stage[i % 2, blk, :, 256 * j : 256 * j + 256] = val.astype(BF)

        @pl.when(k > 0)
        def _():
            rs_slot(group, k, blk, True).start()

    def rs_sum(group):
        i = RS[group]
        for s in range(3):
            arrived(group, s, r.part.at[i, s])
        return r.mine[...] + (
            r.part[i, 0].astype(F32) + (r.part[i, 1].astype(F32) + r.part[i, 2].astype(F32))
        )

    def rs_sent(group):
        i = RS[group]
        for k in (1, 2, 3):
            rs_slot(group, k, (z + 4 - k) % 4, False).wait_send()

    def ag_wait(group, ref, k, blk):
        @pl.when(k > 0)
        def _():
            copy(group, k - 1, ref.at[blk], ref.at[blk], sib).wait_recv()

    def attn_forward(l, xhat, gap_a, gap_b):
        if l > 0:
            r.h1[l, z] = (xhat * gain(l, 0)).astype(BF)
            send_block("h1" + str(l), r.h1.at[l])
        gap_a()
        weight_done("q", l)

        def body(k, blk):
            if l > 0:
                ag_wait("h1" + str(l), r.h1.at[l], k, blk)
            else:
                ag_wait("h10", r.xall, k, blk)
                hat, _ = normalise(r.xall[blk].astype(F32))
                r.h1[0, blk] = (hat * gain(0, 0)).astype(BF)
            for j in range(2):
                w = wref("q")[l, j].reshape(D, 384)
                r.qkv[l, blk, :, 384 * j : 384 * j + 384] = dot(r.h1[l, blk], w).astype(BF)
            if l > 0:
                send_beyond("h1" + str(l), r.h1.at[l], k)

        each_block(body)

        gap_b()
        same = image(0) == image(1)

        @pl.loop(0, 2)
        def _(pair):
            base = pl.multiple_of(pair * 384, 128)
            q = flat(r.qkv[l, :, :, pl.ds(base, 128)])
            kk = flat(r.qkv[l, :, :, pl.ds(pl.multiple_of(base + 128, 128), 128)])
            vv = flat(r.qkv[l, :, :, pl.ds(pl.multiple_of(base + 256, 128), 128)])
            q = q * jnp.asarray(0.125, BF)
            res = []
            for head in range(2):
                s = dot_cols(mask_head(q, head), kk)
                s = jnp.where(same, s, NEG)
                e = jnp.exp(s - jnp.max(s, axis=-1, keepdims=True))
                pb = (e * (1.0 / jnp.sum(e, axis=-1, keepdims=True))).astype(BF)
                r.prob[l, 2 * pair + head] = pb
                res.append(dot(pb, vv))
            o = jnp.where(low_lanes, res[0], res[1]).astype(BF)
            r.osend[l, :, :, pl.ds(pl.multiple_of(pair * 128, 128), 128)] = o.reshape(4, ROWS, 128)

        for k in (1, 2, 3):
            blk = (z + k) % 4
            push("o" + str(l), k - 1, r.osend.at[l, blk], r.ojoin.at[l, z], zpeer(k))
        r.ojoin[l, z] = r.osend[l, z]

    def out_proj(l, xin):
        weight_done("o", l)
        for k in (1, 2, 3):
            arrived("o" + str(l), k - 1, r.ojoin.at[l, (z + 4 - k) % 4])
        for j in range(4):
            cols = pl.ds(256 * j, 256)
            acc = None
            for b in range(4):
                w = wref("o")[l, j // 2, b, :, :, 256 * (j % 2) : 256 * (j % 2) + 256].reshape(256, 256)
                term = dot(r.ojoin[l, b], w)
                acc = term if acc is None else acc + term
            r.a[l, :, cols] = acc
        y1 = xin + gain(l, 1) * r.a[l]
        r.y1[l] = y1
        yhat, _ = normalise(y1)
        r.h2[l, z] = (yhat * gain(l, 2)).astype(BF)
        send_block("h2" + str(l), r.h2.at[l])

    def mlp_forward(l, gap_a):
        gap_a()
        weight_done("u", l)
        weight_done("d", l)

        def body(k, blk):
            ag_wait("h2" + str(l), r.h2.at[l], k, blk)
            for j in range(4):
                cols = pl.ds(256 * j, 256)
                u = dot(r.h2[l, blk], weight("u", l, j))
                g, slope = gelu_parts(u)
                r.g[l, blk, :, cols] = g.astype(BF)
                r.slope[l, blk, :, cols] = slope.astype(BF)

            def make(j):
                return dot(r.g[l, blk], weight("d", l, j))

            rs_put("m" + str(l), k, blk, make)
            send_beyond("h2" + str(l), r.h2.at[l], k)

        each_block(body)

    def finish_layer(l):
        m = rs_sum("m" + str(l))
        r.m[l] = m
        r.zout[l] = (r.y1[l] + gain(l, 3) * m).astype(BF)

    def grad_first(t, l, left, right):
        _, h, _ = TENSORS[t]
        gs, lt = getattr(r, "gs" + t), getattr(r, "lt" + t)

        @pl.loop(0, 4)
        def _(b):
            turned = left(b).T
            lt[b, :, : turned.shape[1]] = turned
            gs[b] = dot(turned, right(half(h, 1 - c))).astype(BF).reshape(4, 64, h)

        push("ga" + t + str(l), 0, gs, getattr(r, "ra" + t).at[l], sib)

    def grad_second(t, l, right):
        _, h, xfirst = TENSORS[t]
        ra, lt = getattr(r, "ra" + t), getattr(r, "lt" + t)
        depth = ROWS if t == "o" else N
        arrived("ga" + t + str(l), 0, ra.at[l])

        @pl.loop(0, 4)
        def _(b):
            val = dot(lt[b, :, :depth], right(half(h, c))).reshape(4, 64, h)
            ra[l, b] = (val + ra[l, b].astype(F32)).astype(BF)

        if t == "q" and l == 0:
            for n in ORDER:
                src = ra.at[0, (y + n // 4) % 4, (x + n % 4) % 4]
                push("R", n, src, r.rdq.at[n], any_peer(n))
            return
        for k in (1, 2, 3):
            if xfirst:
                src, dev = ra.at[l, (y + k) % 4], ypeer(k)
            else:
                src, dev = ra.at[l, :, (x + k) % 4], xpeer(k)
            push("gb" + t + str(l), k - 1, src, getattr(r, "rb" + t).at[l, k - 1], dev)

    def grad_third(t, l):
        _, h, xfirst = TENSORS[t]
        ra, rb = getattr(r, "ra" + t), getattr(r, "rb" + t)
        for k in (1, 2, 3):
            arrived("gb" + t + str(l), k - 1, rb.at[l, k - 1])

        @pl.loop(0, 4)
        def _(i):
            yy, xx = (y, i) if xfirst else (i, x)
            val = ra[l, yy, xx].astype(F32) + rb[l, 0, i].astype(F32)
            val = val + (rb[l, 1, i].astype(F32) + rb[l, 2, i].astype(F32))
            ra[l, yy, xx] = val.astype(BF)

        for k in (1, 2, 3):
            if xfirst:
                src, dev = ra.at[l, y, (x + k) % 4], xpeer(k)
            else:
                src, dev = ra.at[l, (y + k) % 4, x], ypeer(k)
            push("gc" + t + str(l), k - 1, src, getattr(r, "rc" + t).at[l, k - 1], dev)

    def grad_fourth(t, l):
        off, h, xfirst = TENSORS[t]
        ra, rc = getattr(r, "ra" + t), getattr(r, "rc" + t)
        val = ra[l, y, x].astype(F32)
        if t == "q" and l == 0:
            for n in ORDER:
                arrived("R", n, r.rdq.at[n])
                val = val + r.rdq[n].astype(F32)
        else:
            for k in (1, 2, 3):
                arrived("gc" + t + str(l), k - 1, rc.at[l, k - 1])
            val = val + (rc[l, 0].astype(F32) + (rc[l, 1].astype(F32) + rc[l, 2].astype(F32)))
        r.fin[l, z, :, off : off + h] = val.astype(BF)
        block = r.fin.at[l, z, :, pl.ds(off, h)]
        for k in (1, 2, 3):
            push("ge" + t + str(l), k - 1, block, block, zpeer(k))

    def grad_done(t, l):
        off, h, _ = TENSORS[t]
        for k in (1, 2, 3):
            arrived("ge" + t + str(l), k - 1, r.fin.at[l, (z + 4 - k) % 4, :, pl.ds(off, h)])

    def mlp_backward(l, dz, gap_a, gap_b, gap_c):
        r.dm[l, z] = (gain(l, 3) * dz).astype(BF)
        send_block("dm" + str(l), r.dm.at[l])
        r.vgrad[4 * l + 3 : 4 * l + 4, :] = jnp.sum(dz * r.m[l], axis=0, keepdims=True)
        r.dy1[...] = dz
        gap_a()

        def body(k, blk):
            ag_wait("dm" + str(l), r.dm.at[l], k, blk)
            for b in range(4):
                cols = pl.ds(256 * b, 256)
                grad = dot(r.dm[l, blk], weight("d", l, b))
                r.du[blk, :, cols] = (grad * r.slope[l, blk, :, cols].astype(F32)).astype(BF)

            def make(b):
                return dot(r.du[blk], weight("u", l, b))

            rs_put("dh2" + str(l), k, blk, make)
            send_beyond("dm" + str(l), r.dm.at[l], k)

        each_block(body)

        def tile(ref):
            return lambda b: flat(ref[:, :, pl.ds(pl.multiple_of(b * 256, 256), 256)])

        def cols_of(ref):
            return lambda cols: flat(ref[:, :, cols])

        g_l, h2_l, dm_l = r.g.at[l], r.h2.at[l], r.dm.at[l]
        grad_first("d", l, tile(g_l), cols_of(dm_l))
        grad_first("u", l, tile(h2_l), cols_of(r.du))
        grad_second("d", l, cols_of(dm_l))
        grad_second("u", l, cols_of(r.du))
        gap_b()
        dh2 = rs_sum("dh2" + str(l))
        dn, dg2 = norm_back(dh2, r.y1[l], gain(l, 2))
        r.vgrad[4 * l + 2 : 4 * l + 3, :] = dg2
        dy1 = r.dy1[...] + dn
        r.dy1[...] = dy1
        r.da[...] = (gain(l, 1) * dy1).astype(BF)
        for b in range(4):
            r.dosend[l, b] = dot(r.da[...], weight("o", l, b)).astype(BF)
        for k in (1, 2, 3):
            push("do" + str(l), k - 1, r.dosend.at[l, (z + k) % 4], r.dojoin.at[l, z], zpeer(k))
        r.dojoin[l, z] = r.dosend[l, z]
        r.vgrad[4 * l + 1 : 4 * l + 2, :] = jnp.sum(dy1 * r.a[l], axis=0, keepdims=True)

        def right_o(cols):
            return r.da[:, cols]

        grad_first("o", l, lambda b: r.ojoin[l, b], right_o)
        gap_c()
        grad_second("o", l, right_o)

    def attn_backward(l, gap_a, gap_b):
        gap_a()
        for k in (1, 2, 3):
            arrived("do" + str(l), k - 1, r.dojoin.at[l, (z + 4 - k) % 4])

        @pl.loop(0, 2)
        def _(pair):
            base = pl.multiple_of(pair * 384, 128)
            c_k = pl.ds(pl.multiple_of(base + 128, 128), 128)
            c_v = pl.ds(pl.multiple_of(base + 256, 128), 128)
            q = flat(r.qkv[l, :, :, pl.ds(base, 128)]) * jnp.asarray(0.125, BF)
            kk = flat(r.qkv[l, :, :, c_k])
            vv = flat(r.qkv[l, :, :, c_v])
            do = flat(r.dojoin[l, :, :, pl.ds(pl.multiple_of(pair * 128, 128), 128)])
            dq, dk, dv = [], [], []
            for head in range(2):
                pb = r.prob[l, 2 * pair + head]
                pf = pb.astype(F32)
                dp = dot_cols(mask_head(do, head), vv)
                dv.append(dot_rows(pb, do))
                ds = (pf * (dp - jnp.sum(pf * dp, axis=-1, keepdims=True))).astype(BF)
                dq.append(dot(ds, kk))
                dk.append(dot_rows(ds, q))

            def put(cols, both, scale):
                val = jnp.where(low_lanes, both[0], both[1])
                if scale is not None:
                    val = val * scale
                r.dqkv[:, :, cols] = val.astype(BF).reshape(4, ROWS, 128)

            put(pl.ds(base, 128), dq, 0.125)
            put(c_k, dk, None)
            put(c_v, dv, None)

        def body(k, blk):
            def make(b):
                return dot(r.dqkv[blk], r.wqt[l, :, 256 * b : 256 * b + 256])

            rs_put("dh1" + str(l), k, blk, make)

        each_block(body)

        def left_q(b):
            return flat(r.h1[l, :, :, pl.ds(pl.multiple_of(b * 256, 256), 256)])

        def right_q(cols):
            return flat(r.dqkv[:, :, cols])

        grad_first("q", l, left_q, right_q)
        gap_b()
        grad_second("q", l, right_q)
        dh1 = rs_sum("dh1" + str(l))
        xin = (r.xall[z] if l == 0 else r.zout[0]).astype(F32)
        dn, dg1 = norm_back(dh1, xin, gain(l, 0))
        r.vgrad[4 * l : 4 * l + 1, :] = dg1
        dx = (r.dy1[...] + dn).astype(BF)
        r.gout[l] = dx
        return dx

    def gap_f0a():
        weight_e("o", 0)
        first_qkv()

    def gap_f0b():
        weight_d("o", 0)
        weight_e("u", 0)
        weight_e("d", 0)
        weight_b("q", 1)
        weight_b("o", 1)

    attn_forward(0, None, gap_f0a, gap_f0b)
    turn_qkv(0)
    out_proj(0, r.xall[z].astype(F32))

    def gap_f0c():
        weight_c("q", 1)
        weight_c("o", 1)
        turn("o", 0)
        weight_d("u", 0)
        weight_d("d", 0)
        weight_b("u", 1)
        weight_b("d", 1)

    mlp_forward(0, gap_f0c)
    weight_e("q", 1)
    weight_e("o", 1)
    weight_c("u", 1)
    weight_c("d", 1)
    turn("u", 0)
    weight_d("q", 1)
    weight_d("o", 1)
    turn("d", 0)
    finish_layer(0)
    xhat1, _ = normalise(r.zout[0].astype(F32))

    def gap_f1b():
        weight_e("u", 1)
        weight_e("d", 1)

    attn_forward(1, xhat1, lambda: None, gap_f1b)
    turn_qkv(1)
    out_proj(1, r.zout[0].astype(F32))

    def gap_f1c():
        turn("o", 1)
        weight_d("u", 1)
        weight_d("d", 1)

    mlp_forward(1, gap_f1c)
    turn("u", 1)
    turn("d", 1)
    finish_layer(1)
    push("zo", 0, r.zout.at[1 - c], lo_ref.at[c], sib)
    local_start("out", 0, r.zout.at[c], lo_ref.at[c])

    rs_sent("m0")
    def nothing():
        pass

    local_wait("dz", 0, r.dzin)
    mlp_backward(1, r.dzin[...].astype(F32), nothing, nothing, nothing)
    rs_sent("m1")
    attn_backward(1, nothing, nothing)

    def gap_b0a():
        grad_third("d", 1)
        grad_third("u", 1)
        grad_third("o", 1)
        for t in "qoud":
            sent("ga" + t + "1")
        rs_sent("dh21")

    def gap_b0b():
        grad_third("q", 1)

    def gap_b0c():
        grad_fourth("d", 1)
        grad_fourth("u", 1)
        grad_fourth("o", 1)

    mlp_backward(0, r.gout[1].astype(F32), gap_b0a, gap_b0b, gap_b0c)
    rs_sent("dh11")

    attn_backward(0, nothing, nothing)

    push("go", 0, r.gout.at[1 - c], gi_ref.at[c], sib)
    local_start("out", 1, r.gout.at[c], gi_ref.at[c])
    gv = r.vgrad[...]
    r.vsend[2] = gv
    push("ga", 0, r.vsend.at[2], r.vrecv.at[7], sib)
    grad_fourth("q", 1)
    grad_third("d", 0)
    grad_third("u", 0)
    arrived("ga", 0, r.vrecv.at[7])
    gv = gv + r.vrecv[7]
    spread("gx", 3, 8, gv, xpeer)
    grad_third("o", 0)
    grad_fourth("d", 0)
    grad_fourth("u", 0)
    gv = gathered("gx", 8, gv)
    spread("gy", 4, 11, gv, ypeer)
    grad_fourth("o", 0)
    grad_fourth("q", 0)
    gv = gathered("gy", 11, gv)
    spread("gz", 5, 14, gv, zpeer)
    for l in (1, 0):
        for t in "duqo":
            grad_done(t, l)
    push("fo", 0, r.fin.at[1 - c], fother_ref, sib)
    local_start("out", 2, r.fin.at[c], fin_ref)
    r.vgrad[...] = gathered("gz", 14, gv)
    local_start("out2", 0, r.vgrad, gv_ref)
    arrived("zo", 0, lo_ref.at[1 - c])
    arrived("go", 0, gi_ref.at[1 - c])
    arrived("fo", 0, fother_ref)
    local_wait("out", 0, lo_ref.at[c])
    local_wait("out", 1, gi_ref.at[c])
    local_wait("out", 2, fin_ref)
    local_wait("out2", 0, gv_ref)
    rs_sent("dh20")
    rs_sent("dh10")
    for group in {k[0]: None for k in list(pending)}:
        sent(group)


def assemble(fin_in, fother_in, lo, gi, gv_in, lo_ref, gi_ref, gq_ref, go_ref, gu_ref, gd_ref, gv_ref, fin, fother, gv, sem):
    c = lax.axis_index("section")
    p = lax.axis_index("shard")
    pairs = [(fin_in, fin), (fother_in, fother), (gv_in, gv)]
    pairs += [(lo.at[m], lo_ref.at[0, m, 0]) for m in range(2)]
    pairs += [(gi.at[m], gi_ref.at[0, m, 0]) for m in range(2)]
    moves = [pltpu.make_async_copy(a, b, sem.at[n]) for n, (a, b) in enumerate(pairs)]
    for move in moves:
        move.start()
    moves[2].wait()
    both = gv[:, pl.ds(pl.multiple_of((p // 2) * 128, 128), 128)]
    both = jnp.where(c == 0, both[:4], both[4:])
    gv_ref[0] = jnp.where(p % 2 == 0, both[:, :64], both[:, 64:])
    for n, ref, which in ((0, fin, c), (1, fother, 1 - c)):
        moves[n].wait()
        wide = pl.ds(pl.multiple_of(which * 512, 512), 512)
        for zz in range(4):
            for t in range(3):
                col = pl.multiple_of(t * 1024 + zz * 256 + which * 128, 128)
                gq_ref[0, :, pl.ds(col, 128)] = ref[zz, :, t * 128 : t * 128 + 128].astype(F32)
            gd_ref[0, 64 * zz : 64 * zz + 64, wide] = ref[zz, :, 1408:1920].astype(F32)
        total = ref[0, :, 384:896].astype(F32)
        for zz in range(1, 4):
            total = total + ref[zz, :, 384:896].astype(F32)
        go_ref[0, :, wide] = total
        ups = [ref[zz, :, 896:1408].astype(F32) for zz in range(4)]
        for n in range(8):
            row = jnp.concatenate([u[:, 64 * n : 64 * n + 64] for u in ups], axis=1)
            gu_ref[0, :, pl.ds(pl.multiple_of((which * 8 + n) * 256, 256), 256)] = row
    for move in moves[3:]:
        move.wait()


def local(acts_in, cotangent, qkv_weight, out_weight, up_weight, down_weight, vectors, image_ids):
    vmem = pl.BlockSpec(memory_space=pltpu.VMEM)
    hbm = pl.BlockSpec(memory_space=pl.ANY)
    out = pl.pallas_call(
        kernel,
        out_shape=(
            jax.ShapeDtypeStruct((4, 64, HALF), BF),
            jax.ShapeDtypeStruct((4, 64, HALF), BF),
            jax.ShapeDtypeStruct((2, ROWS, D), BF),
            jax.ShapeDtypeStruct((2, ROWS, D), BF),
            jax.ShapeDtypeStruct((8, D), F32),
        ),
        in_specs=[hbm] * 8,
        out_specs=(hbm,) * 5,
        scratch_shapes=[pltpu.VMEM(s, t) for s, t in SCRATCH.values()]
        + [pltpu.SemaphoreType.DMA((len(GROUP), 3)), pltpu.SemaphoreType.DMA((len(GROUP), 3))]
        + [pltpu.SemaphoreType.DMA((2, 16)), pltpu.SemaphoreType.DMA((2, 16))],
        compiler_params=pltpu.CompilerParams(
            collective_id=0, has_side_effects=True, vmem_limit_bytes=64 * 1024 * 1024 - 65536
        ),
    )(acts_in, cotangent, qkv_weight, out_weight, up_weight, down_weight, vectors, image_ids)
    return pl.pallas_call(
        assemble,
        out_shape=(
            jax.ShapeDtypeStruct((1, 2, 1, ROWS, D), BF),
            jax.ShapeDtypeStruct((1, 2, 1, ROWS, D), BF),
            jax.ShapeDtypeStruct((1, 64, 3072), F32),
            jax.ShapeDtypeStruct((1, 64, D), F32),
            jax.ShapeDtypeStruct((1, 64, 4096), F32),
            jax.ShapeDtypeStruct((1, 256, D), F32),
            jax.ShapeDtypeStruct((1, 4, 64), F32),
        ),
        in_specs=[hbm] * 5,
        out_specs=(hbm,) * 2 + (vmem,) * 5,
        scratch_shapes=[
            pltpu.VMEM((4, 64, HALF), BF),
            pltpu.VMEM((4, 64, HALF), BF),
            pltpu.VMEM((8, D), F32),
            pltpu.SemaphoreType.DMA((7,)),
        ],
        compiler_params=pltpu.CompilerParams(vmem_limit_bytes=64 * 1024 * 1024 - 65536),
    )(*out)


def solution(mesh):
    placed = (
        P(None, "shard", "seq", None),
        P(None, "shard", "seq", None),
        P("section", "shard", None),
        P("section", "shard", None),
        P("section", "shard", None),
        P("section", "shard", None),
        P("section", None, "shard"),
        P(None, "shard", None),
    )
    return jax.shard_map(
        local,
        mesh=mesh,
        in_specs=placed,
        out_specs=(
            P("section", None, "shard", "seq", None),
            P("section", None, "shard", "seq", None),
            P("section", "shard", None),
            P("section", "shard", None),
            P("section", "shard", None),
            P("section", "shard", None),
            P("section", None, "shard"),
        ),
        check_vma=False,
    )
```

```python
import jax
import jax.numpy as jnp
from jax import lax
from jax.experimental import pallas as pl
from jax.experimental.pallas import tpu as pltpu
from jax.sharding import PartitionSpec as P

EPS = 1e-06
NEG = -1e30
BF = jnp.bfloat16
F32 = jnp.float32
MESH = pl.DeviceIdType.MESH
D = 1024
ROWS = 72
N = 4 * ROWS
TENSORS = {"q": (0, 384, True), "o": (384, 512, False), "u": (896, 512, True), "d": (1408, 512, False)}
HALF = 1920


def dot(a, b):
    return lax.dot_general(a, b, (((1,), (0,)), ((), ())), preferred_element_type=F32)


def dot_rows(a, b):
    return lax.dot_general(a, b, (((0,), (0,)), ((), ())), preferred_element_type=F32)


def dot_cols(a, b):
    return lax.dot_general(a, b, (((1,), (1,)), ((), ())), preferred_element_type=F32)


def normalise(values):
    centre = values - jnp.mean(values, axis=-1, keepdims=True)
    scale = lax.rsqrt(jnp.mean(centre * centre, axis=-1, keepdims=True) + EPS)
    return centre * scale, scale


def norm_back(grad, values, gain):
    xhat, scale = normalise(values)
    f = grad * gain
    dv = scale * (
        f
        - jnp.mean(f, axis=-1, keepdims=True)
        - xhat * jnp.mean(f * xhat, axis=-1, keepdims=True)
    )
    return dv, jnp.sum(grad * xhat, axis=0, keepdims=True)


def gelu_parts(u):
    cdf = 0.5 * (1.0 + lax.erf(u * 0.7071067811865476))
    slope = cdf + u * jnp.exp(-0.5 * u * u) * 0.3989422804014327
    return u * cdf, slope


SCRATCH = dict(
    vectors=((1, 4, 64), BF),
    ids=((1, N), jnp.int32),
    ustage=((16, 64, 128), BF),
    usend=((64, 512), BF),
    xin=((ROWS, D), BF),
    dzin=((ROWS, D), BF),
    vsend=((7, 8, D), F32),
    vrecv=((17, 8, D), F32),
    vec=((8, D), F32),
    vgrad=((8, D), F32),
    h1=((2, 4, ROWS, D), BF),
    qkv=((2, 4, ROWS, 768), BF),
    prob=((2, 4, N, N), BF),
    wqt=((2, 768, D), BF),
    osend=((2, 4, ROWS, 256), BF),
    ojoin=((2, 4, ROWS, 256), BF),
    a=((2, ROWS, D), F32),
    y1=((2, ROWS, D), F32),
    h2=((2, 4, ROWS, D), BF),
    slope=((2, 4, ROWS, D), BF),
    g=((2, 4, ROWS, D), BF),
    stage=((2, 4, ROWS, D), BF),
    part=((6, 3, ROWS, D), BF),
    mine=((ROWS, D), F32),
    m=((2, ROWS, D), F32),
    dm=((2, 4, ROWS, D), BF),
    du=((4, ROWS, D), BF),
    dy1=((ROWS, D), F32),
    da=((ROWS, D), BF),
    dosend=((2, 4, ROWS, 256), BF),
    dojoin=((2, 4, ROWS, 256), BF),
    dqkv=((4, ROWS, 768), BF),
    zout=((2, ROWS, D), BF),
    gout=((2, ROWS, D), BF),
    fin=((2, 4, 64, HALF), BF),
)
for _t, (_, _h, _x) in TENSORS.items():
    SCRATCH["own" + _t] = ((2, 64, _h), BF)
    SCRATCH["w" + _t] = ((2, 2, 4, 4, 64, _h), BF)
    SCRATCH["lt" + _t] = ((4, 256, 4 * ROWS), BF)
    SCRATCH["gs" + _t] = ((4, 4, 64, _h), BF)
    SCRATCH["ra" + _t] = ((2, 4, 4, 64, _h), BF)
    SCRATCH["rb" + _t] = ((2, 3, 4, 64, _h), BF)
    SCRATCH["rc" + _t] = ((2, 3, 64, _h), BF)

GROUPS = (
    ["x", "dz", "us", "vin", "iin", "out", "out2", "out3", "va", "vx", "vy", "ga", "gx", "gy", "gz", "zo", "go", "fo"]
    + [n + t + str(l) for n in ("A", "L", "B", "Bl", "C", "E", "D", "ga", "gb", "gc", "ge") for t in "qoud" for l in (0, 1)]
    + [n + str(l) for n in ("h1", "h2", "o", "m", "dm", "dh2", "do", "dh1") for l in (0, 1)]
)
GROUP = {n: i for i, n in enumerate(dict.fromkeys(GROUPS))}


class Refs:
    pass


def kernel(acts, cot, wq, wo, wu, wd, vectors_in, ids_in, fin_ref, fother_ref, lo_ref, gi_ref, gv_ref, *scratch):
    r = Refs()
    for name, ref in zip(SCRATCH, scratch):
        setattr(r, name, ref)
    ssem, rsem = scratch[len(SCRATCH) :]
    c = lax.axis_index("section")
    z = lax.axis_index("seq")
    p = lax.axis_index("shard")
    y, x = p // 4, p % 4
    sib = {"section": 1 - c}

    def zpeer(k):
        return {"seq": (z + k) % 4}

    def xpeer(k):
        return {"shard": y * 4 + (x + k) % 4}

    def ypeer(k):
        return {"shard": ((y + k) % 4) * 4 + x}

    pending = {}

    def copy(group, slot, src, dst, dev):
        return pltpu.make_async_remote_copy(
            src_ref=src,
            dst_ref=dst,
            send_sem=ssem.at[GROUP[group], slot],
            recv_sem=rsem.at[GROUP[group], slot],
            device_id=dev,
            device_id_type=MESH,
        )

    def push(group, slot, src, dst, dev):
        copy(group, slot, src, dst, dev).start()
        pending[(group, slot)] = (src, dev)

    def sent(group):
        for key in [k for k in pending if k[0] == group]:
            src, dev = pending.pop(key)
            copy(group, key[1], src, src, dev).wait_send()

    def arrived(group, slot, dst):
        copy(group, slot, dst, dst, sib).wait_recv()

    def local_start(group, slot, src, dst):
        pltpu.make_async_copy(src, dst, ssem.at[GROUP[group], slot]).start()

    def local_wait(group, slot, dst):
        pltpu.make_async_copy(dst, dst, ssem.at[GROUP[group], slot]).wait()

    def piece(t, which):
        if t == "q":
            return [
                (wq.at[0, :, pl.ds(pl.multiple_of(n * 1024 + z * 256 + which * 128, 128), 128)], n * 128, 128)
                for n in range(3)
            ]
        cols = pl.ds(pl.multiple_of(which * 512, 512), 512)
        if t == "o":
            return [(wo.at[0, :, cols], 0, 512)]
        return [(wd.at[0, pl.ds(pl.multiple_of(z * 64, 64), 64), cols], 0, 512)]

    def own(t):
        return getattr(r, "own" + t)

    local_start("vin", 0, vectors_in, r.vectors)
    local_start("iin", 0, ids_in.at[c], r.ids)
    local_start("x", 0, acts.at[c, 0], r.xin)

    @pl.loop(0, 16)
    def _(n):
        col = pl.multiple_of(n * 256 + (z // 2) * 128, 128)
        local_start("us", 0, wu.at[0, :, pl.ds(col, 128)], r.ustage.at[n])

    for t in "qod":
        for n, (src, at, width) in enumerate(piece(t, c)):
            local_start("L" + t + "0", n, src, own(t).at[c, :, pl.ds(at, width)])
    local_start("dz", 0, cot.at[c, 0], r.dzin)

    barrier = pltpu.get_barrier_semaphore()
    for dev in [sib] + [f(k) for f in (xpeer, ypeer, zpeer) for k in (1, 2, 3)]:
        pl.semaphore_signal(barrier, inc=1, device_id=dev, device_id_type=MESH)
    rows8 = lax.broadcasted_iota(jnp.int32, (8, 128), 0)
    lanes8 = lax.broadcasted_iota(jnp.int32, (8, 128), 1)
    local_wait("vin", 0, r.vectors)
    vown = r.vectors[0].astype(F32)
    vown = jnp.concatenate([vown, vown], axis=0)
    vown = jnp.concatenate([vown, vown], axis=1)
    keep = jnp.logical_and(rows8 // 4 == c, lanes8 // 64 == p % 2)
    r.vsend[6] = jnp.zeros((8, D), F32)
    r.vsend[6, :, pl.ds(pl.multiple_of((p // 2) * 128, 128), 128)] = jnp.where(keep, vown, 0.0)
    pl.semaphore_wait(barrier, 10)

    def half(h, which):
        return pl.ds(pl.multiple_of(which * h, 128), h)

    for t in "qod":
        for n, (src, at, width) in enumerate(piece(t, 1 - c)):
            push("A" + t + "0", n, src, own(t).at[c, :, pl.ds(at, width)], sib)
    push("va", 0, r.vsend.at[6], r.vrecv.at[0], sib)
    local_wait("us", 0, r.ustage)

    def up_half(which):
        lower = lax.broadcasted_iota(jnp.int32, (64, 128), 1) < 64
        tiles = []
        for n in range(4):
            first = r.ustage[8 * which + 2 * n].astype(F32)
            second = r.ustage[8 * which + 2 * n + 1].astype(F32)
            even = jnp.where(lower, first, pltpu.roll(second, 64, 1))
            odd = jnp.where(lower, pltpu.roll(first, 64, 1), second)
            tiles.append(jnp.where(z % 2 == 0, even, odd).astype(BF))
        return jnp.concatenate(tiles, axis=1)

    r.usend[...] = up_half(1 - c)
    push("Au0", 0, r.usend, own("u").at[c], sib)
    r.ownu[c] = up_half(c)

    def own_ready(t):
        for n, (_, at, width) in enumerate(piece(t, c) if t != "u" else [(None, 0, 512)]):
            if t != "u":
                local_wait("L" + t + "0", n, own(t).at[c, :, pl.ds(at, width)])
            arrived("A" + t + "0", n, own(t).at[1 - c, :, pl.ds(at, width)])

    def wref(t):
        return getattr(r, "w" + t)

    def local_copy(t, l):
        return pltpu.make_async_copy(
            own(t).at[l], wref(t).at[l, c, y, x], ssem.at[GROUP["Bl" + t + str(l)], 0]
        )

    def weight_b(t, l):
        _, h, xfirst = TENSORS[t]
        peer = xpeer if xfirst else ypeer
        for k in (1, 3, 2):
            push("B" + t + str(l), k - 1, own(t).at[l], wref(t).at[l, c, y, x], peer(k))
        local_copy(t, l).start()

    def weight_c(t, l):
        _, h, xfirst = TENSORS[t]
        local_copy(t, l).wait()
        for k in (1, 2, 3):
            if xfirst:
                arrived("B" + t + str(l), k - 1, wref(t).at[l, c, y, (x + 4 - k) % 4])
            else:
                arrived("B" + t + str(l), k - 1, wref(t).at[l, c, (y + 4 - k) % 4, x])
        line = wref(t).at[l, c, y] if xfirst else wref(t).at[l, c, :, x]
        peer = ypeer if xfirst else xpeer
        for k in (1, 3):
            push("C" + t + str(l), k - 1, line, line, peer(k))

    def line_of(t, l, back, part=None):
        if TENSORS[t][2]:
            ref = wref(t).at[l, c, (y + 4 - back) % 4]
            return ref if part is None else ref.at[pl.ds(2 * part, 2)]
        if part is None:
            return wref(t).at[l, c, :, (x + 4 - back) % 4]
        return wref(t).at[l, c, pl.ds(2 * part, 2), (x + 4 - back) % 4]

    def weight_e(t, l):
        peer = ypeer if TENSORS[t][2] else xpeer
        for k, part in ((1, 0), (3, 1)):
            arrived("C" + t + str(l), k - 1, line_of(t, l, k))
            push("E" + t + str(l), k - 1, line_of(t, l, k, part), line_of(t, l, k, part), peer(k))

    def weight_d(t, l):
        for k, part in ((1, 0), (3, 1)):
            arrived("E" + t + str(l), k - 1, line_of(t, l, 2, part))
        mine = wref(t).at[l, c]
        push("D" + t + str(l), 0, mine, mine, sib)

    def weight_done(t, l):
        arrived("D" + t + str(l), 0, wref(t).at[l, 1 - c])

    def spread(group, at, slots, value, peer):
        r.vsend[at] = value
        for k in (1, 2, 3):
            push(group, k - 1, r.vsend.at[at], r.vrecv.at[slots + k - 1], peer(k))

    def gathered(group, slots, value):
        for k in (1, 2, 3):
            arrived(group, k - 1, r.vrecv.at[slots + k - 1])
        return value + (r.vrecv[slots] + (r.vrecv[slots + 1] + r.vrecv[slots + 2]))

    own_ready("q")
    weight_b("q", 0)
    arrived("va", 0, r.vrecv.at[0])
    v = r.vsend[6] + r.vrecv[0]
    spread("vx", 0, 1, v, xpeer)
    own_ready("o")
    weight_b("o", 0)
    own_ready("u")
    own_ready("d")
    local_wait("x", 0, r.xin)
    local_wait("iin", 0, r.ids)
    xhat0, _ = normalise(r.xin[...].astype(F32))
    v = gathered("vx", 1, v)
    spread("vy", 1, 4, v, ypeer)
    weight_c("q", 0)
    weight_c("o", 0)
    weight_b("u", 0)
    weight_b("d", 0)
    v = gathered("vy", 4, v)
    r.vec[...] = v

    def gain(l, row):
        return r.vec[4 * l + row : 4 * l + row + 1, :]

    def send_block(group, ref):
        for k in (1, 3, 2):
            push(group, k - 1, ref.at[z], ref.at[z], zpeer(k))

    def each_block(body):
        @pl.loop(0, 4)
        def _(n):
            k = jnp.where(n == 2, 3, jnp.where(n == 3, 2, n))
            body(k, (z + 4 - k) % 4)

    def flat(value):
        return value.reshape(N, value.shape[-1])

    def weight(t, l, j):
        return wref(t)[l, j // 2, :, :, :, 256 * (j % 2) : 256 * (j % 2) + 256].reshape(D, 256)

    def turn(t, l):
        for n in "CED":
            sent(n + t + str(l))

        def tile(a, b):
            return wref(t).at[l, b // 2, a, :, :, pl.ds(256 * (b % 2), 256)]

        for a in range(4):
            for b in range(a, 4):
                upper = tile(a, b)[...].reshape(256, 256)
                if a < b:
                    lower = tile(b, a)[...].reshape(256, 256)
                    tile(a, b)[...] = lower.T.reshape(4, 64, 256)
                tile(b, a)[...] = upper.T.reshape(4, 64, 256)

    def turn_qkv(l):
        for h in range(2):
            for n in range(3):
                for a in range(4):
                    w = wref("q")[l, h, a, :, :, 128 * n : 128 * n + 128].reshape(256, 128)
                    r.wqt[l, 384 * h + 128 * n : 384 * h + 128 * n + 128, 256 * a : 256 * a + 256] = w.T

    def image(axis):
        row = r.ids[...]
        place = lax.broadcasted_iota(jnp.int32, (N, 1) if axis == 0 else (1, N), axis)
        one = jnp.sum((row < 1).astype(jnp.int32), axis=1, keepdims=True)
        two = jnp.sum((row < 2).astype(jnp.int32), axis=1, keepdims=True)
        return (place >= one).astype(jnp.int32) + (place >= two).astype(jnp.int32)

    lanes = lax.broadcasted_iota(jnp.int32, (1, 128), 1)
    low_lanes = lanes < 64

    def mask_head(value, head):
        keep = low_lanes if head == 0 else jnp.logical_not(low_lanes)
        return jnp.where(keep, value, jnp.zeros_like(value))

    RS = {"m0": 0, "m1": 1, "dh21": 2, "dh11": 3, "dh20": 4, "dh10": 5}

    def rs_slot(group, k, blk, start):
        i = RS[group]
        return copy(
            group, 3 - k,
            r.stage.at[i % 2, blk], r.part.at[i, 3 - k],
            {"seq": blk},
        )

    def rs_put(group, k, blk, make):
        i = RS[group]
        for j in range(4):
            val = make(j)

            @pl.when(k == 0)
            def _():
                r.mine[:, 256 * j : 256 * j + 256] = val

            @pl.when(k > 0)
            def _():
                r.stage[i % 2, blk, :, 256 * j : 256 * j + 256] = val.astype(BF)

        @pl.when(k > 0)
        def _():
            rs_slot(group, k, blk, True).start()

    def rs_sum(group):
        i = RS[group]
        for s in range(3):
            arrived(group, s, r.part.at[i, s])
        return r.mine[...] + (
            r.part[i, 0].astype(F32) + (r.part[i, 1].astype(F32) + r.part[i, 2].astype(F32))
        )

    def rs_sent(group):
        i = RS[group]
        for k in (1, 2, 3):
            rs_slot(group, k, (z + 4 - k) % 4, False).wait_send()

    def ag_wait(group, ref, k, blk):
        @pl.when(k > 0)
        def _():
            copy(group, k - 1, ref.at[blk], ref.at[blk], sib).wait_recv()

    def attn_forward(l, xhat, gap_a, gap_b):
        r.h1[l, z] = (xhat * gain(l, 0)).astype(BF)
        send_block("h1" + str(l), r.h1.at[l])
        gap_a()
        weight_done("q", l)

        def body(k, blk):
            ag_wait("h1" + str(l), r.h1.at[l], k, blk)
            for j in range(2):
                w = wref("q")[l, j].reshape(D, 384)
                r.qkv[l, blk, :, 384 * j : 384 * j + 384] = dot(r.h1[l, blk], w).astype(BF)

        each_block(body)

        gap_b()
        same = image(0) == image(1)

        @pl.loop(0, 2)
        def _(pair):
            base = pl.multiple_of(pair * 384, 128)
            q = flat(r.qkv[l, :, :, pl.ds(base, 128)])
            kk = flat(r.qkv[l, :, :, pl.ds(pl.multiple_of(base + 128, 128), 128)])
            vv = flat(r.qkv[l, :, :, pl.ds(pl.multiple_of(base + 256, 128), 128)])
            q = q * jnp.asarray(0.125, BF)
            res = []
            for head in range(2):
                s = dot_cols(mask_head(q, head), kk)
                s = jnp.where(same, s, NEG)
                e = jnp.exp(s - jnp.max(s, axis=-1, keepdims=True))
                pb = (e * (1.0 / jnp.sum(e, axis=-1, keepdims=True))).astype(BF)
                r.prob[l, 2 * pair + head] = pb
                res.append(dot(pb, vv))
            o = jnp.where(low_lanes, res[0], res[1]).astype(BF)
            r.osend[l, :, :, pl.ds(pl.multiple_of(pair * 128, 128), 128)] = o.reshape(4, ROWS, 128)

        for k in (1, 2, 3):
            blk = (z + k) % 4
            push("o" + str(l), k - 1, r.osend.at[l, blk], r.ojoin.at[l, z], zpeer(k))
        r.ojoin[l, z] = r.osend[l, z]

    def out_proj(l, xin):
        weight_done("o", l)
        for k in (1, 2, 3):
            arrived("o" + str(l), k - 1, r.ojoin.at[l, (z + 4 - k) % 4])
        for j in range(4):
            cols = pl.ds(256 * j, 256)
            acc = None
            for b in range(4):
                w = wref("o")[l, j // 2, b, :, :, 256 * (j % 2) : 256 * (j % 2) + 256].reshape(256, 256)
                term = dot(r.ojoin[l, b], w)
                acc = term if acc is None else acc + term
            r.a[l, :, cols] = acc
        y1 = xin + gain(l, 1) * r.a[l]
        r.y1[l] = y1
        yhat, _ = normalise(y1)
        r.h2[l, z] = (yhat * gain(l, 2)).astype(BF)
        send_block("h2" + str(l), r.h2.at[l])

    def mlp_forward(l, gap_a):
        gap_a()
        weight_done("u", l)
        weight_done("d", l)

        def body(k, blk):
            ag_wait("h2" + str(l), r.h2.at[l], k, blk)
            for j in range(4):
                cols = pl.ds(256 * j, 256)
                u = dot(r.h2[l, blk], weight("u", l, j))
                g, slope = gelu_parts(u)
                r.g[l, blk, :, cols] = g.astype(BF)
                r.slope[l, blk, :, cols] = slope.astype(BF)

            def make(j):
                return dot(r.g[l, blk], weight("d", l, j))

            rs_put("m" + str(l), k, blk, make)

        each_block(body)

    def finish_layer(l):
        m = rs_sum("m" + str(l))
        r.m[l] = m
        r.zout[l] = (r.y1[l] + gain(l, 3) * m).astype(BF)

    def grad_first(t, l, left, right):
        _, h, _ = TENSORS[t]
        gs, lt = getattr(r, "gs" + t), getattr(r, "lt" + t)

        @pl.loop(0, 4)
        def _(b):
            turned = left(b).T
            lt[b, :, : turned.shape[1]] = turned
            gs[b] = dot(turned, right(half(h, 1 - c))).astype(BF).reshape(4, 64, h)

        push("ga" + t + str(l), 0, gs, getattr(r, "ra" + t).at[l], sib)

    def grad_second(t, l, right):
        _, h, xfirst = TENSORS[t]
        ra, lt = getattr(r, "ra" + t), getattr(r, "lt" + t)
        depth = ROWS if t == "o" else N
        arrived("ga" + t + str(l), 0, ra.at[l])

        @pl.loop(0, 4)
        def _(b):
            val = dot(lt[b, :, :depth], right(half(h, c))).reshape(4, 64, h)
            ra[l, b] = (val + ra[l, b].astype(F32)).astype(BF)

        for k in (1, 2, 3):
            if xfirst:
                src, dev = ra.at[l, (y + k) % 4], ypeer(k)
            else:
                src, dev = ra.at[l, :, (x + k) % 4], xpeer(k)
            push("gb" + t + str(l), k - 1, src, getattr(r, "rb" + t).at[l, k - 1], dev)

    def grad_third(t, l):
        _, h, xfirst = TENSORS[t]
        ra, rb = getattr(r, "ra" + t), getattr(r, "rb" + t)
        for k in (1, 2, 3):
            arrived("gb" + t + str(l), k - 1, rb.at[l, k - 1])

        @pl.loop(0, 4)
        def _(i):
            yy, xx = (y, i) if xfirst else (i, x)
            val = ra[l, yy, xx].astype(F32) + rb[l, 0, i].astype(F32)
            val = val + (rb[l, 1, i].astype(F32) + rb[l, 2, i].astype(F32))
            ra[l, yy, xx] = val.astype(BF)

        for k in (1, 2, 3):
            if xfirst:
                src, dev = ra.at[l, y, (x + k) % 4], xpeer(k)
            else:
                src, dev = ra.at[l, (y + k) % 4, x], ypeer(k)
            push("gc" + t + str(l), k - 1, src, getattr(r, "rc" + t).at[l, k - 1], dev)

    def grad_fourth(t, l):
        off, h, xfirst = TENSORS[t]
        ra, rc = getattr(r, "ra" + t), getattr(r, "rc" + t)
        for k in (1, 2, 3):
            arrived("gc" + t + str(l), k - 1, rc.at[l, k - 1])
        val = ra[l, y, x].astype(F32) + rc[l, 0].astype(F32)
        val = val + (rc[l, 1].astype(F32) + rc[l, 2].astype(F32))
        r.fin[l, z, :, off : off + h] = val.astype(BF)
        block = r.fin.at[l, z, :, pl.ds(off, h)]
        for k in (1, 2, 3):
            push("ge" + t + str(l), k - 1, block, block, zpeer(k))

    def grad_done(t, l):
        off, h, _ = TENSORS[t]
        for k in (1, 2, 3):
            arrived("ge" + t + str(l), k - 1, r.fin.at[l, (z + 4 - k) % 4, :, pl.ds(off, h)])

    def mlp_backward(l, dz, gap_a, gap_b):
        r.dm[l, z] = (gain(l, 3) * dz).astype(BF)
        send_block("dm" + str(l), r.dm.at[l])
        r.vgrad[4 * l + 3 : 4 * l + 4, :] = jnp.sum(dz * r.m[l], axis=0, keepdims=True)
        r.dy1[...] = dz
        gap_a()

        def body(k, blk):
            ag_wait("dm" + str(l), r.dm.at[l], k, blk)
            for b in range(4):
                cols = pl.ds(256 * b, 256)
                grad = dot(r.dm[l, blk], weight("d", l, b))
                r.du[blk, :, cols] = (grad * r.slope[l, blk, :, cols].astype(F32)).astype(BF)

            def make(b):
                return dot(r.du[blk], weight("u", l, b))

            rs_put("dh2" + str(l), k, blk, make)

        each_block(body)

        def tile(ref):
            return lambda b: flat(ref[:, :, pl.ds(pl.multiple_of(b * 256, 256), 256)])

        def cols_of(ref):
            return lambda cols: flat(ref[:, :, cols])

        g_l, h2_l, dm_l = r.g.at[l], r.h2.at[l], r.dm.at[l]
        grad_first("d", l, tile(g_l), cols_of(dm_l))
        grad_first("u", l, tile(h2_l), cols_of(r.du))
        gap_b()
        dh2 = rs_sum("dh2" + str(l))
        dn, dg2 = norm_back(dh2, r.y1[l], gain(l, 2))
        r.vgrad[4 * l + 2 : 4 * l + 3, :] = dg2
        dy1 = r.dy1[...] + dn
        r.dy1[...] = dy1
        r.da[...] = (gain(l, 1) * dy1).astype(BF)
        for b in range(4):
            r.dosend[l, b] = dot(r.da[...], weight("o", l, b)).astype(BF)
        for k in (1, 2, 3):
            push("do" + str(l), k - 1, r.dosend.at[l, (z + k) % 4], r.dojoin.at[l, z], zpeer(k))
        r.dojoin[l, z] = r.dosend[l, z]
        r.vgrad[4 * l + 1 : 4 * l + 2, :] = jnp.sum(dy1 * r.a[l], axis=0, keepdims=True)
        grad_second("d", l, cols_of(dm_l))
        grad_second("u", l, cols_of(r.du))

    def attn_backward(l, gap_a, gap_b):
        gap_a()
        for k in (1, 2, 3):
            arrived("do" + str(l), k - 1, r.dojoin.at[l, (z + 4 - k) % 4])

        @pl.loop(0, 2)
        def _(pair):
            base = pl.multiple_of(pair * 384, 128)
            c_k = pl.ds(pl.multiple_of(base + 128, 128), 128)
            c_v = pl.ds(pl.multiple_of(base + 256, 128), 128)
            q = flat(r.qkv[l, :, :, pl.ds(base, 128)]) * jnp.asarray(0.125, BF)
            kk = flat(r.qkv[l, :, :, c_k])
            vv = flat(r.qkv[l, :, :, c_v])
            do = flat(r.dojoin[l, :, :, pl.ds(pl.multiple_of(pair * 128, 128), 128)])
            dq, dk, dv = [], [], []
            for head in range(2):
                pb = r.prob[l, 2 * pair + head]
                pf = pb.astype(F32)
                dp = dot_cols(mask_head(do, head), vv)
                dv.append(dot_rows(pb, do))
                ds = (pf * (dp - jnp.sum(pf * dp, axis=-1, keepdims=True))).astype(BF)
                dq.append(dot(ds, kk))
                dk.append(dot_rows(ds, q))

            def put(cols, both, scale):
                val = jnp.where(low_lanes, both[0], both[1])
                if scale is not None:
                    val = val * scale
                r.dqkv[:, :, cols] = val.astype(BF).reshape(4, ROWS, 128)

            put(pl.ds(base, 128), dq, 0.125)
            put(c_k, dk, None)
            put(c_v, dv, None)

        def body(k, blk):
            def make(b):
                return dot(r.dqkv[blk], r.wqt[l, :, 256 * b : 256 * b + 256])

            rs_put("dh1" + str(l), k, blk, make)

        each_block(body)

        def left_q(b):
            return flat(r.h1[l, :, :, pl.ds(pl.multiple_of(b * 256, 256), 256)])

        def right_q(cols):
            return flat(r.dqkv[:, :, cols])

        def left_o(b):
            return r.ojoin[l, b]

        def right_o(cols):
            return r.da[:, cols]

        grad_first("q", l, left_q, right_q)
        grad_first("o", l, left_o, right_o)
        gap_b()
        grad_second("q", l, right_q)
        grad_second("o", l, right_o)
        dh1 = rs_sum("dh1" + str(l))
        xin = (r.xin[...] if l == 0 else r.zout[0]).astype(F32)
        dn, dg1 = norm_back(dh1, xin, gain(l, 0))
        r.vgrad[4 * l : 4 * l + 1, :] = dg1
        dx = (r.dy1[...] + dn).astype(BF)
        r.gout[l] = dx
        return dx

    def gap_f0a():
        weight_e("q", 0)
        weight_e("o", 0)
        weight_c("u", 0)
        weight_c("d", 0)
        weight_d("q", 0)

    def gap_f0b():
        weight_d("o", 0)

    attn_forward(0, xhat0, gap_f0a, gap_f0b)
    weight_b("q", 1)
    weight_b("o", 1)
    turn_qkv(0)
    weight_e("u", 0)
    weight_e("d", 0)
    out_proj(0, r.xin[...].astype(F32))

    def gap_f0c():
        weight_c("q", 1)
        weight_c("o", 1)
        turn("o", 0)
        weight_d("u", 0)
        weight_d("d", 0)
        weight_b("u", 1)
        weight_b("d", 1)

    mlp_forward(0, gap_f0c)
    weight_e("q", 1)
    weight_e("o", 1)
    weight_c("u", 1)
    weight_c("d", 1)
    turn("u", 0)
    weight_d("q", 1)
    weight_d("o", 1)
    turn("d", 0)
    finish_layer(0)
    xhat1, _ = normalise(r.zout[0].astype(F32))

    def gap_f1b():
        weight_e("u", 1)
        weight_e("d", 1)

    attn_forward(1, xhat1, lambda: None, gap_f1b)
    turn_qkv(1)
    out_proj(1, r.zout[0].astype(F32))

    def gap_f1c():
        turn("o", 1)
        weight_d("u", 1)
        weight_d("d", 1)

    mlp_forward(1, gap_f1c)
    turn("u", 1)
    turn("d", 1)
    finish_layer(1)
    push("zo", 0, r.zout.at[1 - c], lo_ref.at[c], sib)
    local_start("out", 0, r.zout.at[c], lo_ref.at[c])

    rs_sent("m0")
    local_wait("dz", 0, r.dzin)
    mlp_backward(1, r.dzin[...].astype(F32), lambda: None, lambda: None)
    rs_sent("m1")

    def nothing():
        pass

    attn_backward(1, nothing, nothing)
    for t in "qoud":
        sent("ga" + t + "1")
    rs_sent("dh21")

    def gap_b0a():
        grad_third("d", 1)
        grad_third("u", 1)

    def gap_b0b():
        grad_third("q", 1)
        grad_third("o", 1)

    mlp_backward(0, r.gout[1].astype(F32), gap_b0a, gap_b0b)
    rs_sent("dh11")

    def gap_b0c():
        grad_fourth("d", 1)
        grad_fourth("u", 1)

    def gap_b0d():
        grad_fourth("q", 1)
        grad_fourth("o", 1)
        grad_third("d", 0)
        grad_third("u", 0)

    attn_backward(0, gap_b0c, gap_b0d)

    push("go", 0, r.gout.at[1 - c], gi_ref.at[c], sib)
    local_start("out", 1, r.gout.at[c], gi_ref.at[c])
    gv = r.vgrad[...]
    r.vsend[2] = gv
    push("ga", 0, r.vsend.at[2], r.vrecv.at[7], sib)
    grad_fourth("d", 0)
    grad_fourth("u", 0)
    arrived("ga", 0, r.vrecv.at[7])
    gv = gv + r.vrecv[7]
    spread("gx", 3, 8, gv, xpeer)
    grad_third("q", 0)
    grad_third("o", 0)
    gv = gathered("gx", 8, gv)
    spread("gy", 4, 11, gv, ypeer)
    grad_fourth("q", 0)
    grad_fourth("o", 0)
    gv = gathered("gy", 11, gv)
    spread("gz", 5, 14, gv, zpeer)
    for l in (1, 0):
        for t in "duqo":
            grad_done(t, l)
    push("fo", 0, r.fin.at[1 - c], fother_ref, sib)
    local_start("out", 2, r.fin.at[c], fin_ref)
    r.vgrad[...] = gathered("gz", 14, gv)
    local_start("out2", 0, r.vgrad, gv_ref)
    arrived("zo", 0, lo_ref.at[1 - c])
    arrived("go", 0, gi_ref.at[1 - c])
    arrived("fo", 0, fother_ref)
    local_wait("out", 0, lo_ref.at[c])
    local_wait("out", 1, gi_ref.at[c])
    local_wait("out", 2, fin_ref)
    local_wait("out2", 0, gv_ref)
    rs_sent("dh20")
    rs_sent("dh10")
    for group in {k[0]: None for k in list(pending)}:
        sent(group)


def assemble(fin_in, fother_in, lo, gi, gv_in, lo_ref, gi_ref, gq_ref, go_ref, gu_ref, gd_ref, gv_ref, fin, fother, gv, sem):
    c = lax.axis_index("section")
    p = lax.axis_index("shard")
    pairs = [(fin_in, fin), (fother_in, fother), (gv_in, gv)]
    pairs += [(lo.at[m], lo_ref.at[0, m, 0]) for m in range(2)]
    pairs += [(gi.at[m], gi_ref.at[0, m, 0]) for m in range(2)]
    moves = [pltpu.make_async_copy(a, b, sem.at[n]) for n, (a, b) in enumerate(pairs)]
    for move in moves:
        move.start()
    moves[2].wait()
    both = gv[:, pl.ds(pl.multiple_of((p // 2) * 128, 128), 128)]
    both = jnp.where(c == 0, both[:4], both[4:])
    gv_ref[0] = jnp.where(p % 2 == 0, both[:, :64], both[:, 64:])
    for n, ref, which in ((0, fin, c), (1, fother, 1 - c)):
        moves[n].wait()
        wide = pl.ds(pl.multiple_of(which * 512, 512), 512)
        for zz in range(4):
            for t in range(3):
                col = pl.multiple_of(t * 1024 + zz * 256 + which * 128, 128)
                gq_ref[0, :, pl.ds(col, 128)] = ref[zz, :, t * 128 : t * 128 + 128].astype(F32)
            gd_ref[0, 64 * zz : 64 * zz + 64, wide] = ref[zz, :, 1408:1920].astype(F32)
        total = ref[0, :, 384:896].astype(F32)
        for zz in range(1, 4):
            total = total + ref[zz, :, 384:896].astype(F32)
        go_ref[0, :, wide] = total
        ups = [ref[zz, :, 896:1408].astype(F32) for zz in range(4)]
        for n in range(8):
            row = jnp.concatenate([u[:, 64 * n : 64 * n + 64] for u in ups], axis=1)
            gu_ref[0, :, pl.ds(pl.multiple_of((which * 8 + n) * 256, 256), 256)] = row
    for move in moves[3:]:
        move.wait()


def local(acts_in, cotangent, qkv_weight, out_weight, up_weight, down_weight, vectors, image_ids):
    vmem = pl.BlockSpec(memory_space=pltpu.VMEM)
    hbm = pl.BlockSpec(memory_space=pl.ANY)
    out = pl.pallas_call(
        kernel,
        out_shape=(
            jax.ShapeDtypeStruct((4, 64, HALF), BF),
            jax.ShapeDtypeStruct((4, 64, HALF), BF),
            jax.ShapeDtypeStruct((2, ROWS, D), BF),
            jax.ShapeDtypeStruct((2, ROWS, D), BF),
            jax.ShapeDtypeStruct((8, D), F32),
        ),
        in_specs=[hbm] * 8,
        out_specs=(hbm,) * 5,
        scratch_shapes=[pltpu.VMEM(s, t) for s, t in SCRATCH.values()]
        + [pltpu.SemaphoreType.DMA((len(GROUP), 3)), pltpu.SemaphoreType.DMA((len(GROUP), 3))],
        compiler_params=pltpu.CompilerParams(
            collective_id=0, has_side_effects=True, vmem_limit_bytes=64 * 1024 * 1024 - 65536
        ),
    )(acts_in, cotangent, qkv_weight, out_weight, up_weight, down_weight, vectors, image_ids)
    return pl.pallas_call(
        assemble,
        out_shape=(
            jax.ShapeDtypeStruct((1, 2, 1, ROWS, D), BF),
            jax.ShapeDtypeStruct((1, 2, 1, ROWS, D), BF),
            jax.ShapeDtypeStruct((1, 64, 3072), F32),
            jax.ShapeDtypeStruct((1, 64, D), F32),
            jax.ShapeDtypeStruct((1, 64, 4096), F32),
            jax.ShapeDtypeStruct((1, 256, D), F32),
            jax.ShapeDtypeStruct((1, 4, 64), F32),
        ),
        in_specs=[hbm] * 5,
        out_specs=(vmem,) * 7,
        scratch_shapes=[
            pltpu.VMEM((4, 64, HALF), BF),
            pltpu.VMEM((4, 64, HALF), BF),
            pltpu.VMEM((8, D), F32),
            pltpu.SemaphoreType.DMA((7,)),
        ],
        compiler_params=pltpu.CompilerParams(vmem_limit_bytes=64 * 1024 * 1024 - 65536),
    )(*out)


def solution(mesh):
    placed = (
        P(None, "shard", "seq", None),
        P(None, "shard", "seq", None),
        P("section", "shard", None),
        P("section", "shard", None),
        P("section", "shard", None),
        P("section", "shard", None),
        P("section", None, "shard"),
        P(None, "shard", None),
    )
    return jax.shard_map(
        local,
        mesh=mesh,
        in_specs=placed,
        out_specs=(
            P("section", None, "shard", "seq", None),
            P("section", None, "shard", "seq", None),
            P("section", "shard", None),
            P("section", "shard", None),
            P("section", "shard", None),
            P("section", "shard", None),
            P("section", None, "shard"),
        ),
        check_vma=False,
    )
```

```python
import jax
import jax.numpy as jnp
from jax import lax
from jax.experimental import pallas as pl
from jax.experimental.pallas import tpu as pltpu
from jax.sharding import PartitionSpec as P

EPS = 1e-06
NEG = -1e30
BF = jnp.bfloat16
F32 = jnp.float32
MESH = pl.DeviceIdType.MESH
D = 1024
ROWS = 72
N = 4 * ROWS
TENSORS = {"q": (0, 384, True), "o": (384, 512, False), "u": (896, 512, True), "d": (1408, 512, False)}
HALF = 1920


def dot(a, b):
    return lax.dot_general(a, b, (((1,), (0,)), ((), ())), preferred_element_type=F32)


def dot_rows(a, b):
    return lax.dot_general(a, b, (((0,), (0,)), ((), ())), preferred_element_type=F32)


def dot_cols(a, b):
    return lax.dot_general(a, b, (((1,), (1,)), ((), ())), preferred_element_type=F32)


def normalise(values):
    centre = values - jnp.mean(values, axis=-1, keepdims=True)
    scale = lax.rsqrt(jnp.mean(centre * centre, axis=-1, keepdims=True) + EPS)
    return centre * scale, scale


def norm_back(grad, values, gain):
    xhat, scale = normalise(values)
    f = grad * gain
    dv = scale * (
        f
        - jnp.mean(f, axis=-1, keepdims=True)
        - xhat * jnp.mean(f * xhat, axis=-1, keepdims=True)
    )
    return dv, jnp.sum(grad * xhat, axis=0, keepdims=True)


def gelu_parts(u):
    cdf = 0.5 * (1.0 + lax.erf(u * 0.7071067811865476))
    slope = cdf + u * jnp.exp(-0.5 * u * u) * 0.3989422804014327
    return u * cdf, slope


SCRATCH = dict(
    vectors=((1, 4, 64), BF),
    ids=((1, N), jnp.int32),
    ustage=((16, 64, 128), BF),
    usend=((64, 512), BF),
    xall=((4, ROWS, D), BF),
    dzin=((ROWS, D), BF),
    vsend=((7, 8, D), F32),
    vrecv=((17, 8, D), F32),
    vec=((8, D), F32),
    vgrad=((8, D), F32),
    h1=((2, 4, ROWS, D), BF),
    qkv=((2, 4, ROWS, 768), BF),
    prob=((2, 4, N, N), BF),
    wqt=((2, 768, D), BF),
    osend=((2, 4, ROWS, 256), BF),
    ojoin=((2, 4, ROWS, 256), BF),
    a=((2, ROWS, D), F32),
    y1=((2, ROWS, D), F32),
    h2=((2, 4, ROWS, D), BF),
    slope=((2, 4, ROWS, D), BF),
    g=((2, 4, ROWS, D), BF),
    stage=((2, 4, ROWS, D), BF),
    part=((6, 3, ROWS, D), BF),
    m=((2, ROWS, D), F32),
    dm=((2, 4, ROWS, D), BF),
    du=((4, ROWS, D), BF),
    dy1=((ROWS, D), F32),
    da=((ROWS, D), BF),
    dosend=((2, 4, ROWS, 256), BF),
    dojoin=((2, 4, ROWS, 256), BF),
    dqkv=((4, ROWS, 768), BF),
    zout=((2, ROWS, D), BF),
    gout=((2, ROWS, D), BF),
    fin=((2, 4, 64, HALF), BF),
)
for _t, (_, _h, _x) in TENSORS.items():
    SCRATCH["own" + _t] = ((2, 64, _h), BF)
    SCRATCH["w" + _t] = ((2, 2, 4, 4, 64, _h), BF)
    SCRATCH["lt" + _t] = ((4, 256, 4 * ROWS), BF)
    SCRATCH["gs" + _t] = ((4, 4, 64, _h), BF)
    SCRATCH["ra" + _t] = ((2, 4, 4, 64, _h), BF)
    SCRATCH["rb" + _t] = ((2, 3, 4, 64, _h), BF)
    SCRATCH["rc" + _t] = ((2, 3, 64, _h), BF)

GROUPS = (
    ["x", "dz", "us", "vin", "iin", "out", "out2", "out3", "va", "vx", "vy", "ga", "gx", "gy", "gz", "zo", "go", "fo"]
    + [n + t + str(l) for n in ("A", "L", "B", "Bl", "C", "E", "D", "ga", "gb", "gc", "ge") for t in "qoud" for l in (0, 1)]
    + [n + str(l) for n in ("h1", "h2", "o", "m", "dm", "dh2", "do", "dh1") for l in (0, 1)]
)
GROUP = {n: i for i, n in enumerate(dict.fromkeys(GROUPS))}


class Refs:
    pass


def kernel(acts, cot, wq, wo, wu, wd, vectors_in, ids_in, fin_ref, fother_ref, lo_ref, gi_ref, gv_ref, *scratch):
    r = Refs()
    for name, ref in zip(SCRATCH, scratch):
        setattr(r, name, ref)
    ssem, rsem = scratch[len(SCRATCH) :]
    c = lax.axis_index("section")
    z = lax.axis_index("seq")
    p = lax.axis_index("shard")
    y, x = p // 4, p % 4
    sib = {"section": 1 - c}

    def zpeer(k):
        return {"seq": (z + k) % 4}

    def xpeer(k):
        return {"shard": y * 4 + (x + k) % 4}

    def ypeer(k):
        return {"shard": ((y + k) % 4) * 4 + x}

    pending = {}

    def copy(group, slot, src, dst, dev):
        return pltpu.make_async_remote_copy(
            src_ref=src,
            dst_ref=dst,
            send_sem=ssem.at[GROUP[group], slot],
            recv_sem=rsem.at[GROUP[group], slot],
            device_id=dev,
            device_id_type=MESH,
        )

    def push(group, slot, src, dst, dev):
        copy(group, slot, src, dst, dev).start()
        pending[(group, slot)] = (src, dev)

    def sent(group):
        for key in [k for k in pending if k[0] == group]:
            src, dev = pending.pop(key)
            copy(group, key[1], src, src, dev).wait_send()

    def arrived(group, slot, dst):
        copy(group, slot, dst, dst, sib).wait_recv()

    def local_start(group, slot, src, dst):
        pltpu.make_async_copy(src, dst, ssem.at[GROUP[group], slot]).start()

    def local_wait(group, slot, dst):
        pltpu.make_async_copy(dst, dst, ssem.at[GROUP[group], slot]).wait()

    def piece(t, which):
        if t == "q":
            return [
                (wq.at[0, :, pl.ds(pl.multiple_of(n * 1024 + z * 256 + which * 128, 128), 128)], n * 128, 128)
                for n in range(3)
            ]
        cols = pl.ds(pl.multiple_of(which * 512, 512), 512)
        if t == "o":
            return [(wo.at[0, :, cols], 0, 512)]
        return [(wd.at[0, pl.ds(pl.multiple_of(z * 64, 64), 64), cols], 0, 512)]

    def own(t):
        return getattr(r, "own" + t)

    local_start("vin", 0, vectors_in, r.vectors)
    local_start("iin", 0, ids_in.at[c], r.ids)
    local_start("x", 0, acts.at[c, 0], r.xall.at[z])

    @pl.loop(0, 16)
    def _(n):
        col = pl.multiple_of(n * 256 + (z // 2) * 128, 128)
        local_start("us", 0, wu.at[0, :, pl.ds(col, 128)], r.ustage.at[n])

    for t in "qod":
        for n, (src, at, width) in enumerate(piece(t, c)):
            local_start("L" + t + "0", n, src, own(t).at[c, :, pl.ds(at, width)])
    local_start("dz", 0, cot.at[c, 0], r.dzin)

    barrier = pltpu.get_barrier_semaphore()
    for dev in [sib] + [f(k) for f in (xpeer, ypeer, zpeer) for k in (1, 2, 3)]:
        pl.semaphore_signal(barrier, inc=1, device_id=dev, device_id_type=MESH)
    rows8 = lax.broadcasted_iota(jnp.int32, (8, 128), 0)
    lanes8 = lax.broadcasted_iota(jnp.int32, (8, 128), 1)
    local_wait("vin", 0, r.vectors)
    vown = r.vectors[0].astype(F32)
    vown = jnp.concatenate([vown, vown], axis=0)
    vown = jnp.concatenate([vown, vown], axis=1)
    keep = jnp.logical_and(rows8 // 4 == c, lanes8 // 64 == p % 2)
    r.vsend[6] = jnp.zeros((8, D), F32)
    r.vsend[6, :, pl.ds(pl.multiple_of((p // 2) * 128, 128), 128)] = jnp.where(keep, vown, 0.0)
    pl.semaphore_wait(barrier, 10)

    def half(h, which):
        return pl.ds(pl.multiple_of(which * h, 128), h)

    push("va", 0, r.vsend.at[6], r.vrecv.at[0], sib)
    for t in "qod":
        for n, (src, at, width) in enumerate(piece(t, 1 - c)):
            push("A" + t + "0", n, src, own(t).at[c, :, pl.ds(at, width)], sib)
    local_wait("x", 0, r.xall.at[z])
    for k in (1, 3, 2):
        push("h10", k - 1, r.xall.at[z], r.xall.at[z], zpeer(k))
    local_wait("us", 0, r.ustage)

    def up_half(which):
        lower = lax.broadcasted_iota(jnp.int32, (64, 128), 1) < 64
        tiles = []
        for n in range(4):
            first = r.ustage[8 * which + 2 * n].astype(F32)
            second = r.ustage[8 * which + 2 * n + 1].astype(F32)
            even = jnp.where(lower, first, pltpu.roll(second, 64, 1))
            odd = jnp.where(lower, pltpu.roll(first, 64, 1), second)
            tiles.append(jnp.where(z % 2 == 0, even, odd).astype(BF))
        return jnp.concatenate(tiles, axis=1)

    r.usend[...] = up_half(1 - c)
    push("Au0", 0, r.usend, own("u").at[c], sib)
    r.ownu[c] = up_half(c)

    def own_ready(t):
        for n, (_, at, width) in enumerate(piece(t, c) if t != "u" else [(None, 0, 512)]):
            if t != "u":
                local_wait("L" + t + "0", n, own(t).at[c, :, pl.ds(at, width)])
            arrived("A" + t + "0", n, own(t).at[1 - c, :, pl.ds(at, width)])

    def wref(t):
        return getattr(r, "w" + t)

    def local_copy(t, l):
        return pltpu.make_async_copy(
            own(t).at[l], wref(t).at[l, c, y, x], ssem.at[GROUP["Bl" + t + str(l)], 0]
        )

    def weight_b(t, l):
        _, h, xfirst = TENSORS[t]
        peer = xpeer if xfirst else ypeer
        for k in (1, 3, 2):
            push("B" + t + str(l), k - 1, own(t).at[l], wref(t).at[l, c, y, x], peer(k))
        local_copy(t, l).start()

    def weight_c(t, l):
        _, h, xfirst = TENSORS[t]
        local_copy(t, l).wait()
        for k in (1, 2, 3):
            if xfirst:
                arrived("B" + t + str(l), k - 1, wref(t).at[l, c, y, (x + 4 - k) % 4])
            else:
                arrived("B" + t + str(l), k - 1, wref(t).at[l, c, (y + 4 - k) % 4, x])
        line = wref(t).at[l, c, y] if xfirst else wref(t).at[l, c, :, x]
        peer = ypeer if xfirst else xpeer
        for k in (1, 3):
            push("C" + t + str(l), k - 1, line, line, peer(k))

    def line_of(t, l, back, part=None):
        if TENSORS[t][2]:
            ref = wref(t).at[l, c, (y + 4 - back) % 4]
            return ref if part is None else ref.at[pl.ds(2 * part, 2)]
        if part is None:
            return wref(t).at[l, c, :, (x + 4 - back) % 4]
        return wref(t).at[l, c, pl.ds(2 * part, 2), (x + 4 - back) % 4]

    def weight_e(t, l):
        peer = ypeer if TENSORS[t][2] else xpeer
        for k, part in ((1, 0), (3, 1)):
            arrived("C" + t + str(l), k - 1, line_of(t, l, k))
            push("E" + t + str(l), k - 1, line_of(t, l, k, part), line_of(t, l, k, part), peer(k))

    def weight_d(t, l):
        for k, part in ((1, 0), (3, 1)):
            arrived("E" + t + str(l), k - 1, line_of(t, l, 2, part))
        mine = wref(t).at[l, c]
        push("D" + t + str(l), 0, mine, mine, sib)

    def weight_done(t, l):
        arrived("D" + t + str(l), 0, wref(t).at[l, 1 - c])

    def spread(group, at, slots, value, peer):
        r.vsend[at] = value
        for k in (1, 2, 3):
            push(group, k - 1, r.vsend.at[at], r.vrecv.at[slots + k - 1], peer(k))

    def gathered(group, slots, value):
        for k in (1, 2, 3):
            arrived(group, k - 1, r.vrecv.at[slots + k - 1])
        return value + (r.vrecv[slots] + (r.vrecv[slots + 1] + r.vrecv[slots + 2]))

    arrived("va", 0, r.vrecv.at[0])
    v = r.vsend[6] + r.vrecv[0]
    spread("vx", 0, 1, v, xpeer)
    own_ready("q")
    weight_b("q", 0)
    own_ready("o")
    weight_b("o", 0)
    v = gathered("vx", 1, v)
    spread("vy", 1, 4, v, ypeer)
    weight_c("q", 0)
    weight_c("o", 0)
    own_ready("u")
    own_ready("d")
    weight_b("u", 0)
    weight_b("d", 0)
    local_wait("iin", 0, r.ids)
    v = gathered("vy", 4, v)
    r.vec[...] = v

    def gain(l, row):
        return r.vec[4 * l + row : 4 * l + row + 1, :]

    def send_block(group, ref):
        for k in (1, 3, 2):
            push(group, k - 1, ref.at[z], ref.at[z], zpeer(k))

    def each_block(body, first=0, last=4):
        @pl.loop(first, last)
        def _(n):
            k = jnp.where(n == 2, 3, jnp.where(n == 3, 2, n))
            body(k, (z + 4 - k) % 4)

    def flat(value):
        return value.reshape(N, value.shape[-1])

    def weight(t, l, j):
        return wref(t)[l, j // 2, :, :, :, 256 * (j % 2) : 256 * (j % 2) + 256].reshape(D, 256)

    def turn(t, l):
        for n in "CED":
            sent(n + t + str(l))

        def tile(a, b):
            return wref(t).at[l, b // 2, a, :, :, pl.ds(256 * (b % 2), 256)]

        for a in range(4):
            for b in range(a, 4):
                upper = tile(a, b)[...].reshape(256, 256)
                if a < b:
                    lower = tile(b, a)[...].reshape(256, 256)
                    tile(a, b)[...] = lower.T.reshape(4, 64, 256)
                tile(b, a)[...] = upper.T.reshape(4, 64, 256)

    def turn_qkv(l):
        for h in range(2):
            for n in range(3):
                for a in range(4):
                    w = wref("q")[l, h, a, :, :, 128 * n : 128 * n + 128].reshape(256, 128)
                    r.wqt[l, 384 * h + 128 * n : 384 * h + 128 * n + 128, 256 * a : 256 * a + 256] = w.T

    def image(axis):
        row = r.ids[...]
        place = lax.broadcasted_iota(jnp.int32, (N, 1) if axis == 0 else (1, N), axis)
        one = jnp.sum((row < 1).astype(jnp.int32), axis=1, keepdims=True)
        two = jnp.sum((row < 2).astype(jnp.int32), axis=1, keepdims=True)
        return (place >= one).astype(jnp.int32) + (place >= two).astype(jnp.int32)

    lanes = lax.broadcasted_iota(jnp.int32, (1, 128), 1)
    low_lanes = lanes < 64

    def mask_head(value, head):
        keep = low_lanes if head == 0 else jnp.logical_not(low_lanes)
        return jnp.where(keep, value, jnp.zeros_like(value))

    RS = {"m0": 0, "m1": 1, "dh21": 2, "dh11": 3, "dh20": 4, "dh10": 5}

    def rs_slot(group, k, blk, start):
        i = RS[group]
        return copy(
            group, 3 - k,
            r.stage.at[i % 2, blk], r.part.at[i, 3 - k],
            {"seq": blk},
        )

    def rs_put(group, k, blk, make):
        i = RS[group]
        for j in range(4):
            r.stage[i % 2, blk, :, 256 * j : 256 * j + 256] = make(j).astype(BF)

        @pl.when(k > 0)
        def _():
            rs_slot(group, k, blk, True).start()

    def rs_sum(group):
        i = RS[group]
        for s in range(3):
            arrived(group, s, r.part.at[i, s])
        return r.stage[i % 2, z].astype(F32) + (
            r.part[i, 0].astype(F32) + (r.part[i, 1].astype(F32) + r.part[i, 2].astype(F32))
        )

    def rs_sent(group):
        i = RS[group]
        for k in (1, 2, 3):
            rs_slot(group, k, (z + 4 - k) % 4, False).wait_send()

    def ag_wait(group, ref, k, blk):
        @pl.when(k > 0)
        def _():
            copy(group, k - 1, ref.at[blk], ref.at[blk], sib).wait_recv()

    def attn_forward(l, xhat, gap_a, gap_b):
        if l > 0:
            r.h1[l, z] = (xhat * gain(l, 0)).astype(BF)
            send_block("h1" + str(l), r.h1.at[l])
        gap_a()
        weight_done("q", l)

        def body(k, blk):
            if l > 0:
                ag_wait("h1" + str(l), r.h1.at[l], k, blk)
            else:
                ag_wait("h10", r.xall, k, blk)
                hat, _ = normalise(r.xall[blk].astype(F32))
                r.h1[0, blk] = (hat * gain(0, 0)).astype(BF)
            for j in range(2):
                w = wref("q")[l, j].reshape(D, 384)
                r.qkv[l, blk, :, 384 * j : 384 * j + 384] = dot(r.h1[l, blk], w).astype(BF)

        each_block(body)

        gap_b()
        same = image(0) == image(1)

        @pl.loop(0, 2)
        def _(pair):
            base = pl.multiple_of(pair * 384, 128)
            q = flat(r.qkv[l, :, :, pl.ds(base, 128)])
            kk = flat(r.qkv[l, :, :, pl.ds(pl.multiple_of(base + 128, 128), 128)])
            vv = flat(r.qkv[l, :, :, pl.ds(pl.multiple_of(base + 256, 128), 128)])
            q = q * jnp.asarray(0.125, BF)
            res = []
            for head in range(2):
                s = dot_cols(mask_head(q, head), kk)
                s = jnp.where(same, s, NEG)
                e = jnp.exp(s - jnp.max(s, axis=-1, keepdims=True))
                pb = (e * (1.0 / jnp.sum(e, axis=-1, keepdims=True))).astype(BF)
                r.prob[l, 2 * pair + head] = pb
                res.append(dot(pb, vv))
            o = jnp.where(low_lanes, res[0], res[1]).astype(BF)
            r.osend[l, :, :, pl.ds(pl.multiple_of(pair * 128, 128), 128)] = o.reshape(4, ROWS, 128)

        for k in (1, 2, 3):
            blk = (z + k) % 4
            push("o" + str(l), k - 1, r.osend.at[l, blk], r.ojoin.at[l, z], zpeer(k))
        r.ojoin[l, z] = r.osend[l, z]

    def out_proj(l, xin):
        weight_done("o", l)
        for k in (1, 2, 3):
            arrived("o" + str(l), k - 1, r.ojoin.at[l, (z + 4 - k) % 4])
        for j in range(4):
            cols = pl.ds(256 * j, 256)
            acc = None
            for b in range(4):
                w = wref("o")[l, j // 2, b, :, :, 256 * (j % 2) : 256 * (j % 2) + 256].reshape(256, 256)
                term = dot(r.ojoin[l, b], w)
                acc = term if acc is None else acc + term
            r.a[l, :, cols] = acc
        y1 = xin + gain(l, 1) * r.a[l]
        r.y1[l] = y1
        yhat, _ = normalise(y1)
        r.h2[l, z] = (yhat * gain(l, 2)).astype(BF)
        send_block("h2" + str(l), r.h2.at[l])

    def mlp_forward(l, gap_a, gap_b):
        gap_a()
        weight_done("u", l)
        weight_done("d", l)

        def body(k, blk):
            ag_wait("h2" + str(l), r.h2.at[l], k, blk)
            for j in range(4):
                cols = pl.ds(256 * j, 256)
                u = dot(r.h2[l, blk], weight("u", l, j))
                g, slope = gelu_parts(u)
                r.g[l, blk, :, cols] = g.astype(BF)
                r.slope[l, blk, :, cols] = slope.astype(BF)

            def make(j):
                return dot(r.g[l, blk], weight("d", l, j))

            rs_put("m" + str(l), k, blk, make)

        if gap_b is None:
            each_block(body)
        else:
            each_block(body, 0, 2)
            gap_b()
            each_block(body, 2, 4)

    def finish_layer(l):
        m = rs_sum("m" + str(l))
        r.m[l] = m
        r.zout[l] = (r.y1[l] + gain(l, 3) * m).astype(BF)

    def grad_first(t, l, left, right):
        _, h, _ = TENSORS[t]
        gs, lt = getattr(r, "gs" + t), getattr(r, "lt" + t)

        @pl.loop(0, 4)
        def _(b):
            turned = left(b).T
            lt[b, :, : turned.shape[1]] = turned
            gs[b] = dot(turned, right(half(h, 1 - c))).astype(BF).reshape(4, 64, h)

        push("ga" + t + str(l), 0, gs, getattr(r, "ra" + t).at[l], sib)

    def grad_second(t, l, right):
        _, h, xfirst = TENSORS[t]
        ra, lt = getattr(r, "ra" + t), getattr(r, "lt" + t)
        depth = ROWS if t == "o" else N
        arrived("ga" + t + str(l), 0, ra.at[l])

        @pl.loop(0, 4)
        def _(b):
            val = dot(lt[b, :, :depth], right(half(h, c))).reshape(4, 64, h)
            ra[l, b] = (val + ra[l, b].astype(F32)).astype(BF)

        for k in (1, 2, 3):
            if xfirst:
                src, dev = ra.at[l, (y + k) % 4], ypeer(k)
            else:
                src, dev = ra.at[l, :, (x + k) % 4], xpeer(k)
            push("gb" + t + str(l), k - 1, src, getattr(r, "rb" + t).at[l, k - 1], dev)

    def grad_third(t, l):
        _, h, xfirst = TENSORS[t]
        ra, rb = getattr(r, "ra" + t), getattr(r, "rb" + t)
        for k in (1, 2, 3):
            arrived("gb" + t + str(l), k - 1, rb.at[l, k - 1])

        @pl.loop(0, 4)
        def _(i):
            yy, xx = (y, i) if xfirst else (i, x)
            val = ra[l, yy, xx].astype(F32) + rb[l, 0, i].astype(F32)
            val = val + (rb[l, 1, i].astype(F32) + rb[l, 2, i].astype(F32))
            ra[l, yy, xx] = val.astype(BF)

        for k in (1, 2, 3):
            if xfirst:
                src, dev = ra.at[l, y, (x + k) % 4], xpeer(k)
            else:
                src, dev = ra.at[l, (y + k) % 4, x], ypeer(k)
            push("gc" + t + str(l), k - 1, src, getattr(r, "rc" + t).at[l, k - 1], dev)

    def grad_fourth(t, l):
        off, h, xfirst = TENSORS[t]
        ra, rc = getattr(r, "ra" + t), getattr(r, "rc" + t)
        for k in (1, 2, 3):
            arrived("gc" + t + str(l), k - 1, rc.at[l, k - 1])
        val = ra[l, y, x].astype(F32) + rc[l, 0].astype(F32)
        val = val + (rc[l, 1].astype(F32) + rc[l, 2].astype(F32))
        r.fin[l, z, :, off : off + h] = val.astype(BF)
        block = r.fin.at[l, z, :, pl.ds(off, h)]
        for k in (1, 2, 3):
            push("ge" + t + str(l), k - 1, block, block, zpeer(k))

    def grad_done(t, l):
        off, h, _ = TENSORS[t]
        for k in (1, 2, 3):
            arrived("ge" + t + str(l), k - 1, r.fin.at[l, (z + 4 - k) % 4, :, pl.ds(off, h)])

    def mlp_backward(l, dz, gap_a, gap_b):
        r.dm[l, z] = (gain(l, 3) * dz).astype(BF)
        send_block("dm" + str(l), r.dm.at[l])
        r.vgrad[4 * l + 3 : 4 * l + 4, :] = jnp.sum(dz * r.m[l], axis=0, keepdims=True)
        r.dy1[...] = dz
        gap_a()

        def body(k, blk):
            ag_wait("dm" + str(l), r.dm.at[l], k, blk)
            for b in range(4):
                cols = pl.ds(256 * b, 256)
                grad = dot(r.dm[l, blk], weight("d", l, b))
                r.du[blk, :, cols] = (grad * r.slope[l, blk, :, cols].astype(F32)).astype(BF)

            def make(b):
                return dot(r.du[blk], weight("u", l, b))

            rs_put("dh2" + str(l), k, blk, make)

        each_block(body)

        def tile(ref):
            return lambda b: flat(ref[:, :, pl.ds(pl.multiple_of(b * 256, 256), 256)])

        def cols_of(ref):
            return lambda cols: flat(ref[:, :, cols])

        g_l, h2_l, dm_l = r.g.at[l], r.h2.at[l], r.dm.at[l]
        grad_first("d", l, tile(g_l), cols_of(dm_l))
        grad_first("u", l, tile(h2_l), cols_of(r.du))
        gap_b()
        dh2 = rs_sum("dh2" + str(l))
        dn, dg2 = norm_back(dh2, r.y1[l], gain(l, 2))
        r.vgrad[4 * l + 2 : 4 * l + 3, :] = dg2
        dy1 = r.dy1[...] + dn
        r.dy1[...] = dy1
        r.da[...] = (gain(l, 1) * dy1).astype(BF)
        for b in range(4):
            r.dosend[l, b] = dot(r.da[...], weight("o", l, b)).astype(BF)
        for k in (1, 2, 3):
            push("do" + str(l), k - 1, r.dosend.at[l, (z + k) % 4], r.dojoin.at[l, z], zpeer(k))
        r.dojoin[l, z] = r.dosend[l, z]
        r.vgrad[4 * l + 1 : 4 * l + 2, :] = jnp.sum(dy1 * r.a[l], axis=0, keepdims=True)
        grad_second("d", l, cols_of(dm_l))
        grad_second("u", l, cols_of(r.du))

    def attn_backward(l, gap_a, gap_b):
        gap_a()
        for k in (1, 2, 3):
            arrived("do" + str(l), k - 1, r.dojoin.at[l, (z + 4 - k) % 4])

        @pl.loop(0, 2)
        def _(pair):
            base = pl.multiple_of(pair * 384, 128)
            c_k = pl.ds(pl.multiple_of(base + 128, 128), 128)
            c_v = pl.ds(pl.multiple_of(base + 256, 128), 128)
            q = flat(r.qkv[l, :, :, pl.ds(base, 128)]) * jnp.asarray(0.125, BF)
            kk = flat(r.qkv[l, :, :, c_k])
            vv = flat(r.qkv[l, :, :, c_v])
            do = flat(r.dojoin[l, :, :, pl.ds(pl.multiple_of(pair * 128, 128), 128)])
            dq, dk, dv = [], [], []
            for head in range(2):
                pb = r.prob[l, 2 * pair + head]
                pf = pb.astype(F32)
                dp = dot_cols(mask_head(do, head), vv)
                dv.append(dot_rows(pb, do))
                ds = (pf * (dp - jnp.sum(pf * dp, axis=-1, keepdims=True))).astype(BF)
                dq.append(dot(ds, kk))
                dk.append(dot_rows(ds, q))

            def put(cols, both, scale):
                val = jnp.where(low_lanes, both[0], both[1])
                if scale is not None:
                    val = val * scale
                r.dqkv[:, :, cols] = val.astype(BF).reshape(4, ROWS, 128)

            put(pl.ds(base, 128), dq, 0.125)
            put(c_k, dk, None)
            put(c_v, dv, None)

        def body(k, blk):
            def make(b):
                return dot(r.dqkv[blk], r.wqt[l, :, 256 * b : 256 * b + 256])

            rs_put("dh1" + str(l), k, blk, make)

        each_block(body)

        def left_q(b):
            return flat(r.h1[l, :, :, pl.ds(pl.multiple_of(b * 256, 256), 256)])

        def right_q(cols):
            return flat(r.dqkv[:, :, cols])

        def left_o(b):
            return r.ojoin[l, b]

        def right_o(cols):
            return r.da[:, cols]

        grad_first("q", l, left_q, right_q)
        grad_first("o", l, left_o, right_o)
        gap_b()
        grad_second("q", l, right_q)
        grad_second("o", l, right_o)
        dh1 = rs_sum("dh1" + str(l))
        xin = (r.xall[z] if l == 0 else r.zout[0]).astype(F32)
        dn, dg1 = norm_back(dh1, xin, gain(l, 0))
        r.vgrad[4 * l : 4 * l + 1, :] = dg1
        dx = (r.dy1[...] + dn).astype(BF)
        r.gout[l] = dx
        return dx

    def gap_f0a():
        weight_e("q", 0)
        weight_c("u", 0)
        weight_e("o", 0)
        weight_c("d", 0)
        weight_d("q", 0)

    def gap_f0b():
        weight_d("o", 0)
        weight_e("u", 0)
        weight_e("d", 0)
        weight_b("q", 1)
        weight_b("o", 1)

    attn_forward(0, None, gap_f0a, gap_f0b)
    turn_qkv(0)
    out_proj(0, r.xall[z].astype(F32))

    def gap_f0c():
        weight_c("q", 1)
        weight_c("o", 1)
        turn("o", 0)
        weight_d("u", 0)
        weight_d("d", 0)
        weight_b("u", 1)
        weight_b("d", 1)

    def gap_f0d():
        weight_e("q", 1)
        weight_e("o", 1)
        weight_c("u", 1)
        weight_c("d", 1)

    mlp_forward(0, gap_f0c, gap_f0d)
    weight_d("q", 1)
    weight_d("o", 1)
    turn("u", 0)
    weight_e("u", 1)
    weight_e("d", 1)
    turn("d", 0)
    finish_layer(0)
    xhat1, _ = normalise(r.zout[0].astype(F32))

    attn_forward(1, xhat1, lambda: None, lambda: None)
    weight_d("u", 1)
    weight_d("d", 1)
    turn_qkv(1)
    out_proj(1, r.zout[0].astype(F32))

    def gap_f1c():
        turn("o", 1)

    mlp_forward(1, gap_f1c, None)
    turn("u", 1)
    turn("d", 1)
    finish_layer(1)
    push("zo", 0, r.zout.at[1 - c], lo_ref.at[c], sib)
    local_start("out", 0, r.zout.at[c], lo_ref.at[c])

    rs_sent("m0")
    local_wait("dz", 0, r.dzin)
    mlp_backward(1, r.dzin[...].astype(F32), lambda: None, lambda: None)
    rs_sent("m1")

    def nothing():
        pass

    attn_backward(1, nothing, nothing)
    for t in "qoud":
        sent("ga" + t + "1")
    rs_sent("dh21")

    def gap_b0a():
        grad_third("d", 1)
        grad_third("u", 1)

    def gap_b0b():
        grad_third("q", 1)
        grad_third("o", 1)

    mlp_backward(0, r.gout[1].astype(F32), gap_b0a, gap_b0b)
    rs_sent("dh11")

    def gap_b0c():
        grad_fourth("d", 1)
        grad_fourth("u", 1)

    def gap_b0d():
        grad_fourth("q", 1)
        grad_fourth("o", 1)

    attn_backward(0, gap_b0c, gap_b0d)

    push("go", 0, r.gout.at[1 - c], gi_ref.at[c], sib)
    local_start("out", 1, r.gout.at[c], gi_ref.at[c])
    gv = r.vgrad[...]
    r.vsend[2] = gv
    push("ga", 0, r.vsend.at[2], r.vrecv.at[7], sib)
    grad_third("d", 0)
    grad_third("u", 0)
    arrived("ga", 0, r.vrecv.at[7])
    gv = gv + r.vrecv[7]
    spread("gx", 3, 8, gv, xpeer)
    late = ["go"] + [n + t + "0" for n in ("ga", "gb", "gc", "ge") for t in "qoud"]
    for group in {k[0]: None for k in list(pending)}:
        if group not in late and group not in ("ga", "gx"):
            sent(group)
    grad_third("q", 0)
    grad_third("o", 0)
    grad_fourth("d", 0)
    grad_fourth("u", 0)
    gv = gathered("gx", 8, gv)
    spread("gy", 4, 11, gv, ypeer)
    grad_fourth("q", 0)
    grad_fourth("o", 0)
    gv = gathered("gy", 11, gv)
    spread("gz", 5, 14, gv, zpeer)
    for l in (1, 0):
        for t in "duqo":
            grad_done(t, l)
    push("fo", 0, r.fin.at[1 - c], fother_ref, sib)
    local_start("out", 2, r.fin.at[c], fin_ref)
    r.vgrad[...] = gathered("gz", 14, gv)
    local_start("out2", 0, r.vgrad, gv_ref)
    arrived("zo", 0, lo_ref.at[1 - c])
    arrived("go", 0, gi_ref.at[1 - c])
    arrived("fo", 0, fother_ref)
    local_wait("out", 0, lo_ref.at[c])
    local_wait("out", 1, gi_ref.at[c])
    local_wait("out", 2, fin_ref)
    local_wait("out2", 0, gv_ref)
    rs_sent("dh20")
    rs_sent("dh10")
    for group in {k[0]: None for k in list(pending)}:
        sent(group)


def assemble(fin_in, fother_in, lo, gi, gv_in, lo_ref, gi_ref, gq_ref, go_ref, gu_ref, gd_ref, gv_ref, fin, fother, gv, sem):
    c = lax.axis_index("section")
    p = lax.axis_index("shard")
    pairs = [(fin_in, fin), (fother_in, fother), (gv_in, gv)]
    pairs += [(lo.at[m], lo_ref.at[0, m, 0]) for m in range(2)]
    pairs += [(gi.at[m], gi_ref.at[0, m, 0]) for m in range(2)]
    moves = [pltpu.make_async_copy(a, b, sem.at[n]) for n, (a, b) in enumerate(pairs)]
    for move in moves:
        move.start()
    moves[2].wait()
    both = gv[:, pl.ds(pl.multiple_of((p // 2) * 128, 128), 128)]
    both = jnp.where(c == 0, both[:4], both[4:])
    gv_ref[0] = jnp.where(p % 2 == 0, both[:, :64], both[:, 64:])
    for n, ref, which in ((0, fin, c), (1, fother, 1 - c)):
        moves[n].wait()
        wide = pl.ds(pl.multiple_of(which * 512, 512), 512)
        for zz in range(4):
            for t in range(3):
                col = pl.multiple_of(t * 1024 + zz * 256 + which * 128, 128)
                gq_ref[0, :, pl.ds(col, 128)] = ref[zz, :, t * 128 : t * 128 + 128].astype(F32)
            gd_ref[0, 64 * zz : 64 * zz + 64, wide] = ref[zz, :, 1408:1920].astype(F32)
        total = ref[0, :, 384:896].astype(F32)
        for zz in range(1, 4):
            total = total + ref[zz, :, 384:896].astype(F32)
        go_ref[0, :, wide] = total
        ups = [ref[zz, :, 896:1408].astype(F32) for zz in range(4)]
        for n in range(8):
            row = jnp.concatenate([u[:, 64 * n : 64 * n + 64] for u in ups], axis=1)
            gu_ref[0, :, pl.ds(pl.multiple_of((which * 8 + n) * 256, 256), 256)] = row
    for move in moves[3:]:
        move.wait()


def local(acts_in, cotangent, qkv_weight, out_weight, up_weight, down_weight, vectors, image_ids):
    vmem = pl.BlockSpec(memory_space=pltpu.VMEM)
    hbm = pl.BlockSpec(memory_space=pl.ANY)
    out = pl.pallas_call(
        kernel,
        out_shape=(
            jax.ShapeDtypeStruct((4, 64, HALF), BF),
            jax.ShapeDtypeStruct((4, 64, HALF), BF),
            jax.ShapeDtypeStruct((2, ROWS, D), BF),
            jax.ShapeDtypeStruct((2, ROWS, D), BF),
            jax.ShapeDtypeStruct((8, D), F32),
        ),
        in_specs=[hbm] * 8,
        out_specs=(hbm,) * 5,
        scratch_shapes=[pltpu.VMEM(s, t) for s, t in SCRATCH.values()]
        + [pltpu.SemaphoreType.DMA((len(GROUP), 3)), pltpu.SemaphoreType.DMA((len(GROUP), 3))],
        compiler_params=pltpu.CompilerParams(
            collective_id=0, has_side_effects=True, vmem_limit_bytes=64 * 1024 * 1024 - 65536
        ),
    )(acts_in, cotangent, qkv_weight, out_weight, up_weight, down_weight, vectors, image_ids)
    return pl.pallas_call(
        assemble,
        out_shape=(
            jax.ShapeDtypeStruct((1, 2, 1, ROWS, D), BF),
            jax.ShapeDtypeStruct((1, 2, 1, ROWS, D), BF),
            jax.ShapeDtypeStruct((1, 64, 3072), F32),
            jax.ShapeDtypeStruct((1, 64, D), F32),
            jax.ShapeDtypeStruct((1, 64, 4096), F32),
            jax.ShapeDtypeStruct((1, 256, D), F32),
            jax.ShapeDtypeStruct((1, 4, 64), F32),
        ),
        in_specs=[hbm] * 5,
        out_specs=(vmem,) * 7,
        scratch_shapes=[
            pltpu.VMEM((4, 64, HALF), BF),
            pltpu.VMEM((4, 64, HALF), BF),
            pltpu.VMEM((8, D), F32),
            pltpu.SemaphoreType.DMA((7,)),
        ],
        compiler_params=pltpu.CompilerParams(vmem_limit_bytes=64 * 1024 * 1024 - 65536),
    )(*out)


def solution(mesh):
    placed = (
        P(None, "shard", "seq", None),
        P(None, "shard", "seq", None),
        P("section", "shard", None),
        P("section", "shard", None),
        P("section", "shard", None),
        P("section", "shard", None),
        P("section", None, "shard"),
        P(None, "shard", None),
    )
    return jax.shard_map(
        local,
        mesh=mesh,
        in_specs=placed,
        out_specs=(
            P("section", None, "shard", "seq", None),
            P("section", None, "shard", "seq", None),
            P("section", "shard", None),
            P("section", "shard", None),
            P("section", "shard", None),
            P("section", "shard", None),
            P("section", None, "shard"),
        ),
        check_vma=False,
    )
```

```python
import jax
import jax.numpy as jnp
from jax import lax
from jax.experimental import pallas as pl
from jax.experimental.pallas import tpu as pltpu
from jax.sharding import PartitionSpec as P

EPS = 1e-06
NEG = -1e30
BF = jnp.bfloat16
F32 = jnp.float32
MESH = pl.DeviceIdType.MESH
D = 1024
ROWS = 72
N = 4 * ROWS
TENSORS = {"q": (0, 384, True), "o": (384, 512, False), "u": (896, 512, True), "d": (1408, 512, False)}
HALF = 1920


def dot(a, b):
    return lax.dot_general(a, b, (((1,), (0,)), ((), ())), preferred_element_type=F32)


def dot_rows(a, b):
    return lax.dot_general(a, b, (((0,), (0,)), ((), ())), preferred_element_type=F32)


def dot_cols(a, b):
    return lax.dot_general(a, b, (((1,), (1,)), ((), ())), preferred_element_type=F32)


def normalise(values):
    centre = values - jnp.mean(values, axis=-1, keepdims=True)
    scale = lax.rsqrt(jnp.mean(centre * centre, axis=-1, keepdims=True) + EPS)
    return centre * scale, scale


def norm_back(grad, values, gain):
    xhat, scale = normalise(values)
    f = grad * gain
    dv = scale * (
        f
        - jnp.mean(f, axis=-1, keepdims=True)
        - xhat * jnp.mean(f * xhat, axis=-1, keepdims=True)
    )
    return dv, jnp.sum(grad * xhat, axis=0, keepdims=True)


def gelu_parts(u):
    cdf = 0.5 * (1.0 + lax.erf(u * 0.7071067811865476))
    slope = cdf + u * jnp.exp(-0.5 * u * u) * 0.3989422804014327
    return u * cdf, slope


SCRATCH = dict(
    vectors=((1, 4, 64), BF),
    ids=((1, N), jnp.int32),
    ustage=((16, 64, 128), BF),
    usend=((64, 512), BF),
    xall=((4, ROWS, D), BF),
    dzin=((ROWS, D), BF),
    vsend=((7, 8, D), F32),
    vrecv=((17, 8, D), F32),
    vec=((8, D), F32),
    vgrad=((8, D), F32),
    h1=((2, 4, ROWS, D), BF),
    qkv=((2, 4, ROWS, 768), BF),
    prob=((2, 4, N, N), BF),
    wqt=((2, 768, D), BF),
    osend=((2, 4, ROWS, 256), BF),
    ojoin=((2, 4, ROWS, 256), BF),
    a=((2, ROWS, D), F32),
    y1=((2, ROWS, D), F32),
    h2=((2, 4, ROWS, D), BF),
    slope=((2, 4, ROWS, D), BF),
    g=((2, 4, ROWS, D), BF),
    stage=((2, 4, ROWS, D), BF),
    part=((6, 3, ROWS, D), BF),
    m=((2, ROWS, D), F32),
    dm=((2, 4, ROWS, D), BF),
    du=((4, ROWS, D), BF),
    dy1=((ROWS, D), F32),
    da=((ROWS, D), BF),
    dosend=((2, 4, ROWS, 256), BF),
    dojoin=((2, 4, ROWS, 256), BF),
    dqkv=((4, ROWS, 768), BF),
    zout=((2, ROWS, D), BF),
    gout=((2, ROWS, D), BF),
    fin=((2, 4, 64, HALF), BF),
)
for _t, (_, _h, _x) in TENSORS.items():
    SCRATCH["own" + _t] = ((2, 64, _h), BF)
    SCRATCH["w" + _t] = ((2, 2, 4, 4, 64, _h), BF)
    SCRATCH["lt" + _t] = ((4, 256, 4 * ROWS), BF)
    SCRATCH["gs" + _t] = ((4, 4, 64, _h), BF)
    SCRATCH["ra" + _t] = ((2, 4, 4, 64, _h), BF)
    SCRATCH["rb" + _t] = ((2, 3, 4, 64, _h), BF)
    SCRATCH["rc" + _t] = ((2, 3, 64, _h), BF)

GROUPS = (
    ["x", "dz", "us", "vin", "iin", "out", "out2", "out3", "va", "vx", "vy", "ga", "gx", "gy", "gz", "zo", "go", "fo"]
    + [n + t + str(l) for n in ("A", "L", "B", "Bl", "C", "E", "D", "ga", "gb", "gc", "ge") for t in "qoud" for l in (0, 1)]
    + [n + str(l) for n in ("h1", "h2", "o", "m", "dm", "dh2", "do", "dh1") for l in (0, 1)]
)
GROUP = {n: i for i, n in enumerate(dict.fromkeys(GROUPS))}


class Refs:
    pass


def kernel(acts, cot, wq, wo, wu, wd, vectors_in, ids_in, fin_ref, fother_ref, lo_ref, gi_ref, gv_ref, *scratch):
    r = Refs()
    for name, ref in zip(SCRATCH, scratch):
        setattr(r, name, ref)
    ssem, rsem = scratch[len(SCRATCH) :]
    c = lax.axis_index("section")
    z = lax.axis_index("seq")
    p = lax.axis_index("shard")
    y, x = p // 4, p % 4
    sib = {"section": 1 - c}

    def zpeer(k):
        return {"seq": (z + k) % 4}

    def xpeer(k):
        return {"shard": y * 4 + (x + k) % 4}

    def ypeer(k):
        return {"shard": ((y + k) % 4) * 4 + x}

    pending = {}

    def copy(group, slot, src, dst, dev):
        return pltpu.make_async_remote_copy(
            src_ref=src,
            dst_ref=dst,
            send_sem=ssem.at[GROUP[group], slot],
            recv_sem=rsem.at[GROUP[group], slot],
            device_id=dev,
            device_id_type=MESH,
        )

    def push(group, slot, src, dst, dev):
        copy(group, slot, src, dst, dev).start()
        pending[(group, slot)] = (src, dev)

    def sent(group):
        for key in [k for k in pending if k[0] == group]:
            src, dev = pending.pop(key)
            copy(group, key[1], src, src, dev).wait_send()

    def arrived(group, slot, dst):
        copy(group, slot, dst, dst, sib).wait_recv()

    def local_start(group, slot, src, dst):
        pltpu.make_async_copy(src, dst, ssem.at[GROUP[group], slot]).start()

    def local_wait(group, slot, dst):
        pltpu.make_async_copy(dst, dst, ssem.at[GROUP[group], slot]).wait()

    def piece(t, which):
        if t == "q":
            return [
                (wq.at[0, :, pl.ds(pl.multiple_of(n * 1024 + z * 256 + which * 128, 128), 128)], n * 128, 128)
                for n in range(3)
            ]
        cols = pl.ds(pl.multiple_of(which * 512, 512), 512)
        if t == "o":
            return [(wo.at[0, :, cols], 0, 512)]
        return [(wd.at[0, pl.ds(pl.multiple_of(z * 64, 64), 64), cols], 0, 512)]

    def own(t):
        return getattr(r, "own" + t)

    local_start("vin", 0, vectors_in, r.vectors)
    local_start("iin", 0, ids_in.at[c], r.ids)
    local_start("x", 0, acts.at[c, 0], r.xall.at[z])

    @pl.loop(0, 16)
    def _(n):
        col = pl.multiple_of(n * 256 + (z // 2) * 128, 128)
        local_start("us", 0, wu.at[0, :, pl.ds(col, 128)], r.ustage.at[n])

    for t in "qod":
        for n, (src, at, width) in enumerate(piece(t, c)):
            local_start("L" + t + "0", n, src, own(t).at[c, :, pl.ds(at, width)])
    local_start("dz", 0, cot.at[c, 0], r.dzin)

    barrier = pltpu.get_barrier_semaphore()
    for dev in [sib] + [f(k) for f in (xpeer, ypeer, zpeer) for k in (1, 2, 3)]:
        pl.semaphore_signal(barrier, inc=1, device_id=dev, device_id_type=MESH)
    rows8 = lax.broadcasted_iota(jnp.int32, (8, 128), 0)
    lanes8 = lax.broadcasted_iota(jnp.int32, (8, 128), 1)
    local_wait("vin", 0, r.vectors)
    vown = r.vectors[0].astype(F32)
    vown = jnp.concatenate([vown, vown], axis=0)
    vown = jnp.concatenate([vown, vown], axis=1)
    keep = jnp.logical_and(rows8 // 4 == c, lanes8 // 64 == p % 2)
    r.vsend[6] = jnp.zeros((8, D), F32)
    r.vsend[6, :, pl.ds(pl.multiple_of((p // 2) * 128, 128), 128)] = jnp.where(keep, vown, 0.0)
    pl.semaphore_wait(barrier, 10)

    def half(h, which):
        return pl.ds(pl.multiple_of(which * h, 128), h)

    push("va", 0, r.vsend.at[6], r.vrecv.at[0], sib)
    for t in "qod":
        for n, (src, at, width) in enumerate(piece(t, 1 - c)):
            push("A" + t + "0", n, src, own(t).at[c, :, pl.ds(at, width)], sib)
    local_wait("x", 0, r.xall.at[z])
    for k in (1, 3, 2):
        push("h10", k - 1, r.xall.at[z], r.xall.at[z], zpeer(k))
    local_wait("us", 0, r.ustage)

    def up_half(which):
        lower = lax.broadcasted_iota(jnp.int32, (64, 128), 1) < 64
        tiles = []
        for n in range(4):
            first = r.ustage[8 * which + 2 * n].astype(F32)
            second = r.ustage[8 * which + 2 * n + 1].astype(F32)
            even = jnp.where(lower, first, pltpu.roll(second, 64, 1))
            odd = jnp.where(lower, pltpu.roll(first, 64, 1), second)
            tiles.append(jnp.where(z % 2 == 0, even, odd).astype(BF))
        return jnp.concatenate(tiles, axis=1)

    r.usend[...] = up_half(1 - c)
    push("Au0", 0, r.usend, own("u").at[c], sib)
    r.ownu[c] = up_half(c)

    def own_ready(t):
        for n, (_, at, width) in enumerate(piece(t, c) if t != "u" else [(None, 0, 512)]):
            if t != "u":
                local_wait("L" + t + "0", n, own(t).at[c, :, pl.ds(at, width)])
            arrived("A" + t + "0", n, own(t).at[1 - c, :, pl.ds(at, width)])

    def wref(t):
        return getattr(r, "w" + t)

    def local_copy(t, l):
        return pltpu.make_async_copy(
            own(t).at[l], wref(t).at[l, c, y, x], ssem.at[GROUP["Bl" + t + str(l)], 0]
        )

    def weight_b(t, l):
        _, h, xfirst = TENSORS[t]
        peer = xpeer if xfirst else ypeer
        for k in (1, 3, 2):
            push("B" + t + str(l), k - 1, own(t).at[l], wref(t).at[l, c, y, x], peer(k))
        local_copy(t, l).start()

    def weight_c(t, l):
        _, h, xfirst = TENSORS[t]
        local_copy(t, l).wait()
        for k in (1, 2, 3):
            if xfirst:
                arrived("B" + t + str(l), k - 1, wref(t).at[l, c, y, (x + 4 - k) % 4])
            else:
                arrived("B" + t + str(l), k - 1, wref(t).at[l, c, (y + 4 - k) % 4, x])
        line = wref(t).at[l, c, y] if xfirst else wref(t).at[l, c, :, x]
        peer = ypeer if xfirst else xpeer
        for k in (1, 3):
            push("C" + t + str(l), k - 1, line, line, peer(k))

    def line_of(t, l, back, part=None):
        if TENSORS[t][2]:
            ref = wref(t).at[l, c, (y + 4 - back) % 4]
            return ref if part is None else ref.at[pl.ds(2 * part, 2)]
        if part is None:
            return wref(t).at[l, c, :, (x + 4 - back) % 4]
        return wref(t).at[l, c, pl.ds(2 * part, 2), (x + 4 - back) % 4]

    def weight_e(t, l):
        peer = ypeer if TENSORS[t][2] else xpeer
        for k, part in ((1, 0), (3, 1)):
            arrived("C" + t + str(l), k - 1, line_of(t, l, k))
            push("E" + t + str(l), k - 1, line_of(t, l, k, part), line_of(t, l, k, part), peer(k))

    def weight_d(t, l):
        for k, part in ((1, 0), (3, 1)):
            arrived("E" + t + str(l), k - 1, line_of(t, l, 2, part))
        mine = wref(t).at[l, c]
        push("D" + t + str(l), 0, mine, mine, sib)

    def weight_done(t, l):
        arrived("D" + t + str(l), 0, wref(t).at[l, 1 - c])

    def spread(group, at, slots, value, peer):
        r.vsend[at] = value
        for k in (1, 2, 3):
            push(group, k - 1, r.vsend.at[at], r.vrecv.at[slots + k - 1], peer(k))

    def gathered(group, slots, value):
        for k in (1, 2, 3):
            arrived(group, k - 1, r.vrecv.at[slots + k - 1])
        return value + (r.vrecv[slots] + (r.vrecv[slots + 1] + r.vrecv[slots + 2]))

    arrived("va", 0, r.vrecv.at[0])
    v = r.vsend[6] + r.vrecv[0]
    spread("vx", 0, 1, v, xpeer)
    own_ready("q")
    weight_b("q", 0)
    own_ready("o")
    weight_b("o", 0)
    v = gathered("vx", 1, v)
    spread("vy", 1, 4, v, ypeer)
    weight_c("q", 0)
    weight_c("o", 0)
    own_ready("u")
    own_ready("d")
    weight_b("u", 0)
    weight_b("d", 0)
    local_wait("iin", 0, r.ids)
    v = gathered("vy", 4, v)
    r.vec[...] = v

    def gain(l, row):
        return r.vec[4 * l + row : 4 * l + row + 1, :]

    def send_block(group, ref):
        for k in (1, 3, 2):
            push(group, k - 1, ref.at[z], ref.at[z], zpeer(k))

    def each_block(body, first=0, last=4):
        @pl.loop(first, last)
        def _(n):
            k = jnp.where(n == 2, 3, jnp.where(n == 3, 2, n))
            body(k, (z + 4 - k) % 4)

    def flat(value):
        return value.reshape(N, value.shape[-1])

    def weight(t, l, j):
        return wref(t)[l, j // 2, :, :, :, 256 * (j % 2) : 256 * (j % 2) + 256].reshape(D, 256)

    def turn(t, l):
        for n in "CED":
            sent(n + t + str(l))

        def tile(a, b):
            return wref(t).at[l, b // 2, a, :, :, pl.ds(256 * (b % 2), 256)]

        for a in range(4):
            for b in range(a, 4):
                upper = tile(a, b)[...].reshape(256, 256)
                if a < b:
                    lower = tile(b, a)[...].reshape(256, 256)
                    tile(a, b)[...] = lower.T.reshape(4, 64, 256)
                tile(b, a)[...] = upper.T.reshape(4, 64, 256)

    def turn_qkv(l):
        for h in range(2):
            for n in range(3):
                for a in range(4):
                    w = wref("q")[l, h, a, :, :, 128 * n : 128 * n + 128].reshape(256, 128)
                    r.wqt[l, 384 * h + 128 * n : 384 * h + 128 * n + 128, 256 * a : 256 * a + 256] = w.T

    def image(axis):
        row = r.ids[...]
        place = lax.broadcasted_iota(jnp.int32, (N, 1) if axis == 0 else (1, N), axis)
        one = jnp.sum((row < 1).astype(jnp.int32), axis=1, keepdims=True)
        two = jnp.sum((row < 2).astype(jnp.int32), axis=1, keepdims=True)
        return (place >= one).astype(jnp.int32) + (place >= two).astype(jnp.int32)

    lanes = lax.broadcasted_iota(jnp.int32, (1, 128), 1)
    low_lanes = lanes < 64

    def mask_head(value, head):
        keep = low_lanes if head == 0 else jnp.logical_not(low_lanes)
        return jnp.where(keep, value, jnp.zeros_like(value))

    RS = {"m0": 0, "m1": 1, "dh21": 2, "dh11": 3, "dh20": 4, "dh10": 5}

    def rs_slot(group, k, blk, start):
        i = RS[group]
        return copy(
            group, 3 - k,
            r.stage.at[i % 2, blk], r.part.at[i, 3 - k],
            {"seq": blk},
        )

    def rs_put(group, k, blk, make):
        i = RS[group]
        for j in range(4):
            r.stage[i % 2, blk, :, 256 * j : 256 * j + 256] = make(j).astype(BF)

        @pl.when(k > 0)
        def _():
            rs_slot(group, k, blk, True).start()

    def rs_sum(group):
        i = RS[group]
        for s in range(3):
            arrived(group, s, r.part.at[i, s])
        return r.stage[i % 2, z].astype(F32) + (
            r.part[i, 0].astype(F32) + (r.part[i, 1].astype(F32) + r.part[i, 2].astype(F32))
        )

    def rs_sent(group):
        i = RS[group]
        for k in (1, 2, 3):
            rs_slot(group, k, (z + 4 - k) % 4, False).wait_send()

    def ag_wait(group, ref, k, blk):
        @pl.when(k > 0)
        def _():
            copy(group, k - 1, ref.at[blk], ref.at[blk], sib).wait_recv()

    def attn_forward(l, xhat, gap_a, gap_b):
        if l > 0:
            r.h1[l, z] = (xhat * gain(l, 0)).astype(BF)
            send_block("h1" + str(l), r.h1.at[l])
        gap_a()
        weight_done("q", l)

        def body(k, blk):
            if l > 0:
                ag_wait("h1" + str(l), r.h1.at[l], k, blk)
            else:
                ag_wait("h10", r.xall, k, blk)
                hat, _ = normalise(r.xall[blk].astype(F32))
                r.h1[0, blk] = (hat * gain(0, 0)).astype(BF)
            for j in range(2):
                w = wref("q")[l, j].reshape(D, 384)
                r.qkv[l, blk, :, 384 * j : 384 * j + 384] = dot(r.h1[l, blk], w).astype(BF)

        each_block(body)

        gap_b()
        same = image(0) == image(1)

        @pl.loop(0, 2)
        def _(pair):
            base = pl.multiple_of(pair * 384, 128)
            q = flat(r.qkv[l, :, :, pl.ds(base, 128)])
            kk = flat(r.qkv[l, :, :, pl.ds(pl.multiple_of(base + 128, 128), 128)])
            vv = flat(r.qkv[l, :, :, pl.ds(pl.multiple_of(base + 256, 128), 128)])
            q = q * jnp.asarray(0.125, BF)
            res = []
            for head in range(2):
                s = dot_cols(mask_head(q, head), kk)
                s = jnp.where(same, s, NEG)
                e = jnp.exp(s - jnp.max(s, axis=-1, keepdims=True))
                pb = (e * (1.0 / jnp.sum(e, axis=-1, keepdims=True))).astype(BF)
                r.prob[l, 2 * pair + head] = pb
                res.append(dot(pb, vv))
            o = jnp.where(low_lanes, res[0], res[1]).astype(BF)
            r.osend[l, :, :, pl.ds(pl.multiple_of(pair * 128, 128), 128)] = o.reshape(4, ROWS, 128)

        for k in (1, 2, 3):
            blk = (z + k) % 4
            push("o" + str(l), k - 1, r.osend.at[l, blk], r.ojoin.at[l, z], zpeer(k))
        r.ojoin[l, z] = r.osend[l, z]

    def out_proj(l, xin):
        weight_done("o", l)
        for k in (1, 2, 3):
            arrived("o" + str(l), k - 1, r.ojoin.at[l, (z + 4 - k) % 4])
        for j in range(4):
            cols = pl.ds(256 * j, 256)
            acc = None
            for b in range(4):
                w = wref("o")[l, j // 2, b, :, :, 256 * (j % 2) : 256 * (j % 2) + 256].reshape(256, 256)
                term = dot(r.ojoin[l, b], w)
                acc = term if acc is None else acc + term
            r.a[l, :, cols] = acc
        y1 = xin + gain(l, 1) * r.a[l]
        r.y1[l] = y1
        yhat, _ = normalise(y1)
        r.h2[l, z] = (yhat * gain(l, 2)).astype(BF)
        send_block("h2" + str(l), r.h2.at[l])

    def mlp_forward(l, gap_a, gap_b):
        gap_a()
        weight_done("u", l)
        weight_done("d", l)

        def body(k, blk):
            ag_wait("h2" + str(l), r.h2.at[l], k, blk)
            for j in range(4):
                cols = pl.ds(256 * j, 256)
                u = dot(r.h2[l, blk], weight("u", l, j))
                g, slope = gelu_parts(u)
                r.g[l, blk, :, cols] = g.astype(BF)
                r.slope[l, blk, :, cols] = slope.astype(BF)

            def make(j):
                return dot(r.g[l, blk], weight("d", l, j))

            rs_put("m" + str(l), k, blk, make)

        if gap_b is None:
            each_block(body)
        else:
            each_block(body, 0, 2)
            gap_b()
            each_block(body, 2, 4)

    def finish_layer(l):
        m = rs_sum("m" + str(l))
        r.m[l] = m
        r.zout[l] = (r.y1[l] + gain(l, 3) * m).astype(BF)

    def grad_first(t, l, left, right):
        _, h, _ = TENSORS[t]
        gs, lt = getattr(r, "gs" + t), getattr(r, "lt" + t)

        @pl.loop(0, 4)
        def _(b):
            turned = left(b).T
            lt[b, :, : turned.shape[1]] = turned
            gs[b] = dot(turned, right(half(h, 1 - c))).astype(BF).reshape(4, 64, h)

        push("ga" + t + str(l), 0, gs, getattr(r, "ra" + t).at[l], sib)

    def grad_second(t, l, right):
        _, h, xfirst = TENSORS[t]
        ra, lt = getattr(r, "ra" + t), getattr(r, "lt" + t)
        depth = ROWS if t == "o" else N
        arrived("ga" + t + str(l), 0, ra.at[l])

        @pl.loop(0, 4)
        def _(b):
            val = dot(lt[b, :, :depth], right(half(h, c))).reshape(4, 64, h)
            ra[l, b] = (val + ra[l, b].astype(F32)).astype(BF)

        for k in (1, 2, 3):
            if xfirst:
                src, dev = ra.at[l, (y + k) % 4], ypeer(k)
            else:
                src, dev = ra.at[l, :, (x + k) % 4], xpeer(k)
            push("gb" + t + str(l), k - 1, src, getattr(r, "rb" + t).at[l, k - 1], dev)

    def grad_third(t, l):
        _, h, xfirst = TENSORS[t]
        ra, rb = getattr(r, "ra" + t), getattr(r, "rb" + t)
        for k in (1, 2, 3):
            arrived("gb" + t + str(l), k - 1, rb.at[l, k - 1])

        @pl.loop(0, 4)
        def _(i):
            yy, xx = (y, i) if xfirst else (i, x)
            val = ra[l, yy, xx].astype(F32) + rb[l, 0, i].astype(F32)
            val = val + (rb[l, 1, i].astype(F32) + rb[l, 2, i].astype(F32))
            ra[l, yy, xx] = val.astype(BF)

        for k in (1, 2, 3):
            if xfirst:
                src, dev = ra.at[l, y, (x + k) % 4], xpeer(k)
            else:
                src, dev = ra.at[l, (y + k) % 4, x], ypeer(k)
            push("gc" + t + str(l), k - 1, src, getattr(r, "rc" + t).at[l, k - 1], dev)

    def grad_fourth(t, l):
        off, h, xfirst = TENSORS[t]
        ra, rc = getattr(r, "ra" + t), getattr(r, "rc" + t)
        for k in (1, 2, 3):
            arrived("gc" + t + str(l), k - 1, rc.at[l, k - 1])
        val = ra[l, y, x].astype(F32) + rc[l, 0].astype(F32)
        val = val + (rc[l, 1].astype(F32) + rc[l, 2].astype(F32))
        r.fin[l, z, :, off : off + h] = val.astype(BF)
        block = r.fin.at[l, z, :, pl.ds(off, h)]
        for k in (1, 2, 3):
            push("ge" + t + str(l), k - 1, block, block, zpeer(k))

    def grad_done(t, l):
        off, h, _ = TENSORS[t]
        for k in (1, 2, 3):
            arrived("ge" + t + str(l), k - 1, r.fin.at[l, (z + 4 - k) % 4, :, pl.ds(off, h)])

    def mlp_backward(l, dz, gap_a, gap_b):
        r.dm[l, z] = (gain(l, 3) * dz).astype(BF)
        send_block("dm" + str(l), r.dm.at[l])
        r.vgrad[4 * l + 3 : 4 * l + 4, :] = jnp.sum(dz * r.m[l], axis=0, keepdims=True)
        r.dy1[...] = dz
        gap_a()

        def body(k, blk):
            ag_wait("dm" + str(l), r.dm.at[l], k, blk)
            for b in range(4):
                cols = pl.ds(256 * b, 256)
                grad = dot(r.dm[l, blk], weight("d", l, b))
                r.du[blk, :, cols] = (grad * r.slope[l, blk, :, cols].astype(F32)).astype(BF)

            def make(b):
                return dot(r.du[blk], weight("u", l, b))

            rs_put("dh2" + str(l), k, blk, make)

        each_block(body)

        def tile(ref):
            return lambda b: flat(ref[:, :, pl.ds(pl.multiple_of(b * 256, 256), 256)])

        def cols_of(ref):
            return lambda cols: flat(ref[:, :, cols])

        g_l, h2_l, dm_l = r.g.at[l], r.h2.at[l], r.dm.at[l]
        grad_first("d", l, tile(g_l), cols_of(dm_l))
        grad_first("u", l, tile(h2_l), cols_of(r.du))
        gap_b()
        dh2 = rs_sum("dh2" + str(l))
        dn, dg2 = norm_back(dh2, r.y1[l], gain(l, 2))
        r.vgrad[4 * l + 2 : 4 * l + 3, :] = dg2
        dy1 = r.dy1[...] + dn
        r.dy1[...] = dy1
        r.da[...] = (gain(l, 1) * dy1).astype(BF)
        for k in (2, 1, 3, 0):
            blk = (z + k) % 4
            cols = pl.ds(pl.multiple_of(256 * (blk % 2), 256), 256)
            w = wref("o")[l, blk // 2, :, :, :, cols].reshape(D, 256)
            r.dosend[l, blk] = dot(r.da[...], w).astype(BF)
            if k > 0:
                push("do" + str(l), k - 1, r.dosend.at[l, blk], r.dojoin.at[l, z], zpeer(k))
        r.dojoin[l, z] = r.dosend[l, z]
        r.vgrad[4 * l + 1 : 4 * l + 2, :] = jnp.sum(dy1 * r.a[l], axis=0, keepdims=True)
        grad_second("d", l, cols_of(dm_l))
        grad_second("u", l, cols_of(r.du))

    def attn_backward(l, gap_a, gap_b):
        gap_a()
        for k in (1, 2, 3):
            arrived("do" + str(l), k - 1, r.dojoin.at[l, (z + 4 - k) % 4])

        @pl.loop(0, 2)
        def _(pair):
            base = pl.multiple_of(pair * 384, 128)
            c_k = pl.ds(pl.multiple_of(base + 128, 128), 128)
            c_v = pl.ds(pl.multiple_of(base + 256, 128), 128)
            q = flat(r.qkv[l, :, :, pl.ds(base, 128)]) * jnp.asarray(0.125, BF)
            kk = flat(r.qkv[l, :, :, c_k])
            vv = flat(r.qkv[l, :, :, c_v])
            do = flat(r.dojoin[l, :, :, pl.ds(pl.multiple_of(pair * 128, 128), 128)])
            dq, dk, dv = [], [], []
            for head in range(2):
                pb = r.prob[l, 2 * pair + head]
                pf = pb.astype(F32)
                dp = dot_cols(mask_head(do, head), vv)
                dv.append(dot_rows(pb, do))
                ds = (pf * (dp - jnp.sum(pf * dp, axis=-1, keepdims=True))).astype(BF)
                dq.append(dot(ds, kk))
                dk.append(dot_rows(ds, q))

            def put(cols, both, scale):
                val = jnp.where(low_lanes, both[0], both[1])
                if scale is not None:
                    val = val * scale
                r.dqkv[:, :, cols] = val.astype(BF).reshape(4, ROWS, 128)

            put(pl.ds(base, 128), dq, 0.125)
            put(c_k, dk, None)
            put(c_v, dv, None)

        def body(k, blk):
            def make(b):
                return dot(r.dqkv[blk], r.wqt[l, :, 256 * b : 256 * b + 256])

            rs_put("dh1" + str(l), k, blk, make)

        each_block(body)

        def left_q(b):
            return flat(r.h1[l, :, :, pl.ds(pl.multiple_of(b * 256, 256), 256)])

        def right_q(cols):
            return flat(r.dqkv[:, :, cols])

        def left_o(b):
            return r.ojoin[l, b]

        def right_o(cols):
            return r.da[:, cols]

        grad_first("q", l, left_q, right_q)
        grad_first("o", l, left_o, right_o)
        gap_b()
        grad_second("q", l, right_q)
        grad_second("o", l, right_o)
        dh1 = rs_sum("dh1" + str(l))
        xin = (r.xall[z] if l == 0 else r.zout[0]).astype(F32)
        dn, dg1 = norm_back(dh1, xin, gain(l, 0))
        r.vgrad[4 * l : 4 * l + 1, :] = dg1
        dx = (r.dy1[...] + dn).astype(BF)
        r.gout[l] = dx
        return dx

    def gap_f0a():
        weight_e("q", 0)
        weight_c("u", 0)
        weight_e("o", 0)
        weight_c("d", 0)
        weight_d("q", 0)

    def gap_f0b():
        weight_d("o", 0)
        weight_e("u", 0)
        weight_e("d", 0)
        weight_b("q", 1)
        weight_b("o", 1)

    attn_forward(0, None, gap_f0a, gap_f0b)
    turn_qkv(0)
    out_proj(0, r.xall[z].astype(F32))

    def gap_f0c():
        weight_c("q", 1)
        weight_c("o", 1)
        turn("o", 0)
        weight_d("u", 0)
        weight_d("d", 0)
        weight_b("u", 1)
        weight_b("d", 1)

    def gap_f0d():
        weight_e("q", 1)
        weight_e("o", 1)
        weight_c("u", 1)
        weight_c("d", 1)

    mlp_forward(0, gap_f0c, gap_f0d)
    weight_d("q", 1)
    weight_d("o", 1)
    turn("u", 0)
    weight_e("u", 1)
    weight_e("d", 1)
    turn("d", 0)
    finish_layer(0)
    xhat1, _ = normalise(r.zout[0].astype(F32))

    attn_forward(1, xhat1, lambda: None, lambda: None)
    weight_d("u", 1)
    weight_d("d", 1)
    turn_qkv(1)
    out_proj(1, r.zout[0].astype(F32))

    def gap_f1c():
        turn("o", 1)

    mlp_forward(1, gap_f1c, None)
    turn("u", 1)
    turn("d", 1)
    finish_layer(1)
    push("zo", 0, r.zout.at[1 - c], lo_ref.at[c], sib)
    local_start("out", 0, r.zout.at[c], lo_ref.at[c])

    rs_sent("m0")
    local_wait("dz", 0, r.dzin)
    mlp_backward(1, r.dzin[...].astype(F32), lambda: None, lambda: None)
    rs_sent("m1")

    def nothing():
        pass

    attn_backward(1, nothing, nothing)
    for t in "qoud":
        sent("ga" + t + "1")
    rs_sent("dh21")

    def gap_b0a():
        grad_third("d", 1)
        grad_third("u", 1)

    def gap_b0b():
        grad_third("q", 1)
        grad_third("o", 1)

    mlp_backward(0, r.gout[1].astype(F32), gap_b0a, gap_b0b)
    rs_sent("dh11")

    def gap_b0c():
        grad_fourth("d", 1)
        grad_fourth("u", 1)

    def gap_b0d():
        grad_fourth("q", 1)
        grad_fourth("o", 1)

    attn_backward(0, gap_b0c, gap_b0d)

    push("go", 0, r.gout.at[1 - c], gi_ref.at[c], sib)
    local_start("out", 1, r.gout.at[c], gi_ref.at[c])
    gv = r.vgrad[...]
    r.vsend[2] = gv
    push("ga", 0, r.vsend.at[2], r.vrecv.at[7], sib)
    grad_third("d", 0)
    grad_third("u", 0)
    arrived("ga", 0, r.vrecv.at[7])
    gv = gv + r.vrecv[7]
    spread("gx", 3, 8, gv, xpeer)
    late = ["go"] + [n + t + "0" for n in ("ga", "gb", "gc", "ge") for t in "qoud"]
    for group in {k[0]: None for k in list(pending)}:
        if group not in late and group not in ("ga", "gx"):
            sent(group)
    grad_third("q", 0)
    grad_third("o", 0)
    grad_fourth("d", 0)
    grad_fourth("u", 0)
    gv = gathered("gx", 8, gv)
    spread("gy", 4, 11, gv, ypeer)
    grad_fourth("q", 0)
    grad_fourth("o", 0)
    gv = gathered("gy", 11, gv)
    spread("gz", 5, 14, gv, zpeer)
    for l in (1, 0):
        for t in "duqo":
            grad_done(t, l)
    push("fo", 0, r.fin.at[1 - c], fother_ref, sib)
    local_start("out", 2, r.fin.at[c], fin_ref)
    r.vgrad[...] = gathered("gz", 14, gv)
    local_start("out2", 0, r.vgrad, gv_ref)
    arrived("zo", 0, lo_ref.at[1 - c])
    arrived("go", 0, gi_ref.at[1 - c])
    arrived("fo", 0, fother_ref)
    local_wait("out", 0, lo_ref.at[c])
    local_wait("out", 1, gi_ref.at[c])
    local_wait("out", 2, fin_ref)
    local_wait("out2", 0, gv_ref)
    rs_sent("dh20")
    rs_sent("dh10")
    for group in {k[0]: None for k in list(pending)}:
        sent(group)


def assemble(fin_in, fother_in, lo, gi, gv_in, lo_ref, gi_ref, gq_ref, go_ref, gu_ref, gd_ref, gv_ref, fin, fother, gv, sem):
    c = lax.axis_index("section")
    p = lax.axis_index("shard")
    pairs = [(fin_in, fin), (fother_in, fother), (gv_in, gv)]
    pairs += [(lo.at[m], lo_ref.at[0, m, 0]) for m in range(2)]
    pairs += [(gi.at[m], gi_ref.at[0, m, 0]) for m in range(2)]
    moves = [pltpu.make_async_copy(a, b, sem.at[n]) for n, (a, b) in enumerate(pairs)]
    for move in moves:
        move.start()
    moves[2].wait()
    both = gv[:, pl.ds(pl.multiple_of((p // 2) * 128, 128), 128)]
    both = jnp.where(c == 0, both[:4], both[4:])
    gv_ref[0] = jnp.where(p % 2 == 0, both[:, :64], both[:, 64:])
    for n, ref, which in ((0, fin, c), (1, fother, 1 - c)):
        moves[n].wait()
        wide = pl.ds(pl.multiple_of(which * 512, 512), 512)
        for zz in range(4):
            for t in range(3):
                col = pl.multiple_of(t * 1024 + zz * 256 + which * 128, 128)
                gq_ref[0, :, pl.ds(col, 128)] = ref[zz, :, t * 128 : t * 128 + 128].astype(F32)
            gd_ref[0, 64 * zz : 64 * zz + 64, wide] = ref[zz, :, 1408:1920].astype(F32)
        total = ref[0, :, 384:896].astype(F32)
        for zz in range(1, 4):
            total = total + ref[zz, :, 384:896].astype(F32)
        go_ref[0, :, wide] = total
        ups = [ref[zz, :, 896:1408].astype(F32) for zz in range(4)]
        for n in range(8):
            row = jnp.concatenate([u[:, 64 * n : 64 * n + 64] for u in ups], axis=1)
            gu_ref[0, :, pl.ds(pl.multiple_of((which * 8 + n) * 256, 256), 256)] = row
    for move in moves[3:]:
        move.wait()


def local(acts_in, cotangent, qkv_weight, out_weight, up_weight, down_weight, vectors, image_ids):
    vmem = pl.BlockSpec(memory_space=pltpu.VMEM)
    hbm = pl.BlockSpec(memory_space=pl.ANY)
    out = pl.pallas_call(
        kernel,
        out_shape=(
            jax.ShapeDtypeStruct((4, 64, HALF), BF),
            jax.ShapeDtypeStruct((4, 64, HALF), BF),
            jax.ShapeDtypeStruct((2, ROWS, D), BF),
            jax.ShapeDtypeStruct((2, ROWS, D), BF),
            jax.ShapeDtypeStruct((8, D), F32),
        ),
        in_specs=[hbm] * 8,
        out_specs=(hbm,) * 5,
        scratch_shapes=[pltpu.VMEM(s, t) for s, t in SCRATCH.values()]
        + [pltpu.SemaphoreType.DMA((len(GROUP), 3)), pltpu.SemaphoreType.DMA((len(GROUP), 3))],
        compiler_params=pltpu.CompilerParams(
            collective_id=0, has_side_effects=True, vmem_limit_bytes=64 * 1024 * 1024 - 65536
        ),
    )(acts_in, cotangent, qkv_weight, out_weight, up_weight, down_weight, vectors, image_ids)
    return pl.pallas_call(
        assemble,
        out_shape=(
            jax.ShapeDtypeStruct((1, 2, 1, ROWS, D), BF),
            jax.ShapeDtypeStruct((1, 2, 1, ROWS, D), BF),
            jax.ShapeDtypeStruct((1, 64, 3072), F32),
            jax.ShapeDtypeStruct((1, 64, D), F32),
            jax.ShapeDtypeStruct((1, 64, 4096), F32),
            jax.ShapeDtypeStruct((1, 256, D), F32),
            jax.ShapeDtypeStruct((1, 4, 64), F32),
        ),
        in_specs=[hbm] * 5,
        out_specs=(vmem,) * 7,
        scratch_shapes=[
            pltpu.VMEM((4, 64, HALF), BF),
            pltpu.VMEM((4, 64, HALF), BF),
            pltpu.VMEM((8, D), F32),
            pltpu.SemaphoreType.DMA((7,)),
        ],
        compiler_params=pltpu.CompilerParams(vmem_limit_bytes=64 * 1024 * 1024 - 65536),
    )(*out)


def solution(mesh):
    placed = (
        P(None, "shard", "seq", None),
        P(None, "shard", "seq", None),
        P("section", "shard", None),
        P("section", "shard", None),
        P("section", "shard", None),
        P("section", "shard", None),
        P("section", None, "shard"),
        P(None, "shard", None),
    )
    return jax.shard_map(
        local,
        mesh=mesh,
        in_specs=placed,
        out_specs=(
            P("section", None, "shard", "seq", None),
            P("section", None, "shard", "seq", None),
            P("section", "shard", None),
            P("section", "shard", None),
            P("section", "shard", None),
            P("section", "shard", None),
            P("section", None, "shard"),
        ),
        check_vma=False,
    )
```
